128 devices in a mesh: seq: 64 (over x, y, z), head: 2 (over core).
Axes of the slice: x: 4, y: 4, z: 4, core: 2. Of those that a mesh axis runs over, the one named last changes fastest.
Arguments:
- queries: bfloat16 [65536, 2048], P(('seq', 'head')), may hold values from -120 to 120
- keys: bfloat16 [65536, 2048], P(('seq', 'head')), may hold values from -4.5 to 4.5
- values: bfloat16 [65536, 2048], P(('seq', 'head')), may hold values from -6 to 6
- offsets: int32 [2, 4], replicated, may hold values from 0 to 31, as said below
Outputs:
- attention_out: bfloat16 [65536, 2048], P(('seq', 'head'))
The draws below stay inside these ranges and needn't reach their ends.
Inputs may be any that keep to these rules, and one draw needn't show every extreme that they name: offsets[0, g] is below 2 and offsets[1, g] is below 32; some head group has offsets[0, g] = 0 and some head group has offsets[1, g] = 31.
All inputs are finite; a program needn't handle non-finite values.
Results may differ from the reference program's by a relative error of at most 0.0032.
Values may be sent and summed in bfloat16 or wider, within the bound.
No kernel may reach another device: no remote copies, remote signals or barrier semaphores. Data moves between devices by JAX's collectives and lax.ppermute only.
A program may use at most 128 MiB of HBM per device.

```python
import jax
import jax.numpy as jnp
from jax import lax

HEADS = 16
HD = 128
GROUP_HEADS = 4
GROUPS = 4
BLK = 128
TOK_DEV = 1024
TOKENS = 65536
R1 = 2
W1 = 2048
R2 = 32


def shared_keys(key):
    base = jnp.clip(jax.random.normal(jax.random.fold_in(key, 22), (TOKENS // BLK, BLK, HEADS, HD), jnp.float32), -4.5, 4.5)
    planted = BLK // 16
    firsts = base[:, 0:2 * planted:2]
    seconds = base[:, 1:2 * planted:2]
    paired = jnp.stack([firsts, seconds], axis=2).reshape(TOKENS // BLK, 2 * planted, HEADS, HD)
    return jnp.concatenate([paired, base[:, 2 * planted:]], axis=1)


def draw_keys(key, part):
    field_all = shared_keys(key)
    return field_all.reshape(TOKENS, HEADS * HD).astype(jnp.bfloat16)


def draw_queries(key, part):
    key = jax.random.fold_in(key, 5)
    base = jnp.clip(2.0 * jax.random.normal(key, (TOKENS // BLK, BLK, HEADS, HD), jnp.float32), -10.0, 10.0)
    planted = BLK // 16
    tail_rows = base[:, BLK - planted:]
    joined = jnp.concatenate([base[:, :BLK - planted], tail_rows], axis=1)
    return joined.reshape(TOKENS, HEADS * HD).astype(jnp.bfloat16)


def draw_offsets(key, part):
    key = jax.random.fold_in(key, 7)
    near_part = jax.random.randint(jax.random.fold_in(key, 1), (GROUPS,), 0, R1)
    far_part = jax.random.randint(jax.random.fold_in(key, 2), (GROUPS,), 0, R2)
    near_pick = jax.random.randint(jax.random.fold_in(key, 3), (), 0, GROUPS)
    far_pick = jax.random.randint(jax.random.fold_in(key, 4), (), 0, GROUPS)
    group_ids = jnp.arange(GROUPS)
    near_part = jnp.where(group_ids == near_pick, 0, near_part)
    far_part = jnp.where(group_ids == far_pick, R2 - 1, far_part)
    return jnp.stack([near_part, far_part], axis=0).astype(jnp.int32)


def block_scale(own_key, shape, split, low, high):
    gain, own = 1.0, jax.random.fold_in(own_key, 6)
    for dim, parts in split:
        heights = jnp.exp(jax.random.uniform(jax.random.fold_in(own, dim), (parts,), jnp.float32, low / len(split), high / len(split)))
        gain = gain * jnp.repeat(heights, shape[dim] // parts).reshape([-1 if axis == dim else 1 for axis in range(len(shape))])
    return gain


def normal_values(stream_key, extent, deviation, limit, shards=(), held_as=jnp.bfloat16):
    values = jax.random.normal(stream_key, extent, jnp.float32) * deviation
    if len(shards) > 0:
        values = block_scale(stream_key, extent, shards, -0.22, 0.18) * values
    return jnp.clip(values, min=-limit, max=limit).astype(held_as)


def setup_inputs(seed: int = 0) -> dict:
    streams_of = jax.random.split(jax.random.key(seed), 5)
    return {
        "queries": draw_queries(jax.random.fold_in(streams_of[4], 71), 0),
        "keys": draw_keys(jax.random.fold_in(streams_of[4], 71), 0),
        "values": normal_values(streams_of[2], (TOKENS, HEADS * HD), 1.0, 6.0, ((0, 128),)),
        "offsets": draw_offsets(jax.random.fold_in(streams_of[4], 71), 0),
    }


def attend(query_rows, key_rows, value_rows, allowed):
    scores = jnp.einsum("qhd,khd->hqk", query_rows.astype(jnp.float32), key_rows.astype(jnp.float32)) * (HD ** -0.5)
    scores = jnp.where(allowed[None], scores, -jnp.inf)
    highest = jnp.max(scores, axis=-1)
    raised = jnp.exp(scores - highest[..., None])
    totals = jnp.sum(raised, axis=-1)
    weights = lax.optimization_barrier(raised.astype(jnp.bfloat16)).astype(jnp.float32)
    output = jnp.einsum("hqk,khd->qhd", weights, value_rows.astype(jnp.float32)) / jnp.transpose(totals)[:, :, None]
    return output, jnp.transpose(highest + jnp.log(totals))


def causal(length):
    places = jnp.arange(length)
    return places[None, :] <= places[:, None]


def dilated(source, offset, dilation):
    blocks = source.reshape((source.shape[0] // (dilation * BLK), dilation, BLK) + source.shape[1:])
    return lax.dynamic_index_in_dim(blocks, offset, 1, keepdims=False).reshape((-1,) + source.shape[1:])


def spread(rows_out, rows_mass, offset, dilation):
    block_count = rows_out.shape[0] // BLK
    width_heads = rows_out.shape[1]
    chosen = jnp.arange(dilation) == offset
    output = jnp.where(chosen[None, :, None, None, None], rows_out.reshape(block_count, 1, BLK, width_heads, HD), 0.0)
    log_mass = jnp.where(chosen[None, :, None, None], rows_mass.reshape(block_count, 1, BLK, width_heads), -jnp.inf)
    total_rows = block_count * dilation * BLK
    return output.reshape(total_rows, width_heads, HD), log_mass.reshape(total_rows, width_heads)


def level_groups(query_all, key_all, value_all, offset_row, dilation):
    outputs = []
    masses = []
    for member in range(GROUPS):
        heads_cut = slice(member * GROUP_HEADS, (member + 1) * GROUP_HEADS)
        offset = offset_row[member]
        query_rows = dilated(query_all[:, heads_cut], offset, dilation)
        key_rows = dilated(key_all[:, heads_cut], offset, dilation)
        value_rows = dilated(value_all[:, heads_cut], offset, dilation)
        output, log_mass = attend(query_rows, key_rows, value_rows, causal(query_rows.shape[0]))
        output, log_mass = spread(output, log_mass, offset, dilation)
        outputs.append(output)
        masses.append(log_mass)
    return jnp.concatenate(outputs, axis=1), jnp.concatenate(masses, axis=1)


def reference(queries, keys, values, offsets):
    query_all = queries.reshape(TOKENS, HEADS, HD)
    key_all = keys.reshape(TOKENS, HEADS, HD)
    value_all = values.reshape(TOKENS, HEADS, HD)
    far_out, far_mass = level_groups(query_all, key_all, value_all, offsets[1], R2)

    def segment(number):
        first_row = (number * W1).astype(jnp.int32)

        def window(source):
            return lax.dynamic_slice_in_dim(source, first_row, W1, 0)

        seg_query = window(query_all)
        seg_key = window(key_all)
        seg_value = window(value_all)
        local_outs = []
        local_masses = []
        for portion in range(W1 // TOK_DEV):
            row_cut = slice(portion * TOK_DEV, (portion + 1) * TOK_DEV)
            output, log_mass = attend(seg_query[row_cut], seg_key[row_cut], seg_value[row_cut], causal(TOK_DEV))
            local_outs.append(output)
            local_masses.append(log_mass)
        local_out = jnp.concatenate(local_outs, axis=0)
        local_mass = jnp.concatenate(local_masses, axis=0)
        near_out, near_mass = level_groups(seg_query, seg_key, seg_value, offsets[0], R1)
        far_slice = window(far_out)
        far_slice_mass = window(far_mass)
        masses = jnp.stack([local_mass, near_mass, far_slice_mass])
        summit = jnp.max(masses, axis=0)
        scales = jnp.exp(masses - summit[None])
        blended = (scales[0][..., None] * local_out + scales[1][..., None] * near_out + scales[2][..., None] * far_slice) / jnp.sum(scales, axis=0)[..., None]
        return blended.astype(jnp.bfloat16).reshape(W1, HEADS * HD)

    blended_all = lax.map(segment, jnp.arange(TOKENS // W1, dtype=jnp.int32))
    return blended_all.reshape(TOKENS, HEADS * HD)
```

```python
import functools

import jax
import jax.numpy as jnp
import numpy as np
from jax import lax
from jax.experimental import pallas as pl
from jax.experimental.pallas import tpu as pltpu
from jax.sharding import Mesh
from jax.sharding import PartitionSpec as P

HD = 128
BLK = 128
HALF = 64
HEADS = 16
GROUPS = 4
GH = 4
GW = GH * HD
ROWS = 512
NSEL = 256
AXES = ("x", "y", "z", "c")
SIZES = (4, 4, 4, 2)
SCALE = float(HD**-0.5 * np.log2(np.e))
LOW = -1e30
BF, F32 = jnp.bfloat16, jnp.float32

I_CORE, I_ODD, I_FACTIVE, I_PAR, I_NEAR, I_FBLK, I_FMINE = 0, 1, 2, 3, 4, 8, 12


def route(step):
    pairs = []
    for index in np.ndindex(*SIZES):
        target = step(*index)
        if target is not None:
            pairs.append((int(np.ravel_multi_index(index, SIZES)), int(np.ravel_multi_index(target, SIZES))))
    return pairs


CORE = route(lambda x, y, z, c: (x, y, z, 1 - c))
TO_EVEN = route(lambda x, y, z, c: (x, y, z - 1, c) if z % 2 else None)
TO_ODD = route(lambda x, y, z, c: (x, y, z + 1, c) if z % 2 == 0 else None)


def move(array, pairs):
    return lax.ppermute(array, AXES, pairs)


def cost(flops, nbytes, exps=0):
    return pl.CostEstimate(flops=int(flops), bytes_accessed=int(nbytes), transcendentals=int(exps))


ANY = pl.BlockSpec(memory_space=pl.ANY)
SMEM = pl.BlockSpec(memory_space=pltpu.SMEM)
PARAMS = dict(vmem_limit_bytes=48 * 1024 * 1024)


def nt(a, b):
    return lax.dot_general(a, b, (((1,), (1,)), ((), ())), preferred_element_type=F32)


def nn(a, b):
    return lax.dot_general(a, b, (((1,), (0,)), ((), ())), preferred_element_type=F32)


def three(x):
    hi = x.astype(BF).astype(F32)
    rest = x - hi
    mid = rest.astype(BF).astype(F32)
    return hi, mid, rest - mid


def run_copies(copies):
    for copy in copies:
        copy.start()
    for copy in copies:
        copy.wait()


def pack_first(info, q, k, v, *rest):
    near_outs, far_out, sems = rest[:GROUPS], rest[GROUPS], rest[GROUPS + 1]
    core = info[I_CORE]
    copies = []
    n = 0
    for g in range(GROUPS):
        cols = pl.ds(g * GW, GW)
        for half in range(2):
            first = pl.multiple_of((info[I_NEAR + g] + 2 * half) * BLK, BLK)
            copies.append(
                pltpu.make_async_copy(
                    q.at[pl.ds(first, BLK), cols], near_outs[g].at[pl.ds(half * BLK, BLK)], sems.at[n]
                )
            )
            n += 1
        first = pl.multiple_of((info[I_FBLK + g] % 4) * BLK + (1 - core) * HALF, HALF)
        for t, source in enumerate((q, k, v)):
            copies.append(
                pltpu.make_async_copy(source.at[pl.ds(first, HALF), cols], far_out.at[g, t], sems.at[n])
            )
            n += 1
    run_copies(copies)


def pack_second(info, q, k, v, received, out, sems):
    core = info[I_CORE]

    def all_copies(g, mine):
        copies = []
        first = pl.multiple_of((info[I_FBLK + g] % 4) * BLK + core * HALF, HALF)
        for t, source in enumerate((q, k, v)):
            for h in range(GH):
                if mine:
                    piece = source.at[pl.ds(first, HALF), pl.ds(g * GW + h * HD, HD)]
                else:
                    piece = received.at[g, t, :, pl.ds(h * HD, HD)]
                copies.append(
                    pltpu.make_async_copy(piece, out.at[h * GROUPS + g, t], sems.at[(g * 3 + t) * GH + h])
                )
        return copies

    for g in range(GROUPS):
        here = info[I_FBLK + g] // 4 == core

        @pl.when(here)
        def _():
            for copy in all_copies(g, True):
                copy.start()

        @pl.when(jnp.logical_not(here))
        def _():
            for copy in all_copies(g, False):
                copy.start()

    for g in range(GROUPS):
        for copy in all_copies(g, False):
            copy.wait()


def softmax_parts(parts, values):
    top = functools.reduce(jnp.maximum, [jnp.max(s, axis=1, keepdims=True) for s in parts]) * SCALE
    total = 0.0
    out = 0.0
    for s, val in zip(parts, values):
        p = jnp.exp2(s * SCALE - top)
        total = total + jnp.sum(p, axis=1, keepdims=True)
        out = out + nn(p.astype(BF), val)
    return out / total, top + jnp.log2(total)


def local_kernel(info, q, k, v, ko, vo, out, mass):
    head = pl.program_id(0)
    near = info[I_NEAR + head // GH]
    extra = [jnp.where(near == i, 1.0, 0.0).astype(F32) for i in range(2)]

    def tile(t, with_other):
        rows = pl.ds(t * 256, 256)
        qt = q[rows, :]
        width = (t + 1) * 256
        s = nt(qt, k[0:width, :])
        ri = lax.broadcasted_iota(jnp.int32, (256, 256), 0)
        ci = lax.broadcasted_iota(jnp.int32, (256, 256), 1)
        diag = jnp.where(ri >= ci, s[:, t * 256 :], LOW)
        s = diag if t == 0 else jnp.concatenate([s[:, : t * 256], diag], axis=1)
        scores = [(s, v[0:width, :])]
        if with_other:
            scores.append((nt(qt, ko[...]), vo[...]))
        ps = [[] for _ in scores]
        totals, tops = [], []
        for i in range(2):
            mine = [sc[i * 128 : (i + 1) * 128] for sc, _ in scores]
            top = functools.reduce(jnp.maximum, [jnp.max(m, axis=1, keepdims=True) for m in mine]) * SCALE
            raised = top - extra[i]
            total = 0.0
            for n, m in enumerate(mine):
                pieces = []
                for j in range(m.shape[1] // 128):
                    p = jnp.exp2(m[:, j * 128 : (j + 1) * 128] * SCALE - (raised if j % 2 == i else top))
                    total = total + p
                    pieces.append(p.astype(BF))
                ps[n].append(jnp.concatenate(pieces, axis=1))
            totals.append(jnp.sum(total, axis=1, keepdims=True))
            tops.append(top)
        acc = 0.0
        for n, (_, val) in enumerate(scores):
            acc = acc + nn(jnp.concatenate(ps[n], axis=0), val)
        total = jnp.concatenate(totals, axis=0)
        top = jnp.concatenate(tops, axis=0)
        out[rows, :] = acc / total
        lane = lax.broadcasted_iota(jnp.int32, (256, HD), 1)
        mass[rows, :] = jnp.where(lane == head, top + jnp.log2(total), mass[rows, :])

    for with_other in (False, True):

        @pl.when(info[I_CORE] == int(with_other))
        def _():
            tile(0, with_other)
            tile(1, with_other)


def near_kernel(group, info, qr, k0, k1, ko0, ko1, v0, v1, vo0, vo1, out):
    @pl.when(info[I_ODD] == 0)
    def _():
        lane = lax.broadcasted_iota(jnp.int32, (NSEL, HD), 1)
        stats = jnp.zeros((NSEL, HD), F32)
        for h in range(GH):
            cols = slice(h * HD, (h + 1) * HD)
            keys = jnp.concatenate([r[:, cols] for r in (k0, k1, ko0, ko1)], axis=0)
            vals = jnp.concatenate([r[:, cols] for r in (v0, v1, vo0, vo1)], axis=0)
            o, m = softmax_parts([nt(qr[:, cols], keys)], [vals])
            out[:, cols] = o.astype(BF)
            for n, term in enumerate(three(m)):
                stats = jnp.where(lane == n * GH + h, term, stats)
        out[:, GW:] = stats.astype(BF)


def far_kernel(info, mine, other, out):
    @pl.when(info[I_FACTIVE] == 1)
    def _():
        late = info[I_CORE] == 1
        for t in range(4):
            upto = 4 * t + 4
            q = mine[4 * t : upto, 0].reshape(256, HD)
            ri = lax.broadcasted_iota(jnp.int32, (256, 256), 0)
            ci = lax.broadcasted_iota(jnp.int32, (256, 256), 1)
            own_ok = (ci // HALF < ri // HALF) | ((ci // HALF == ri // HALF) & (ci <= ri))
            oth_ok = (ci // HALF < ri // HALF) | ((ci // HALF == ri // HALF) & late)
            parts, vals = [], []
            for source, ok in ((mine, own_ok), (other, oth_ok)):
                s = nt(q, source[0:upto, 1].reshape(upto * HALF, HD))
                d = jnp.where(ok, s[:, t * 256 :], LOW)
                parts.append(d if t == 0 else jnp.concatenate([s[:, : t * 256], d], axis=1))
                vals.append(source[0:upto, 2].reshape(upto * HALF, HD))
            o, m = softmax_parts(parts, vals)
            o = o.astype(BF)
            turned = jnp.transpose(jnp.broadcast_to(m, (256, HD)))[0:16]
            row = lax.broadcasted_iota(jnp.int32, (16, 256), 0)
            stats = jnp.zeros((16, 256), F32)
            for n, term in enumerate(three(turned)):
                stats = jnp.where(row == n, term, stats)
            stats = stats.astype(BF)
            for b in range(4):
                out[4 * t + b, 0:HALF] = o[b * HALF : (b + 1) * HALF]
                out[4 * t + b, HALF:] = stats[:, (b // 2) * 128 : (b // 2) * 128 + 128]


def merge_kernel(info, local_out, mass, near, far_own, far_oth, out):
    g = pl.program_id(0)
    core = info[I_CORE]
    near_par = info[I_NEAR + g]
    odd = info[I_ODD] == 1
    far_here = info[I_FMINE + g] == 1
    far_blk = info[I_FBLK + g] % 4
    second = info[I_PAR] == 1
    lane = lax.broadcasted_iota(jnp.int32, (BLK, HD), 1)

    def column(array, place):
        picked = jnp.where(lane == place, array, 0.0)
        return jnp.sum(picked, axis=1, keepdims=True)

    for h in range(GH):
        cols = slice(h * HD, (h + 1) * HD)
        halves, masses = [], []
        for source in (far_own, far_oth):
            halves.append(source[h, 0, 0:HALF].astype(F32))
            st = source[h, 0, HALF:].astype(F32)
            line = st[0:1] + st[1:2] + st[2:3]
            turned = jnp.transpose(jnp.broadcast_to(line, (128, 128)))
            masses.append(jnp.where(second, turned[HALF:], turned[:HALF]))
        first = core == 0
        far_o = jnp.concatenate(
            [jnp.where(first, halves[0], halves[1]), jnp.where(first, halves[1], halves[0])], axis=0
        )
        far_m = jnp.concatenate(
            [jnp.where(first, masses[0], masses[1]), jnp.where(first, masses[1], masses[0])], axis=0
        )
        for i in range(4):
            rows = slice(i * BLK, (i + 1) * BLK)
            half = slice((i // 2) * BLK, (i // 2 + 1) * BLK)
            m0 = column(mass[rows, :], g * GH + h)
            st = near[0, half, GW:].astype(F32)
            st = jnp.where((lane == h) | (lane == GH + h) | (lane == 2 * GH + h), st, 0.0)
            near_on = odd & (near_par == i % 2)
            m1 = jnp.where(near_on, jnp.sum(st, axis=1, keepdims=True), LOW)
            o1 = jnp.where(near_on, near[0, half, cols].astype(F32), 0.0)
            far_on = far_here & (far_blk == i)
            m2 = jnp.where(far_on, far_m, LOW)
            o2 = jnp.where(far_on, far_o, 0.0)
            top = jnp.maximum(jnp.maximum(m0, m1), m2)
            e0, e1, e2 = jnp.exp2(m0 - top), jnp.exp2(m1 - top), jnp.exp2(m2 - top)
            mixed = (e0 * local_out[rows, cols] + e1 * o1 + e2 * o2) / (e0 + e1 + e2)
            out[rows, cols] = mixed.astype(BF)


def device_part(q, k, v, offsets):
    x, y, z, c = (lax.axis_index(a) for a in AXES)
    near_off, far_off = offsets[0], offsets[1]
    far_z = far_off // 8
    far_blk = far_off % 8
    info = jnp.concatenate(
        [
            jnp.stack([c, z % 2, (far_z[y] == z).astype(jnp.int32), y % 2]).astype(jnp.int32),
            near_off,
            far_blk,
            ((far_z == z) & (far_blk // 4 == c)).astype(jnp.int32),
        ]
    )

    packed = pl.pallas_call(
        pack_first,
        out_shape=[jax.ShapeDtypeStruct((NSEL, GW), BF)] * GROUPS
        + [jax.ShapeDtypeStruct((GROUPS, 3, HALF, GW), BF)],
        in_specs=[SMEM, ANY, ANY, ANY],
        out_specs=[ANY] * (GROUPS + 1),
        scratch_shapes=[pltpu.SemaphoreType.DMA((5 * GROUPS,))],
        cost_estimate=cost(0, 4 << 20),
        name="pack_first",
    )(info, q, k, v)
    near_q, far_send = packed[:GROUPS], packed[GROUPS]

    far_recv = move(far_send, CORE)
    near_recv = [move(a, TO_EVEN) for a in near_q]
    ko, vo = move(k, CORE), move(v, CORE)

    far_pack = pl.pallas_call(
        pack_second,
        out_shape=jax.ShapeDtypeStruct((HEADS, 3, HALF, HD), BF),
        in_specs=[SMEM, ANY, ANY, ANY, ANY],
        out_specs=ANY,
        scratch_shapes=[pltpu.SemaphoreType.DMA((HEADS * 3,))],
        cost_estimate=cost(0, 3 << 20),
        name="pack_second",
    )(info, q, k, v, far_recv)
    far_mine = lax.all_to_all(far_pack, ("x", "y"), 0, 0, tiled=True)
    far_other = move(far_mine, CORE)
    far_out = pl.pallas_call(
        far_kernel,
        out_shape=jax.ShapeDtypeStruct((HEADS, HALF + 16, HD), BF),
        in_specs=[SMEM, pl.BlockSpec(memory_space=pltpu.VMEM), pl.BlockSpec(memory_space=pltpu.VMEM)],
        out_specs=pl.BlockSpec(memory_space=pltpu.VMEM),
        compiler_params=pltpu.CompilerParams(**PARAMS),
        cost_estimate=cost(4 * 1024 * 1280 * 128, 2 << 20, 1024 * 1280),
        name="far",
    )(info, far_mine, far_other)
    far_back = lax.all_to_all(far_out, ("x", "y"), 0, 0, tiled=True)
    far_back_other = move(far_back, CORE)

    near_back = []
    for g in range(GROUPS):

        def sel(half, g=g):
            return pl.BlockSpec((BLK, GW), lambda i, info: (info[I_NEAR + g] + 2 * half, g))

        near_out = pl.pallas_call(
            functools.partial(near_kernel, g),
            out_shape=jax.ShapeDtypeStruct((NSEL, GW + HD), BF),
            grid_spec=pltpu.PrefetchScalarGridSpec(
                num_scalar_prefetch=1,
                grid=(1,),
                in_specs=[pl.BlockSpec((NSEL, GW), lambda i, info: (0, 0))]
                + [sel(0), sel(1)] * 4,
                out_specs=pl.BlockSpec((NSEL, GW + HD), lambda i, info: (0, 0)),
            ),
            compiler_params=pltpu.CompilerParams(**PARAMS),
            cost_estimate=cost(4 * 4 * NSEL * 512 * HD, 2 << 20, 4 * NSEL * 512),
            name="near",
        )(info, near_recv[g], k, k, ko, ko, v, v, vo, vo)
        near_back.append(move(near_out, TO_ODD))

    def head_block():
        return pl.BlockSpec((ROWS, HD), lambda h, info: (0, h))

    local_out, mass = pl.pallas_call(
        local_kernel,
        out_shape=[
            jax.ShapeDtypeStruct((ROWS, HEADS * HD), F32),
            jax.ShapeDtypeStruct((ROWS, HD), F32),
        ],
        grid_spec=pltpu.PrefetchScalarGridSpec(
            num_scalar_prefetch=1,
            grid=(HEADS,),
            in_specs=[head_block()] * 5,
            out_specs=[head_block(), pl.BlockSpec((ROWS, HD), lambda h, info: (0, 0))],
        ),
        compiler_params=pltpu.CompilerParams(**PARAMS),
        cost_estimate=cost(4 * 16 * 512 * 832 * HD, 15 << 20, 16 * 512 * 832),
        name="local",
    )(info, q, k, v, ko, vo)

    def far_spec():
        return pl.BlockSpec((GH, 1, HALF + 16, HD), lambda g, info: (0, g, 0, 0))

    return pl.pallas_call(
        merge_kernel,
        out_shape=jax.ShapeDtypeStruct((ROWS, HEADS * HD), BF),
        grid_spec=pltpu.PrefetchScalarGridSpec(
            num_scalar_prefetch=1,
            grid=(GROUPS,),
            in_specs=[
                pl.BlockSpec((ROWS, GW), lambda g, info: (0, g)),
                pl.BlockSpec((ROWS, HD), lambda g, info: (0, 0)),
                pl.BlockSpec((1, NSEL, GW + HD), lambda g, info: (g, 0, 0)),
                far_spec(),
                far_spec(),
            ],
            out_specs=pl.BlockSpec((ROWS, GW), lambda g, info: (0, g)),
        ),
        compiler_params=pltpu.CompilerParams(**PARAMS),
        cost_estimate=cost(1 << 22, 8 << 20),
        name="merge",
    )(
        info,
        local_out,
        mass,
        jnp.stack(near_back),
        far_back.reshape(GH, GROUPS, HALF + 16, HD),
        far_back_other.reshape(GH, GROUPS, HALF + 16, HD),
    )


def solution(mesh):
    cube = Mesh(mesh.devices.reshape(SIZES), AXES)
    rows = P(AXES, None)
    return jax.shard_map(
        device_part, mesh=cube, in_specs=(rows, rows, rows, P()), out_specs=rows, check_vma=False
    )
```

```python
import functools

import jax
import jax.numpy as jnp
import numpy as np
from jax import lax
from jax.experimental import pallas as pl
from jax.experimental.pallas import tpu as pltpu
from jax.sharding import Mesh
from jax.sharding import PartitionSpec as P

HD = 128
BLK = 128
HALF = 64
HEADS = 16
GROUPS = 4
GH = 4
GW = GH * HD
ROWS = 512
NSEL = 256
AXES = ("x", "y", "z", "c")
SIZES = (4, 4, 4, 2)
SCALE = float(HD**-0.5 * np.log2(np.e))
LOW = -1e30
BF, F32 = jnp.bfloat16, jnp.float32

I_CORE, I_ODD, I_FACTIVE, I_PAR, I_NEAR, I_FBLK, I_FMINE = 0, 1, 2, 3, 4, 8, 12


def route(step):
    pairs = []
    for index in np.ndindex(*SIZES):
        target = step(*index)
        if target is not None:
            pairs.append((int(np.ravel_multi_index(index, SIZES)), int(np.ravel_multi_index(target, SIZES))))
    return pairs


CORE = route(lambda x, y, z, c: (x, y, z, 1 - c))
TO_EVEN = route(lambda x, y, z, c: (x, y, z - 1, c) if z % 2 else None)
TO_ODD = route(lambda x, y, z, c: (x, y, z + 1, c) if z % 2 == 0 else None)


def move(array, pairs):
    return lax.ppermute(array, AXES, pairs)


def cost(flops, nbytes, exps=0):
    return pl.CostEstimate(flops=int(flops), bytes_accessed=int(nbytes), transcendentals=int(exps))


ANY = pl.BlockSpec(memory_space=pl.ANY)
SMEM = pl.BlockSpec(memory_space=pltpu.SMEM)
PARAMS = dict(vmem_limit_bytes=16 * 1024 * 1024)


def nt(a, b):
    return lax.dot_general(a, b, (((1,), (1,)), ((), ())), preferred_element_type=F32)


def nn(a, b):
    return lax.dot_general(a, b, (((1,), (0,)), ((), ())), preferred_element_type=F32)


def three(x):
    hi = x.astype(BF).astype(F32)
    rest = x - hi
    mid = rest.astype(BF).astype(F32)
    return hi, mid, rest - mid


def rows_at(first, count):
    return pl.ds(pl.multiple_of(first, count), count)


def pack_first(info, q, k, v, near0, near1, near2, near3, far_out):
    for g, near in enumerate((near0, near1, near2, near3)):
        cols = slice(g * GW, (g + 1) * GW)
        for half in range(2):
            near[half * BLK : (half + 1) * BLK, :] = q[rows_at((info[I_NEAR + g] + 2 * half) * BLK, BLK), cols]
        away = rows_at((info[I_FBLK + g] % 4) * BLK + (1 - info[I_CORE]) * HALF, HALF)
        for t, source in enumerate((q, k, v)):
            far_out[g, t] = source[away, cols]


def pack_second(info, q, k, v, received, out):
    for g in range(GROUPS):
        here = info[I_FBLK + g] // 4 == info[I_CORE]
        cols = slice(g * GW, (g + 1) * GW)
        kept = rows_at((info[I_FBLK + g] % 4) * BLK + info[I_CORE] * HALF, HALF)

        def put(pick, g=g):
            for t in range(3):
                for h in range(GH):
                    out[h * GROUPS + g, t] = pick(t)[:, h * HD : (h + 1) * HD]

        @pl.when(here)
        def _():
            put(lambda t: (q, k, v)[t][kept, cols])

        @pl.when(jnp.logical_not(here))
        def _():
            put(lambda t: received[g, t])


def softmax_parts(parts, values):
    top = functools.reduce(jnp.maximum, [jnp.max(s, axis=1, keepdims=True) for s in parts]) * SCALE
    total = 0.0
    out = 0.0
    for s, val in zip(parts, values):
        p = jnp.exp2(s * SCALE - top)
        total = total + jnp.sum(p, axis=1, keepdims=True)
        out = out + nn(p.astype(BF), val)
    return out / total, top + jnp.log2(total)


def local_kernel(info, q, k, v, ko, vo, out, mass):
    mass[...] = jnp.zeros_like(mass)

    def tile(head, t, with_other):
        rows = slice(t * 256, t * 256 + 256)
        cols = pl.ds(pl.multiple_of(head * HD, HD), HD)
        near = info[I_NEAR + head // GH]
        extra = [jnp.where(near == i, 1.0, 0.0).astype(F32) for i in range(2)]
        qt = q[rows, cols]
        width = (t + 1) * 256
        s = nt(qt, k[0:width, cols])
        ri = lax.broadcasted_iota(jnp.int32, (256, 256), 0)
        ci = lax.broadcasted_iota(jnp.int32, (256, 256), 1)
        diag = jnp.where(ri >= ci, s[:, t * 256 :], LOW)
        s = diag if t == 0 else jnp.concatenate([s[:, : t * 256], diag], axis=1)
        scores = [(s, v[0:width, cols])]
        if with_other:
            scores.append((nt(qt, ko[:, cols]), vo[:, cols]))
        ps = [[] for _ in scores]
        totals, tops = [], []
        for i in range(2):
            mine = [sc[i * 128 : (i + 1) * 128] for sc, _ in scores]
            top = functools.reduce(jnp.maximum, [jnp.max(m, axis=1, keepdims=True) for m in mine]) * SCALE
            raised = top - extra[i]
            total = 0.0
            for n, m in enumerate(mine):
                pieces = []
                for j in range(m.shape[1] // 128):
                    p = jnp.exp2(m[:, j * 128 : (j + 1) * 128] * SCALE - (raised if j % 2 == i else top))
                    total = total + p
                    pieces.append(p.astype(BF))
                ps[n].append(jnp.concatenate(pieces, axis=1))
            totals.append(jnp.sum(total, axis=1, keepdims=True))
            tops.append(top)
        acc = 0.0
        for n, (_, val) in enumerate(scores):
            acc = acc + nn(jnp.concatenate(ps[n], axis=0), val)
        total = jnp.concatenate(totals, axis=0)
        top = jnp.concatenate(tops, axis=0)
        out[rows, cols] = acc / total
        lane = lax.broadcasted_iota(jnp.int32, (256, HD), 1)
        mass[rows, :] = jnp.where(lane == head, top + jnp.log2(total), mass[rows, :])

    for with_other in (False, True):

        @pl.when(info[I_CORE] == int(with_other))
        def _():
            @pl.loop(0, HEADS)
            def _(head):
                tile(head, 0, with_other)
                tile(head, 1, with_other)


def near_kernel(group, info, qr, k, ko, v, vo, out):
    @pl.when(info[I_ODD] == 0)
    def _():
        first = info[I_NEAR + group] * BLK
        rows = [pl.ds(pl.multiple_of(first + 2 * half * BLK, BLK), BLK) for half in range(2)]
        lane = lax.broadcasted_iota(jnp.int32, (NSEL, HD), 1)
        stats = jnp.zeros((NSEL, HD), F32)
        for h in range(GH):
            cols = slice(h * HD, (h + 1) * HD)
            place = slice(group * GW + h * HD, group * GW + (h + 1) * HD)
            keys = jnp.concatenate([r[sel, place] for r in (k, ko) for sel in rows], axis=0)
            vals = jnp.concatenate([r[sel, place] for r in (v, vo) for sel in rows], axis=0)
            o, m = softmax_parts([nt(qr[:, cols], keys)], [vals])
            out[:, cols] = o.astype(BF)
            for n, term in enumerate(three(m)):
                stats = jnp.where(lane == n * GH + h, term, stats)
        out[:, GW:] = stats.astype(BF)


def far_kernel(info, mine, other, out):
    @pl.when(info[I_FACTIVE] == 1)
    def _():
        late = info[I_CORE] == 1
        for t in range(4):
            upto = 4 * t + 4
            q = mine[4 * t : upto, 0].reshape(256, HD)
            ri = lax.broadcasted_iota(jnp.int32, (256, 256), 0)
            ci = lax.broadcasted_iota(jnp.int32, (256, 256), 1)
            own_ok = (ci // HALF < ri // HALF) | ((ci // HALF == ri // HALF) & (ci <= ri))
            oth_ok = (ci // HALF < ri // HALF) | ((ci // HALF == ri // HALF) & late)
            parts, vals = [], []
            for source, ok in ((mine, own_ok), (other, oth_ok)):
                s = nt(q, source[0:upto, 1].reshape(upto * HALF, HD))
                d = jnp.where(ok, s[:, t * 256 :], LOW)
                parts.append(d if t == 0 else jnp.concatenate([s[:, : t * 256], d], axis=1))
                vals.append(source[0:upto, 2].reshape(upto * HALF, HD))
            o, m = softmax_parts(parts, vals)
            o = o.astype(BF)
            turned = jnp.transpose(jnp.broadcast_to(m, (256, HD)))[0:16]
            row = lax.broadcasted_iota(jnp.int32, (16, 256), 0)
            stats = jnp.zeros((16, 256), F32)
            for n, term in enumerate(three(turned)):
                stats = jnp.where(row == n, term, stats)
            stats = stats.astype(BF)
            for b in range(4):
                out[4 * t + b, 0:HALF] = o[b * HALF : (b + 1) * HALF]
                out[4 * t + b, HALF:] = stats[:, (b // 2) * 128 : (b // 2) * 128 + 128]


def merge_kernel(info, local_out, mass, near0, near1, near2, near3, far_own, far_oth, out, done, sems):
    core = info[I_CORE]
    odd = info[I_ODD] == 1
    second = info[I_PAR] == 1
    first = core == 0
    lane = lax.broadcasted_iota(jnp.int32, (BLK, HD), 1)

    def column(array, places):
        hit = functools.reduce(jnp.logical_or, [lane == p for p in places])
        return jnp.sum(jnp.where(hit, array, 0.0), axis=1, keepdims=True)

    copies = []
    for g, near in enumerate((near0, near1, near2, near3)):
        near_par = info[I_NEAR + g]
        far_here = info[I_FMINE + g] == 1
        far_blk = info[I_FBLK + g] % 4
        for h in range(GH):
            cols = slice(h * HD, (h + 1) * HD)
            place = slice(g * GW + h * HD, g * GW + (h + 1) * HD)
            halves, masses = [], []
            for source in (far_own, far_oth):
                tile = source[h * GROUPS + g]
                halves.append(tile[0:HALF].astype(F32))
                st = tile[HALF:].astype(F32)
                line = st[0:1] + st[1:2] + st[2:3]
                turned = jnp.transpose(jnp.broadcast_to(line, (128, 128)))
                masses.append(jnp.where(second, turned[HALF:], turned[:HALF]))
            far_o = jnp.concatenate(
                [jnp.where(first, halves[0], halves[1]), jnp.where(first, halves[1], halves[0])], axis=0
            )
            far_m = jnp.concatenate(
                [jnp.where(first, masses[0], masses[1]), jnp.where(first, masses[1], masses[0])], axis=0
            )
            for i in range(4):
                rows = slice(i * BLK, (i + 1) * BLK)
                half = slice((i // 2) * BLK, (i // 2 + 1) * BLK)
                m0 = column(mass[rows, :], [g * GH + h])
                near_on = odd & (near_par == i % 2)
                m1 = column(near[half, GW:].astype(F32), [h, GH + h, 2 * GH + h])
                m1 = jnp.where(near_on, m1, LOW)
                o1 = jnp.where(near_on, near[half, cols].astype(F32), 0.0)
                far_on = far_here & (far_blk == i)
                m2 = jnp.where(far_on, far_m, LOW)
                o2 = jnp.where(far_on, far_o, 0.0)
                top = jnp.maximum(jnp.maximum(m0, m1), m2)
                e0, e1, e2 = jnp.exp2(m0 - top), jnp.exp2(m1 - top), jnp.exp2(m2 - top)
                mixed = (e0 * local_out[rows, place] + e1 * o1 + e2 * o2) / (e0 + e1 + e2)
                done[rows, place] = mixed.astype(BF)
        part = pl.ds(g * GW, GW)
        copies.append(pltpu.make_async_copy(done.at[:, part], out.at[:, part], sems.at[g]))
        copies[-1].start()
    for copy in copies:
        copy.wait()


def device_part(q, k, v, offsets):
    x, y, z, c = (lax.axis_index(a) for a in AXES)
    near_off, far_off = offsets[0], offsets[1]
    far_z = far_off // 8
    far_blk = far_off % 8
    info = jnp.concatenate(
        [
            jnp.stack([c, z % 2, (far_z[y] == z).astype(jnp.int32), y % 2]).astype(jnp.int32),
            near_off,
            far_blk,
            ((far_z == z) & (far_blk // 4 == c)).astype(jnp.int32),
        ]
    )

    vmem = pl.BlockSpec(memory_space=pltpu.VMEM)
    packed = pl.pallas_call(
        pack_first,
        out_shape=[jax.ShapeDtypeStruct((NSEL, GW), BF)] * GROUPS
        + [jax.ShapeDtypeStruct((GROUPS, 3, HALF, GW), BF)],
        in_specs=[SMEM] + [vmem] * 3,
        out_specs=[vmem] * (GROUPS + 1),
        compiler_params=pltpu.CompilerParams(**PARAMS),
        cost_estimate=cost(0, 4 << 20),
        name="pack_first",
    )(info, q, k, v)
    near_q, far_send = packed[:GROUPS], packed[GROUPS]

    far_recv = move(far_send, CORE)
    near_recv = [move(a, TO_EVEN) for a in near_q]
    ko, vo = move(k, CORE), move(v, CORE)

    far_pack = pl.pallas_call(
        pack_second,
        out_shape=jax.ShapeDtypeStruct((HEADS, 3, HALF, HD), BF),
        in_specs=[SMEM] + [vmem] * 4,
        out_specs=vmem,
        compiler_params=pltpu.CompilerParams(**PARAMS),
        cost_estimate=cost(0, 3 << 20),
        name="pack_second",
    )(info, q, k, v, far_recv)
    far_mine = lax.all_to_all(far_pack, ("x", "y"), 0, 0, tiled=True)
    far_other = move(far_mine, CORE)
    far_out = pl.pallas_call(
        far_kernel,
        out_shape=jax.ShapeDtypeStruct((HEADS, HALF + 16, HD), BF),
        in_specs=[SMEM, pl.BlockSpec(memory_space=pltpu.VMEM), pl.BlockSpec(memory_space=pltpu.VMEM)],
        out_specs=pl.BlockSpec(memory_space=pltpu.VMEM),
        compiler_params=pltpu.CompilerParams(**PARAMS),
        cost_estimate=cost(4 * 1024 * 1280 * 128, 2 << 20, 1024 * 1280),
        name="far",
    )(info, far_mine, far_other)
    far_back = lax.all_to_all(far_out, ("x", "y"), 0, 0, tiled=True)
    far_back_other = move(far_back, CORE)

    near_back = []
    for g in range(GROUPS):
        near_out = pl.pallas_call(
            functools.partial(near_kernel, g),
            out_shape=jax.ShapeDtypeStruct((NSEL, GW + HD), BF),
            in_specs=[SMEM] + [vmem] * 5,
            out_specs=vmem,
            compiler_params=pltpu.CompilerParams(**PARAMS),
            cost_estimate=cost(4 * 4 * NSEL * 512 * HD, 2 << 20, 4 * NSEL * 512),
            name="near",
        )(info, near_recv[g], k, ko, v, vo)
        near_back.append(move(near_out, TO_ODD))

    local_out, mass = pl.pallas_call(
        local_kernel,
        out_shape=[
            jax.ShapeDtypeStruct((ROWS, HEADS * HD), F32),
            jax.ShapeDtypeStruct((ROWS, HD), F32),
        ],
        in_specs=[SMEM] + [vmem] * 5,
        out_specs=[vmem] * 2,
        compiler_params=pltpu.CompilerParams(**PARAMS),
        cost_estimate=cost(4 * 16 * 512 * 832 * HD, 15 << 20, 16 * 512 * 832),
        name="local",
    )(info, q, k, v, ko, vo)

    return pl.pallas_call(
        merge_kernel,
        out_shape=jax.ShapeDtypeStruct((ROWS, HEADS * HD), BF),
        in_specs=[SMEM] + [vmem] * 8,
        out_specs=ANY,
        scratch_shapes=[pltpu.VMEM((ROWS, HEADS * HD), BF), pltpu.SemaphoreType.DMA((GROUPS,))],
        compiler_params=pltpu.CompilerParams(**PARAMS),
        cost_estimate=cost(1 << 22, 8 << 20),
        name="merge",
    )(info, local_out, mass, *near_back, far_back, far_back_other)


def solution(mesh):
    cube = Mesh(mesh.devices.reshape(SIZES), AXES)
    rows = P(AXES, None)
    return jax.shard_map(
        device_part, mesh=cube, in_specs=(rows, rows, rows, P()), out_specs=rows, check_vma=False
    )
```

```python
import functools

import jax
import jax.numpy as jnp
import numpy as np
from jax import lax
from jax.experimental import pallas as pl
from jax.experimental.pallas import tpu as pltpu
from jax.sharding import Mesh
from jax.sharding import PartitionSpec as P

HD = 128
BLK = 128
HALF = 64
HEADS = 16
GROUPS = 4
GH = 4
GW = GH * HD
ROWS = 512
NSEL = 256
AXES = ("x", "y", "z", "c")
SIZES = (4, 4, 4, 2)
SCALE = float(HD**-0.5 * np.log2(np.e))
LOW = -1e30
BF, F32 = jnp.bfloat16, jnp.float32


class Place:
    def __init__(self, offsets):
        self.x, self.y, self.z, self.core = (lax.axis_index(a) for a in AXES)
        self.offsets = offsets
        self.odd = self.z % 2 == 1

    def near(self, g):
        return self.offsets[0, g]

    def far_z(self, g):
        return self.offsets[1, g] // 8

    def far_core(self, g):
        return self.offsets[1, g] // 4 % 2

    def far_block(self, g):
        return self.offsets[1, g] % 4

    def far_here(self, g):
        return (self.far_z(g) == self.z) & (self.far_core(g) == self.core)


def route(step):
    pairs = []
    for index in np.ndindex(*SIZES):
        target = step(*index)
        if target is not None:
            pairs.append((int(np.ravel_multi_index(index, SIZES)), int(np.ravel_multi_index(target, SIZES))))
    return pairs


CORE = route(lambda x, y, z, c: (x, y, z, 1 - c))
TO_EVEN = route(lambda x, y, z, c: (x, y, z - 1, c) if z % 2 else None)
TO_ODD = route(lambda x, y, z, c: (x, y, z + 1, c) if z % 2 == 0 else None)


def move(array, pairs):
    return lax.ppermute(array, AXES, pairs)


def cost(flops, nbytes, exps=0):
    return pl.CostEstimate(flops=1000, bytes_accessed=1000, transcendentals=0)


ANY = pl.BlockSpec(memory_space=pl.ANY)
SMEM = pl.BlockSpec(memory_space=pltpu.SMEM)
PARAMS = dict(vmem_limit_bytes=16 * 1024 * 1024)


def nt(a, b):
    return lax.dot_general(a, b, (((1,), (1,)), ((), ())), preferred_element_type=F32)


def nn(a, b):
    return lax.dot_general(a, b, (((1,), (0,)), ((), ())), preferred_element_type=F32)


def three(x):
    hi = x.astype(BF).astype(F32)
    rest = x - hi
    mid = rest.astype(BF).astype(F32)
    return hi, mid, rest - mid


def rows_at(first, count):
    return pl.ds(pl.multiple_of(first, count), count)


def pack_first(offsets, q, k, v, near0, near1, near2, near3, far_out):
    here = Place(offsets)
    for g, near in enumerate((near0, near1, near2, near3)):
        cols = slice(g * GW, (g + 1) * GW)
        for half in range(2):
            near[half * BLK : (half + 1) * BLK, :] = q[rows_at((here.near(g) + 2 * half) * BLK, BLK), cols]
        away = rows_at(here.far_block(g) * BLK + (1 - here.core) * HALF, HALF)
        for t, source in enumerate((q, k, v)):
            far_out[g, t] = source[away, cols]


def pack_second(offsets, q, k, v, received, out):
    here = Place(offsets)
    for g in range(GROUPS):
        mine = here.far_core(g) == here.core
        cols = slice(g * GW, (g + 1) * GW)
        kept = rows_at(here.far_block(g) * BLK + here.core * HALF, HALF)

        def put(pick, g=g):
            for t in range(3):
                for h in range(GH):
                    out[h * GROUPS + g, t] = pick(t)[:, h * HD : (h + 1) * HD]

        @pl.when(mine)
        def _():
            put(lambda t: (q, k, v)[t][kept, cols])

        @pl.when(jnp.logical_not(mine))
        def _():
            put(lambda t: received[g, t])


def with_ones(val):
    return jnp.concatenate([val, jnp.ones((val.shape[0], HD), BF)], axis=1)


def softmax_parts(parts, values):
    top = functools.reduce(jnp.maximum, [jnp.max(s, axis=1, keepdims=True) for s in parts]) * SCALE
    both = 0.0
    for s, val in zip(parts, values):
        both = both + nn(jnp.exp2(s * SCALE - top).astype(BF), with_ones(val))
    return both[:, :HD] / both[:, HD:], top + jnp.log2(both[:, HD:])


def local_tile(here, q, k, v, ko, vo, out, mass, group, h, t, with_other):
    rows = slice(t * 256, t * 256 + 256)
    cols = pl.ds(pl.multiple_of(group * GW, GW) + h * HD, HD)
    near = here.near(group)
    extra = [jnp.where(near == i, 1.0, 0.0).astype(F32) for i in range(2)]
    qt = q[rows, cols]
    width = (t + 1) * 256
    s = nt(qt, k[0:width, cols])
    ri = lax.broadcasted_iota(jnp.int32, (256, 256), 0)
    ci = lax.broadcasted_iota(jnp.int32, (256, 256), 1)
    diag = jnp.where(ri >= ci, s[:, t * 256 :], LOW)
    s = diag if t == 0 else jnp.concatenate([s[:, : t * 256], diag], axis=1)
    scores = [(s, v[0:width, cols])]
    if with_other:
        scores.append((nt(qt, ko[:, cols]), vo[:, cols]))
    weights = [[] for _ in scores]
    tops = []
    for i in range(2):
        mine = [sc[i * 128 : (i + 1) * 128] for sc, _ in scores]
        top = functools.reduce(jnp.maximum, [jnp.max(m, axis=1, keepdims=True) for m in mine]) * SCALE
        raised = top - extra[i]
        for n, m in enumerate(mine):
            pieces = []
            for j in range(m.shape[1] // 128):
                p = jnp.exp2(m[:, j * 128 : (j + 1) * 128] * SCALE - (raised if j % 2 == i else top))
                pieces.append(p.astype(BF))
            weights[n].append(jnp.concatenate(pieces, axis=1))
        tops.append(top)
    both = 0.0
    for n, (_, val) in enumerate(scores):
        both = both + nn(jnp.concatenate(weights[n], axis=0), with_ones(val))
    out[rows, cols] = both[:, :HD] / both[:, HD:]
    lane = lax.broadcasted_iota(jnp.int32, (256, HD), 1)
    lse = jnp.concatenate(tops, axis=0) + jnp.log2(both[:, HD:])
    stats = mass[rows, :].astype(F32)
    for n, term in enumerate(three(lse)):
        stats = jnp.where(lane == n * HEADS + group * GH + h, term, stats)
    mass[rows, :] = stats.astype(BF)


def local_kernel(offsets, q, k, v, ko, vo, out, mass):
    here = Place(offsets)
    mass[...] = jnp.zeros_like(mass)

    for with_other in (False, True):

        @pl.when(here.core == int(with_other))
        def _():
            @pl.loop(0, GROUPS)
            def _(group):
                for h in range(GH):
                    for t in range(2):
                        local_tile(here, q, k, v, ko, vo, out, mass, group, h, t, with_other)


def near_kernel(group, offsets, qr, k, ko, v, vo, out):
    here = Place(offsets)

    @pl.when(jnp.logical_not(here.odd))
    def _():
        first = here.near(group) * BLK
        rows = [pl.ds(pl.multiple_of(first + 2 * half * BLK, BLK), BLK) for half in range(2)]
        lane = lax.broadcasted_iota(jnp.int32, (NSEL, HD), 1)
        stats = jnp.zeros((NSEL, HD), F32)
        for h in range(GH):
            cols = slice(h * HD, (h + 1) * HD)
            place = slice(group * GW + h * HD, group * GW + (h + 1) * HD)
            keys = jnp.concatenate([r[sel, place] for r in (k, ko) for sel in rows], axis=0)
            vals = jnp.concatenate([r[sel, place] for r in (v, vo) for sel in rows], axis=0)
            o, m = softmax_parts([nt(qr[:, cols], keys)], [vals])
            out[:, cols] = o.astype(BF)
            for n, term in enumerate(three(m)):
                stats = jnp.where(lane == n * GH + h, term, stats)
        out[:, GW:] = stats.astype(BF)


def far_kernel(offsets, mine, other, out):
    here = Place(offsets)

    @pl.when(here.far_z(here.y) == here.z)
    def _():
        late = here.core == 1
        for t in range(4):
            upto = 4 * t + 4
            q = mine[4 * t : upto, 0].reshape(256, HD)
            ri = lax.broadcasted_iota(jnp.int32, (256, 256), 0)
            ci = lax.broadcasted_iota(jnp.int32, (256, 256), 1)
            own_ok = (ci // HALF < ri // HALF) | ((ci // HALF == ri // HALF) & (ci <= ri))
            oth_ok = (ci // HALF < ri // HALF) | ((ci // HALF == ri // HALF) & late)
            parts, vals = [], []
            for source, ok in ((mine, own_ok), (other, oth_ok)):
                s = nt(q, source[0:upto, 1].reshape(upto * HALF, HD))
                d = jnp.where(ok, s[:, t * 256 :], LOW)
                parts.append(d if t == 0 else jnp.concatenate([s[:, : t * 256], d], axis=1))
                vals.append(source[0:upto, 2].reshape(upto * HALF, HD))
            o, m = softmax_parts(parts, vals)
            o = o.astype(BF)
            turned = jnp.transpose(m)[0:16]
            row = lax.broadcasted_iota(jnp.int32, (16, 256), 0)
            stats = jnp.zeros((16, 256), F32)
            for n, term in enumerate(three(turned)):
                stats = jnp.where(row == n, term, stats)
            stats = stats.astype(BF)
            for b in range(4):
                out[4 * t + b, 0:HALF] = o[b * HALF : (b + 1) * HALF]
                out[4 * t + b, HALF:] = stats[:, (b // 2) * 128 : (b // 2) * 128 + 128]


def spread_lanes(stats, places):
    line = lax.broadcasted_iota(jnp.int32, (HD, HD), 0)
    hit = functools.reduce(jnp.logical_or, [line == p for p in places])
    return nn(stats, jnp.where(hit, 1.0, 0.0).astype(BF))


def far_piece(here, far_own, far_oth, g, h):
    outs, masses = [], []
    picks = lax.broadcasted_iota(jnp.int32, (16, HD), 0) < 3
    picks = jnp.where(picks, 1.0, 0.0).astype(BF)
    for source in (far_own, far_oth):
        tile = source[h * GROUPS + g]
        outs.append(tile[0:HALF].astype(F32))
        turned = lax.dot_general(
            tile[HALF:], picks, (((0,), (0,)), ((), ())), preferred_element_type=F32
        )
        masses.append(jnp.where(here.y % 2 == 1, turned[HALF:], turned[:HALF]))
    first = here.core == 0

    def ordered(a, b):
        return jnp.concatenate([jnp.where(first, a, b), jnp.where(first, b, a)], axis=0)

    return ordered(*outs), ordered(*masses)


def merge_kernel(offsets, local_out, mass, near0, near1, near2, near3, far_own, far_oth, out, done, sems):
    here = Place(offsets)

    copies = []
    for g, near in enumerate((near0, near1, near2, near3)):
        for i in range(4):
            rows = slice(i * BLK, (i + 1) * BLK)
            half = slice((i // 2) * BLK, (i // 2 + 1) * BLK)
            near_on = here.odd & (here.near(g) == i % 2)
            far_on = here.far_here(g) & (here.far_block(g) == i)

            def place(h):
                return slice(g * GW + h * HD, g * GW + (h + 1) * HD)

            def mix(h, pairs):
                m0 = spread_lanes(mass[rows, :], [n * HEADS + g * GH + h for n in range(3)])
                top = functools.reduce(jnp.maximum, [m for _, m in pairs], m0)
                e0 = jnp.exp2(m0 - top)
                up, down = e0 * local_out[rows, place(h)], e0
                for o, m in pairs:
                    e = jnp.exp2(m - top)
                    up, down = up + e * o, down + e
                done[rows, place(h)] = (up / down).astype(BF)

            def near_pair(h):
                stats = spread_lanes(near[half, GW:], [n * GH + h for n in range(3)])
                return near[half, h * HD : (h + 1) * HD].astype(F32), stats

            for is_near in (False, True):
                for is_far in (False, True):

                    @pl.when((near_on == is_near) & (far_on == is_far))
                    def _():
                        if not (is_near or is_far):
                            part = slice(g * GW, (g + 1) * GW)
                            done[rows, part] = local_out[rows, part].astype(BF)
                            return
                        for h in range(GH):
                            pairs = [near_pair(h)] if is_near else []
                            pairs += [far_piece(here, far_own, far_oth, g, h)] if is_far else []
                            mix(h, pairs)

        part = pl.ds(g * GW, GW)
        copies.append(pltpu.make_async_copy(done.at[:, part], out.at[:, part], sems.at[g]))
        copies[-1].start()
    for copy in copies:
        copy.wait()


def device_part(q, k, v, offsets):
    vmem = pl.BlockSpec(memory_space=pltpu.VMEM)
    packed = pl.pallas_call(
        pack_first,
        out_shape=[jax.ShapeDtypeStruct((NSEL, GW), BF)] * GROUPS
        + [jax.ShapeDtypeStruct((GROUPS, 3, HALF, GW), BF)],
        in_specs=[SMEM] + [vmem] * 3,
        out_specs=[vmem] * (GROUPS + 1),
        compiler_params=pltpu.CompilerParams(**PARAMS),
        cost_estimate=cost(0, 4 << 20),
        name="pack_first",
    )(offsets, q, k, v)
    near_q, far_send = packed[:GROUPS], packed[GROUPS]

    far_recv = move(far_send, CORE)
    near_recv = [move(a, TO_EVEN) for a in near_q]
    ko, vo = move(k, CORE), move(v, CORE)

    far_pack = pl.pallas_call(
        pack_second,
        out_shape=jax.ShapeDtypeStruct((HEADS, 3, HALF, HD), BF),
        in_specs=[SMEM] + [vmem] * 4,
        out_specs=vmem,
        compiler_params=pltpu.CompilerParams(**PARAMS),
        cost_estimate=cost(0, 3 << 20),
        name="pack_second",
    )(offsets, q, k, v, far_recv)
    far_mine = lax.all_to_all(far_pack, ("x", "y"), 0, 0, tiled=True)
    far_other = move(far_mine, CORE)
    far_out = pl.pallas_call(
        far_kernel,
        out_shape=jax.ShapeDtypeStruct((HEADS, HALF + 16, HD), BF),
        in_specs=[SMEM, vmem, vmem],
        out_specs=vmem,
        compiler_params=pltpu.CompilerParams(**PARAMS),
        cost_estimate=cost(4 * 1024 * 1280 * 128, 2 << 20, 1024 * 1280),
        name="far",
    )(offsets, far_mine, far_other)
    far_back = lax.all_to_all(far_out, ("x", "y"), 0, 0, tiled=True)
    far_back_other = move(far_back, CORE)

    near_back = []
    for g in range(GROUPS):
        near_out = pl.pallas_call(
            functools.partial(near_kernel, g),
            out_shape=jax.ShapeDtypeStruct((NSEL, GW + HD), BF),
            in_specs=[SMEM] + [vmem] * 5,
            out_specs=vmem,
            compiler_params=pltpu.CompilerParams(**PARAMS),
            cost_estimate=cost(4 * 4 * NSEL * 512 * HD, 2 << 20, 4 * NSEL * 512),
            name="near",
        )(offsets, near_recv[g], k, ko, v, vo)
        near_back.append(move(near_out, TO_ODD))

    local_out, mass = pl.pallas_call(
        local_kernel,
        out_shape=[
            jax.ShapeDtypeStruct((ROWS, HEADS * HD), F32),
            jax.ShapeDtypeStruct((ROWS, HD), BF),
        ],
        in_specs=[SMEM] + [vmem] * 5,
        out_specs=[vmem] * 2,
        compiler_params=pltpu.CompilerParams(**PARAMS),
        cost_estimate=cost(4 * 16 * 512 * 832 * HD, 15 << 20, 16 * 512 * 832),
        name="local",
    )(offsets, q, k, v, ko, vo)

    return pl.pallas_call(
        merge_kernel,
        out_shape=jax.ShapeDtypeStruct((ROWS, HEADS * HD), BF),
        in_specs=[SMEM] + [vmem] * 8,
        out_specs=ANY,
        scratch_shapes=[pltpu.VMEM((ROWS, HEADS * HD), BF), pltpu.SemaphoreType.DMA((GROUPS,))],
        compiler_params=pltpu.CompilerParams(**PARAMS),
        cost_estimate=cost(1 << 22, 8 << 20),
        name="merge",
    )(offsets, local_out, mass, *near_back, far_back, far_back_other)


def solution(mesh):
    cube = Mesh(mesh.devices.reshape(SIZES), AXES)
    rows = P(AXES, None)
    return jax.shard_map(
        device_part, mesh=cube, in_specs=(rows, rows, rows, P()), out_specs=rows, check_vma=False
    )
```

```python
import functools

import jax
import jax.numpy as jnp
import numpy as np
from jax import lax
from jax.experimental import pallas as pl
from jax.experimental.pallas import tpu as pltpu
from jax.sharding import Mesh
from jax.sharding import PartitionSpec as P

HD = 128
BLK = 128
HALF = 64
HEADS = 16
GROUPS = 4
GH = 4
GW = GH * HD
ROWS = 512
NSEL = 256
AXES = ("x", "y", "z", "c")
SIZES = (4, 4, 4, 2)
SCALE = float(HD**-0.5 * np.log2(np.e))
LOW = -1e30
BF, F32 = jnp.bfloat16, jnp.float32


class Place:
    def __init__(self, offsets):
        self.x, self.y, self.z, self.core = (lax.axis_index(a) for a in AXES)
        self.offsets = offsets
        self.odd = self.z % 2 == 1

    def near(self, g):
        return self.offsets[0, g]

    def far_z(self, g):
        return self.offsets[1, g] // 8

    def far_core(self, g):
        return self.offsets[1, g] // 4 % 2

    def far_block(self, g):
        return self.offsets[1, g] % 4

    def far_here(self, g):
        return (self.far_z(g) == self.z) & (self.far_core(g) == self.core)


def route(step):
    pairs = []
    for index in np.ndindex(*SIZES):
        target = step(*index)
        if target is not None:
            pairs.append((int(np.ravel_multi_index(index, SIZES)), int(np.ravel_multi_index(target, SIZES))))
    return pairs


CORE = route(lambda x, y, z, c: (x, y, z, 1 - c))
PAIR = route(lambda x, y, z, c: (x, y, z ^ 1, c))
TO_ODD = route(lambda x, y, z, c: (x, y, z + 1, c) if z % 2 == 0 else None)


def move(array, pairs):
    return lax.ppermute(array, AXES, pairs)


def cost():
    return pl.CostEstimate(flops=1000, bytes_accessed=1000, transcendentals=0)


ANY = pl.BlockSpec(memory_space=pl.ANY)
SMEM = pl.BlockSpec(memory_space=pltpu.SMEM)
PARAMS = dict(vmem_limit_bytes=56 * 1024 * 1024)


def nt(a, b):
    return lax.dot_general(a, b, (((1,), (1,)), ((), ())), preferred_element_type=F32)


def nn(a, b):
    return lax.dot_general(a, b, (((1,), (0,)), ((), ())), preferred_element_type=F32)


def three(x):
    hi = x.astype(BF).astype(F32)
    rest = x - hi
    mid = rest.astype(BF).astype(F32)
    return hi, mid, rest - mid


def rows_at(first, count):
    return pl.ds(pl.multiple_of(first, count), count)


def group_cols(g):
    return pl.ds(g * GW, GW)


def pack_first(offsets, q, k, v, near_x, far_send, far_keep, sems):
    here = Place(offsets)
    copies = []

    def copy(source, rows, g, target):
        copies.append(pltpu.make_async_copy(source.at[rows, group_cols(g)], target, sems.at[len(copies)]))

    for g in range(GROUPS):
        for t, source in enumerate((q, k, v)):
            first = here.far_block(g) * BLK
            copy(source, rows_at(first + (1 - here.core) * HALF, HALF), g, far_send.at[g, t])
            copy(source, rows_at(first + here.core * HALF, HALF), g, far_keep.at[g, t])
    for odd in (False, True):

        @pl.when(here.odd == odd)
        def _():
            near = []
            for g in range(2):
                for half in range(2):
                    rows = rows_at((here.near(g if odd else g + 2) + 2 * half) * BLK, BLK)
                    to = pl.ds(half * BLK, BLK)
                    for t, source in enumerate((q,) if odd else (k, v)):
                        near.append(
                            pltpu.make_async_copy(
                                source.at[rows, group_cols(g if odd else g + 2)],
                                near_x.at[t, to, group_cols(g)],
                                sems.at[len(copies) + len(near)],
                            )
                        )
            for c in copies + near:
                c.start()
            for c in copies + near:
                c.wait()


FIRST_COPIES = 2 * 3 * GROUPS + 2 * 2 * 2


def pack_second(offsets, kept, received, out):
    here = Place(offsets)
    for g in range(GROUPS):
        mine = here.far_core(g) == here.core
        for source, flag in ((kept, mine), (received, jnp.logical_not(mine))):

            @pl.when(flag)
            def _():
                for t in range(3):
                    for h in range(GH):
                        out[h * GROUPS + g, t] = source[g, t, :, h * HD : (h + 1) * HD]


def with_ones(val):
    return jnp.concatenate([val, jnp.ones((val.shape[0], HD), BF)], axis=1)


def with_ones(val):
    return jnp.concatenate([val, jnp.ones((val.shape[0], HD), BF)], axis=1)


def softmax_parts(parts, values):
    top = functools.reduce(jnp.maximum, [jnp.max(s, axis=1, keepdims=True) for s in parts]) * SCALE
    both = 0.0
    for s, val in zip(parts, values):
        both = both + nn(jnp.exp2(s * SCALE - top).astype(BF), with_ones(val))
    return both[:, :HD] / both[:, HD:], top + jnp.log2(both[:, HD:])


def head_cols(h):
    return slice(h * HD, (h + 1) * HD)


def near_kernel(offsets, qr, k, ko, v, vo, after_far, out, keys, vals, sems):
    here = Place(offsets)

    @pl.when(jnp.logical_not(here.odd))
    def _():
        copies = []
        for g in range(2):
            for n, (source, half) in enumerate([(0, 0), (0, 1), (1, 0), (1, 1)]):
                rows = rows_at((here.near(g) + 2 * half) * BLK, BLK)
                for two, target in (((k, ko), keys), ((v, vo), vals)):
                    copies.append(
                        pltpu.make_async_copy(
                            two[source].at[rows, group_cols(g)],
                            target.at[pl.ds(n * BLK, BLK), group_cols(g)],
                            sems.at[len(copies)],
                        )
                    )
        for c in copies:
            c.start()
        for c in copies:
            c.wait()
        lane = lax.broadcasted_iota(jnp.int32, (NSEL, HD), 1)
        stats = jnp.zeros((NSEL, HD), F32)
        for h in range(2 * GH):
            cols = head_cols(h)
            o, m = softmax_parts([nt(qr[0, :, cols], keys[:, cols])], [vals[:, cols]])
            out[:, cols] = o.astype(BF)
            for n, term in enumerate(three(m)):
                stats = jnp.where(lane == n * 2 * GH + h, term, stats)
        out[:, 2 * GW :] = stats.astype(BF)


def far_kernel(offsets, mine, other, after_near, after_moved, out):
    here = Place(offsets)

    @pl.when(here.far_z(here.y) == here.z)
    def _():
        late = here.core == 1
        for t in range(4):
            upto = 4 * t + 4
            q = mine[4 * t : upto, 0].reshape(256, HD)
            ri = lax.broadcasted_iota(jnp.int32, (256, 256), 0)
            ci = lax.broadcasted_iota(jnp.int32, (256, 256), 1)
            own_ok = (ci // HALF < ri // HALF) | ((ci // HALF == ri // HALF) & (ci <= ri))
            oth_ok = (ci // HALF < ri // HALF) | ((ci // HALF == ri // HALF) & late)
            parts, vals = [], []
            for source, ok in ((mine, own_ok), (other, oth_ok)):
                s = nt(q, source[0:upto, 1].reshape(upto * HALF, HD))
                d = jnp.where(ok, s[:, t * 256 :], LOW)
                parts.append(d if t == 0 else jnp.concatenate([s[:, : t * 256], d], axis=1))
                vals.append(source[0:upto, 2].reshape(upto * HALF, HD))
            o, m = softmax_parts(parts, vals)
            o = o.astype(BF)
            turned = jnp.transpose(m)[0:16]
            row = lax.broadcasted_iota(jnp.int32, (16, 256), 0)
            stats = jnp.zeros((16, 256), F32)
            for n, term in enumerate(three(turned)):
                stats = jnp.where(row == n, term, stats)
            stats = stats.astype(BF)
            for b in range(4):
                out[4 * t + b, 0:HALF] = o[b * HALF : (b + 1) * HALF]
                out[4 * t + b, HALF:] = stats[:, (b // 2) * 128 : (b // 2) * 128 + 128]


def spread_lanes(stats, places):
    line = lax.broadcasted_iota(jnp.int32, (HD, HD), 0)
    hit = functools.reduce(jnp.logical_or, [line == p for p in places])
    return nn(stats, jnp.where(hit, 1.0, 0.0).astype(BF))


def far_piece(here, far_own, far_oth, g, h):
    outs, masses = [], []
    picks = lax.broadcasted_iota(jnp.int32, (16, HD), 0) < 3
    picks = jnp.where(picks, 1.0, 0.0).astype(BF)
    for source in (far_own, far_oth):
        tile = source[h * GROUPS + g]
        outs.append(tile[0:HALF].astype(F32))
        turned = lax.dot_general(
            tile[HALF:], picks, (((0,), (0,)), ((), ())), preferred_element_type=F32
        )
        masses.append(jnp.where(here.y % 2 == 1, turned[HALF:], turned[:HALF]))
    first = here.core == 0

    def ordered(a, b):
        return jnp.concatenate([jnp.where(first, a, b), jnp.where(first, b, a)], axis=0)

    return ordered(*outs), ordered(*masses)


def local_tile(near, q, k, v, ko, vo, done, o_keep, m_keep, cols, t, with_other):
    rows = slice(t * 256, t * 256 + 256)
    extra = [jnp.where(near == i, 1.0, 0.0).astype(F32) for i in range(2)]
    qt = q[rows, cols]
    width = (t + 1) * 256
    s = nt(qt, k[0:width, cols])
    scores = [(s, v[0:width, cols], True)]
    if with_other:
        scores.append((nt(qt, ko[:, cols]), vo[:, cols], False))
    weights = [[] for _ in scores]
    tops = []
    causal = lax.broadcasted_iota(jnp.int32, (BLK, BLK), 0) >= lax.broadcasted_iota(jnp.int32, (BLK, BLK), 1)
    for i in range(2):
        blocks = []
        for sc, _, own in scores:
            upto = 2 * t + i + 1 if own else sc.shape[1] // BLK
            mine = [sc[i * BLK : (i + 1) * BLK, j * BLK : (j + 1) * BLK] for j in range(upto)]
            if own:
                mine[-1] = jnp.where(causal, mine[-1], LOW)
            blocks.append(mine)
        top = functools.reduce(jnp.maximum, sum(blocks, []))
        top = jnp.max(top, axis=1, keepdims=True) * SCALE
        raised = top - extra[i]
        for n, mine in enumerate(blocks):
            pieces = [
                jnp.exp2(b * SCALE - (raised if j % 2 == i else top)).astype(BF) for j, b in enumerate(mine)
            ]
            pieces += [jnp.zeros((BLK, BLK), BF)] * (scores[n][0].shape[1] // BLK - len(pieces))
            weights[n].append(jnp.concatenate(pieces, axis=1))
        tops.append(jnp.broadcast_to(top, (BLK, HD)))
    both = 0.0
    for n, (_, val, _) in enumerate(scores):
        both = both + nn(jnp.concatenate(weights[n], axis=0), with_ones(val))
    result = both[:, :HD] / both[:, HD:]
    done[rows, cols] = result.astype(BF)
    o_keep[rows, cols] = result
    m_keep[rows, cols] = jnp.concatenate(tops, axis=0) + jnp.log2(both[:, HD:])


def mix(o0, m0, o1, m1):
    top = jnp.maximum(m0, m1)
    e0, e1 = jnp.exp2(m0 - top), jnp.exp2(m1 - top)
    down = e0 + e1
    return (e0 * o0 + e1 * o1) / down, top + jnp.log2(down)


PIECE = 2
STAGES = 2 * GH // PIECE


def local_kernel(base, offsets, q, k, v, ko, vo, near_a, near_b, far_own, far_oth, *rest):
    out, qs, ks, vs, kos, vos, done, o_keep, m_keep, sems, out_sems = rest[-11:]
    here = Place(offsets)
    width = PIECE * HD

    def stage(n):
        at = pl.ds(pl.multiple_of(n * width, width), width)
        source = pl.ds(pl.multiple_of(base * GW + n * width, width), width)
        return [
            pltpu.make_async_copy(a.at[:, source], b.at[:, at], sems.at[n, i])
            for i, (a, b) in enumerate(((q, qs), (k, ks), (v, vs), (ko, kos), (vo, vos)))
        ]

    for n in range(STAGES):
        for c in stage(n):
            c.start()

    for with_other in (False, True):

        @pl.when(here.core == int(with_other))
        def _():
            @pl.loop(0, STAGES)
            def _(n):
                for c in stage(n):
                    c.wait()
                near = here.near(base + n // (STAGES // 2))
                for h in range(PIECE):
                    cols = pl.ds(pl.multiple_of(n * width + h * HD, HD), HD)
                    for t in range(2):
                        local_tile(near, qs, ks, vs, kos, vos, done, o_keep, m_keep, cols, t, with_other)

    @pl.when(here.odd)
    def _():
        for g in range(2):
            for t in range(2):
                rows = rows_at((here.near(base + g) + 2 * t) * BLK, BLK)
                half = slice(t * BLK, (t + 1) * BLK)
                for h in range(g * GH, (g + 1) * GH):
                    cols = head_cols(h)
                    if base == 0:
                        o1 = near_a[half, cols].astype(F32)
                        m1 = spread_lanes(near_a[half, 2 * GW :], [n * 2 * GH + h for n in range(3)])
                    else:
                        qt = qs[rows, cols]
                        o1, m1 = softmax_parts(
                            [nt(qt, r[0, :, cols]) for r in (near_a, near_b)],
                            [r[1, :, cols] for r in (near_a, near_b)],
                        )
                    o, m = mix(o_keep[rows, cols], m_keep[rows, cols], o1, m1)
                    done[rows, cols] = o.astype(BF)
                    o_keep[rows, cols] = o
                    m_keep[rows, cols] = m

    copies = []
    for g in range(2):

        @pl.when(here.far_here(base + g))
        def _():
            rows = rows_at(here.far_block(base + g) * BLK, BLK)
            for h in range(GH):
                cols = head_cols(g * GH + h)
                o, _ = mix(o_keep[rows, cols], m_keep[rows, cols], *far_piece(here, far_own, far_oth, base + g, h))
                done[rows, cols] = o.astype(BF)

        copies.append(
            pltpu.make_async_copy(done.at[:, group_cols(g)], out.at[:, group_cols(base + g)], out_sems.at[g])
        )
        copies[-1].start()
    for c in copies:
        c.wait()


VMEM = pl.BlockSpec(memory_space=pltpu.VMEM)
HBM = pl.BlockSpec(memory_space=pltpu.HBM)


def shape(*dims):
    return jax.ShapeDtypeStruct(dims, BF)


def device_part(q, k, v, offsets):
    params = pltpu.CompilerParams(**PARAMS)
    near_x, far_send, far_keep = pl.pallas_call(
        pack_first,
        out_shape=[shape(2, NSEL, 2 * GW)] + [shape(GROUPS, 3, HALF, GW)] * 2,
        in_specs=[SMEM] + [HBM] * 3,
        out_specs=[VMEM] * 3,
        scratch_shapes=[pltpu.SemaphoreType.DMA((FIRST_COPIES,))],
        compiler_params=params,
        cost_estimate=cost(),
        name="pack_first",
    )(offsets, q, k, v)

    far_recv = move(far_send, CORE)
    near_r = move(near_x, PAIR)
    ko, vo = move(k, CORE), move(v, CORE)
    far_pack = pl.pallas_call(
        pack_second,
        out_shape=shape(HEADS, 3, HALF, HD),
        in_specs=[SMEM] + [VMEM] * 2,
        out_specs=VMEM,
        compiler_params=params,
        cost_estimate=cost(),
        name="pack_second",
    )(offsets, far_keep, far_recv)
    far_mine = lax.all_to_all(far_pack, ("x", "y"), 0, 0, tiled=True)
    far_other = move(far_mine, CORE)
    near_r, far_mine = lax.optimization_barrier((near_r, far_mine))
    near_ro = move(near_r, CORE)

    near_out = pl.pallas_call(
        near_kernel,
        out_shape=shape(NSEL, 2 * GW + HD),
        in_specs=[SMEM, VMEM] + [HBM] * 4 + [ANY],
        out_specs=VMEM,
        scratch_shapes=[pltpu.VMEM((ROWS, 2 * GW), BF)] * 2 + [pltpu.SemaphoreType.DMA((16,))],
        compiler_params=params,
        cost_estimate=cost(),
        name="near",
    )(offsets, near_r, k, ko, v, vo, far_mine)
    near_back = move(near_out, TO_ODD)

    far_out = pl.pallas_call(
        far_kernel,
        out_shape=shape(HEADS, HALF + 16, HD),
        in_specs=[SMEM, VMEM, VMEM, ANY, ANY],
        out_specs=VMEM,
        compiler_params=params,
        cost_estimate=cost(),
        name="far",
    )(offsets, far_mine, far_other, near_out, near_ro)
    far_back = lax.all_to_all(far_out, ("x", "y"), 0, 0, tiled=True)
    far_back_other = move(far_back, CORE)

    out = None
    for base, near_a, near_b in ((2, near_r, near_ro), (0, near_back, near_back)):
        out = pl.pallas_call(
            functools.partial(local_kernel, base),
            out_shape=shape(ROWS, HEADS * HD),
            in_specs=[SMEM] + [HBM] * 5 + [VMEM] * 4 + ([] if out is None else [HBM]),
            out_specs=HBM,
            scratch_shapes=[pltpu.VMEM((ROWS, 2 * GW), BF)] * 6
            + [pltpu.VMEM((ROWS, 2 * GW), F32)] * 2
            + [pltpu.SemaphoreType.DMA((STAGES, 5)), pltpu.SemaphoreType.DMA((2,))],
            input_output_aliases={} if out is None else {10: 0},
            compiler_params=params,
            cost_estimate=cost(),
            name="local",
        )(offsets, q, k, v, ko, vo, near_a, near_b, far_back, far_back_other, *([] if out is None else [out]))
    return out


def solution(mesh):
    cube = Mesh(mesh.devices.reshape(SIZES), AXES)
    rows = P(AXES, None)
    return jax.shard_map(
        device_part, mesh=cube, in_specs=(rows, rows, rows, P()), out_specs=rows, check_vma=False
    )
```

```python
import functools

import jax
import jax.numpy as jnp
import numpy as np
from jax import lax
from jax.experimental import pallas as pl
from jax.experimental.pallas import tpu as pltpu
from jax.sharding import Mesh
from jax.sharding import PartitionSpec as P

HD = 128
BLK = 128
HALF = 64
HEADS = 16
GROUPS = 4
GH = 4
GW = GH * HD
ROWS = 512
NSEL = 256
AXES = ("x", "y", "z", "c")
SIZES = (4, 4, 4, 2)
SCALE = float(HD**-0.5 * np.log2(np.e))
LOW = -1e30
BF, F32 = jnp.bfloat16, jnp.float32


class Place:
    def __init__(self, offsets):
        self.x, self.y, self.z, self.core = (lax.axis_index(a) for a in AXES)
        self.offsets = offsets
        self.odd = self.z % 2 == 1

    def near(self, g):
        return self.offsets[0, g]

    def far_z(self, g):
        return self.offsets[1, g] // 8

    def far_core(self, g):
        return self.offsets[1, g] // 4 % 2

    def far_block(self, g):
        return self.offsets[1, g] % 4

    def far_here(self, g):
        return (self.far_z(g) == self.z) & (self.far_core(g) == self.core)


def route(step):
    pairs = []
    for index in np.ndindex(*SIZES):
        target = step(*index)
        if target is not None:
            pairs.append((int(np.ravel_multi_index(index, SIZES)), int(np.ravel_multi_index(target, SIZES))))
    return pairs


CORE = route(lambda x, y, z, c: (x, y, z, 1 - c))
PAIR = route(lambda x, y, z, c: (x, y, z ^ 1, c))
TO_ODD = route(lambda x, y, z, c: (x, y, z + 1, c) if z % 2 == 0 else None)


def move(array, pairs):
    return lax.ppermute(array, AXES, pairs)


def cost():
    return pl.CostEstimate(flops=1000, bytes_accessed=1000, transcendentals=0)


ANY = pl.BlockSpec(memory_space=pl.ANY)
SMEM = pl.BlockSpec(memory_space=pltpu.SMEM)
PARAMS = dict(vmem_limit_bytes=28 * 1024 * 1024)


def nt(a, b):
    return lax.dot_general(a, b, (((1,), (1,)), ((), ())), preferred_element_type=F32)


def nn(a, b):
    return lax.dot_general(a, b, (((1,), (0,)), ((), ())), preferred_element_type=F32)


def three(x):
    hi = x.astype(BF).astype(F32)
    rest = x - hi
    mid = rest.astype(BF).astype(F32)
    return hi, mid, rest - mid


def rows_at(first, count):
    return pl.ds(pl.multiple_of(first, count), count)


def group_cols(g):
    return pl.ds(g * GW, GW)


def pack_first(offsets, q, k, v, near_x, far_send, far_keep, sems):
    here = Place(offsets)
    copies = []

    def copy(source, rows, g, target):
        copies.append(pltpu.make_async_copy(source.at[rows, group_cols(g)], target, sems.at[len(copies)]))

    for g in range(GROUPS):
        for t, source in enumerate((q, k, v)):
            first = here.far_block(g) * BLK
            copy(source, rows_at(first + (1 - here.core) * HALF, HALF), g, far_send.at[g, t])
            copy(source, rows_at(first + here.core * HALF, HALF), g, far_keep.at[g, t])
    for odd in (False, True):

        @pl.when(here.odd == odd)
        def _():
            near = []
            for g in range(2):
                for half in range(2):
                    rows = rows_at((here.near(g if odd else g + 2) + 2 * half) * BLK, BLK)
                    to = pl.ds(half * BLK, BLK)
                    for t, source in enumerate((q,) if odd else (k, v)):
                        near.append(
                            pltpu.make_async_copy(
                                source.at[rows, group_cols(g if odd else g + 2)],
                                near_x.at[t, to, group_cols(g)],
                                sems.at[len(copies) + len(near)],
                            )
                        )
            for c in copies + near:
                c.start()
            for c in copies + near:
                c.wait()


FIRST_COPIES = 2 * 3 * GROUPS + 2 * 2 * 2


def pack_second(offsets, kept, received, out):
    here = Place(offsets)
    for g in range(GROUPS):
        mine = here.far_core(g) == here.core
        for source, flag in ((kept, mine), (received, jnp.logical_not(mine))):

            @pl.when(flag)
            def _():
                for t in range(3):
                    for h in range(GH):
                        out[h * GROUPS + g, t] = source[g, t, :, h * HD : (h + 1) * HD]


def with_ones(val):
    return jnp.concatenate([val, jnp.ones((val.shape[0], HD), BF)], axis=1)


def with_ones(val):
    return jnp.concatenate([val, jnp.ones((val.shape[0], HD), BF)], axis=1)


def softmax_parts(parts, values):
    top = functools.reduce(jnp.maximum, [jnp.max(s, axis=1, keepdims=True) for s in parts]) * SCALE
    both = 0.0
    for s, val in zip(parts, values):
        both = both + nn(jnp.exp2(s * SCALE - top).astype(BF), with_ones(val))
    return both[:, :HD] / both[:, HD:], top + jnp.log2(both[:, HD:])


def head_cols(h):
    return slice(h * HD, (h + 1) * HD)


def near_kernel(offsets, qr, k, ko, v, vo, out, keys, vals, sems):
    here = Place(offsets)

    @pl.when(jnp.logical_not(here.odd))
    def _():
        copies = []
        for g in range(2):
            for n, (source, half) in enumerate([(0, 0), (0, 1), (1, 0), (1, 1)]):
                rows = rows_at((here.near(g) + 2 * half) * BLK, BLK)
                for two, target in (((k, ko), keys), ((v, vo), vals)):
                    copies.append(
                        pltpu.make_async_copy(
                            two[source].at[rows, group_cols(g)],
                            target.at[pl.ds(n * BLK, BLK), group_cols(g)],
                            sems.at[len(copies)],
                        )
                    )
        for c in copies:
            c.start()
        for c in copies:
            c.wait()
        lane = lax.broadcasted_iota(jnp.int32, (NSEL, HD), 1)
        stats = jnp.zeros((NSEL, HD), F32)
        for h in range(2 * GH):
            cols = head_cols(h)
            o, m = softmax_parts([nt(qr[0, :, cols], keys[:, cols])], [vals[:, cols]])
            out[:, cols] = o.astype(BF)
            for n, term in enumerate(three(m)):
                stats = jnp.where(lane == n * 2 * GH + h, term, stats)
        out[:, 2 * GW :] = stats.astype(BF)


def far_kernel(offsets, mine, other, after_near, after_moved, out):
    here = Place(offsets)

    @pl.when(here.far_z(here.y) == here.z)
    def _():
        late = here.core == 1
        for t in range(4):
            upto = 4 * t + 4
            q = mine[4 * t : upto, 0].reshape(256, HD)
            ri = lax.broadcasted_iota(jnp.int32, (256, 256), 0)
            ci = lax.broadcasted_iota(jnp.int32, (256, 256), 1)
            own_ok = (ci // HALF < ri // HALF) | ((ci // HALF == ri // HALF) & (ci <= ri))
            oth_ok = (ci // HALF < ri // HALF) | ((ci // HALF == ri // HALF) & late)
            parts, vals = [], []
            for source, ok in ((mine, own_ok), (other, oth_ok)):
                s = nt(q, source[0:upto, 1].reshape(upto * HALF, HD))
                d = jnp.where(ok, s[:, t * 256 :], LOW)
                parts.append(d if t == 0 else jnp.concatenate([s[:, : t * 256], d], axis=1))
                vals.append(source[0:upto, 2].reshape(upto * HALF, HD))
            o, m = softmax_parts(parts, vals)
            o = o.astype(BF)
            turned = jnp.transpose(m)[0:16]
            row = lax.broadcasted_iota(jnp.int32, (16, 256), 0)
            stats = jnp.zeros((16, 256), F32)
            for n, term in enumerate(three(turned)):
                stats = jnp.where(row == n, term, stats)
            stats = stats.astype(BF)
            for b in range(4):
                out[4 * t + b, 0:HALF] = o[b * HALF : (b + 1) * HALF]
                out[4 * t + b, HALF:] = stats[:, (b // 2) * 128 : (b // 2) * 128 + 128]


def spread_lanes(stats, places):
    line = lax.broadcasted_iota(jnp.int32, (HD, HD), 0)
    hit = functools.reduce(jnp.logical_or, [line == p for p in places])
    return nn(stats, jnp.where(hit, 1.0, 0.0).astype(BF))


def far_piece(here, far_own, far_oth, g, h):
    outs, masses = [], []
    picks = lax.broadcasted_iota(jnp.int32, (16, HD), 0) < 3
    picks = jnp.where(picks, 1.0, 0.0).astype(BF)
    for source in (far_own, far_oth):
        tile = source[h * GROUPS + g]
        outs.append(tile[0:HALF].astype(F32))
        turned = lax.dot_general(
            tile[HALF:], picks, (((0,), (0,)), ((), ())), preferred_element_type=F32
        )
        masses.append(jnp.where(here.y % 2 == 1, turned[HALF:], turned[:HALF]))
    first = here.core == 0

    def ordered(a, b):
        return jnp.concatenate([jnp.where(first, a, b), jnp.where(first, b, a)], axis=0)

    return ordered(*outs), ordered(*masses)


def local_scores(refs, cols, t, with_other):
    q, k, v, ko, vo = refs
    width = (t + 1) * 256
    qt = q[t * 256 : width, cols]
    return [nt(qt, k[0:width, cols])] + ([nt(qt, ko[:, cols])] if with_other else [])


def local_weights(near, t, scores):
    extra = [jnp.where(near == i, 1.0, 0.0).astype(F32) for i in range(2)]
    causal = lax.broadcasted_iota(jnp.int32, (BLK, BLK), 0) >= lax.broadcasted_iota(jnp.int32, (BLK, BLK), 1)
    weights, tops = [[] for _ in scores], []
    for i in range(2):
        blocks = []
        for n, sc in enumerate(scores):
            upto = 2 * t + i + 1 if n == 0 else sc.shape[1] // BLK
            mine = [sc[i * BLK : (i + 1) * BLK, j * BLK : (j + 1) * BLK] for j in range(upto)]
            if n == 0:
                mine[-1] = jnp.where(causal, mine[-1], LOW)
            blocks.append(mine)
        top = functools.reduce(jnp.maximum, sum(blocks, []))
        top = jnp.max(top, axis=1, keepdims=True) * SCALE
        raised = top - extra[i]
        for n, mine in enumerate(blocks):
            pieces = [
                jnp.exp2(b * SCALE - (raised if j % 2 == i else top)).astype(BF) for j, b in enumerate(mine)
            ]
            pieces += [jnp.zeros((BLK, BLK), BF)] * (scores[n].shape[1] // BLK - len(pieces))
            weights[n].append(jnp.concatenate(pieces, axis=1))
        tops.append(jnp.broadcast_to(top, (BLK, HD)))
    return [jnp.concatenate(w, axis=0) for w in weights], jnp.concatenate(tops, axis=0)


def local_finish(refs, done, mass, head, cols, t, weights, top):
    q, k, v, ko, vo = refs
    rows = slice(t * 256, t * 256 + 256)
    both = nn(weights[0], with_ones(v[0 : (t + 1) * 256, cols]))
    if len(weights) > 1:
        both = both + nn(weights[1], with_ones(vo[:, cols]))
    done[rows, cols] = (both[:, :HD] / both[:, HD:]).astype(BF)
    lane = lax.broadcasted_iota(jnp.int32, (256, HD), 1)
    stats = mass[rows, :].astype(F32)
    for n, term in enumerate(three(top + jnp.log2(both[:, HD:]))):
        stats = jnp.where(lane == n * HEADS + head, term, stats)
    mass[rows, :] = stats.astype(BF)


def local_kernel(offsets, q, k, v, ko, vo, out, mass, qs, ks, vs, kos, vos, done, sems, out_sems):
    here = Place(offsets)
    refs = (qs, ks, vs, kos, vos)
    mass[...] = jnp.zeros_like(mass)

    def cols_of(g):
        return pl.ds(pl.multiple_of(g * GW, GW), GW)

    def stage(g, with_other):
        pairs = ((q, qs), (k, ks), (v, vs), (ko, kos), (vo, vos))
        return [
            pltpu.make_async_copy(a.at[:, cols_of(g)], b.at[:, cols_of(g)], sems.at[g, i])
            for i, (a, b) in enumerate(pairs[: 5 if with_other else 3])
        ]

    def leave(g):
        return pltpu.make_async_copy(done.at[:, cols_of(g)], out.at[:, cols_of(g)], out_sems.at[g])

    for with_other in (False, True):

        @pl.when(here.core == int(with_other))
        def _():
            for g in range(GROUPS):
                for c in stage(g, with_other):
                    c.start()

            @pl.loop(0, GROUPS)
            def _(g):
                for c in stage(g, with_other):
                    c.wait()
                near = here.near(g)
                items = [(h, t) for h in range(GH) for t in range(2)]

                def cols(n):
                    return pl.ds(pl.multiple_of(g * GW, GW) + items[n][0] * HD, HD)

                scores = local_scores(refs, cols(0), items[0][1], with_other)
                last = None
                for n, (h, t) in enumerate(items):
                    ahead = None
                    if n + 1 < len(items):
                        ahead = local_scores(refs, cols(n + 1), items[n + 1][1], with_other)
                    current = local_weights(near, t, scores)
                    if last is not None:
                        local_finish(refs, done, mass, *last)
                    last = (g * GH + h, cols(n), t, *current)
                    scores = ahead
                local_finish(refs, done, mass, *last)
                leave(g).start()

    for g in range(GROUPS):
        leave(g).wait()


def mix(parts):
    top = functools.reduce(jnp.maximum, [m for _, m in parts])
    up = down = 0.0
    for o, m in parts:
        e = jnp.exp2(m - top)
        up, down = up + e * o, down + e
    return (up / down).astype(BF)


def merge_kernel(offsets, q, mass, near_a, near_b, near_back, far_own, far_oth, before, out, *rest):
    near_o, far_o, near_q, near_in, far_in, q_in, near_out, far_out = rest
    here = Place(offsets)

    def near_rows(g, half):
        return rows_at((here.near(g) + 2 * half) * BLK, BLK)

    def far_rows(g):
        return rows_at(here.far_block(g) * BLK, BLK)

    def near_copy(g, half, back):
        a, b = out.at[near_rows(g, half), group_cols(g)], near_o.at[g, half]
        return pltpu.make_async_copy(b, a, near_out.at[g, half]) if back else pltpu.make_async_copy(a, b, near_in.at[g, half])

    def far_copy(g, back):
        a, b = out.at[far_rows(g), group_cols(g)], far_o.at[g]
        return pltpu.make_async_copy(b, a, far_out.at[g]) if back else pltpu.make_async_copy(a, b, far_in.at[g])

    def q_copy(g, half):
        return pltpu.make_async_copy(q.at[near_rows(g, half), group_cols(g)], near_q.at[g - 2, half], q_in.at[g - 2, half])

    def far_takes(g):
        return here.odd & (here.far_block(g) % 2 == here.near(g))

    pieces = [(g, half) for g in (2, 3, 0, 1) for half in range(2)]
    for g in range(GROUPS):

        @pl.when(here.far_here(g))
        def _():
            far_copy(g, False).start()

    @pl.when(here.odd)
    def _():
        for g, half in pieces:
            near_copy(g, half, False).start()
            if g >= 2:
                q_copy(g, half).start()

    def near_part(g, half, h):
        cols = head_cols((g % 2) * GH + h)
        if g < 2:
            rows = rows_at(half * BLK, BLK)
            stats = spread_lanes(near_back[rows, 2 * GW :], [n * 2 * GH + g * GH + h for n in range(3)])
            return near_back[rows, cols].astype(F32), stats
        return softmax_parts(
            [nt(near_q[g - 2, half, :, head_cols(h)], r[0, :, cols]) for r in (near_a, near_b)],
            [r[1, :, cols] for r in (near_a, near_b)],
        )

    def own_part(source, rows, g, h):
        return (
            source[:, head_cols(h)].astype(F32),
            spread_lanes(mass[rows, :], [n * HEADS + g * GH + h for n in range(3)]),
        )

    @pl.when(here.odd)
    def _():
        for g, half in pieces:
            near_copy(g, half, False).wait()
            if g >= 2:
                q_copy(g, half).wait()
        for g in range(GROUPS):

            @pl.when(here.far_here(g))
            def _():
                far_copy(g, False).wait()

        for g in (2, 3, 0, 1):
            for half in range(2):
                for h in range(GH):
                    source = near_o.at[g, half]
                    parts = [own_part(source, near_rows(g, half), g, h), near_part(g, half, h)]
                    near_o[g, half, :, head_cols(h)] = mix(parts)

    @pl.when(jnp.logical_not(here.odd))
    def _():
        for g in range(GROUPS):

            @pl.when(here.far_here(g))
            def _():
                far_copy(g, False).wait()

    for g in range(GROUPS):
        for near_too in (False, True):

            @pl.when(here.far_here(g) & (far_takes(g) == near_too))
            def _():
                for h in range(GH):
                    parts = [own_part(far_o.at[g], far_rows(g), g, h), far_piece(here, far_own, far_oth, g, h)]
                    if near_too:
                        parts.append(near_part(g, here.far_block(g) // 2, h))
                    mixed = mix(parts)
                    if near_too:
                        near_o[g, here.far_block(g) // 2, :, head_cols(h)] = mixed
                    else:
                        far_o[g, :, head_cols(h)] = mixed
                if not near_too:
                    far_copy(g, True).start()

    @pl.when(here.odd)
    def _():
        for g, half in pieces:
            near_copy(g, half, True).start()
        for g, half in pieces:
            near_copy(g, half, True).wait()

    for g in range(GROUPS):

        @pl.when(here.far_here(g) & jnp.logical_not(far_takes(g)))
        def _():
            far_copy(g, True).wait()


VMEM = pl.BlockSpec(memory_space=pltpu.VMEM)
HBM = pl.BlockSpec(memory_space=pltpu.HBM)


def shape(*dims):
    return jax.ShapeDtypeStruct(dims, BF)


def hbm(array):
    return pltpu.with_memory_space_constraint(array, pltpu.HBM)


def device_part(q, k, v, offsets):
    params = pltpu.CompilerParams(**PARAMS)
    q, k, v, offsets = hbm(q), hbm(k), hbm(v), hbm(offsets)
    near_x, far_send, far_keep = pl.pallas_call(
        pack_first,
        out_shape=[shape(2, NSEL, 2 * GW)] + [shape(GROUPS, 3, HALF, GW)] * 2,
        in_specs=[SMEM] + [HBM] * 3,
        out_specs=[VMEM] * 3,
        scratch_shapes=[pltpu.SemaphoreType.DMA((FIRST_COPIES,))],
        compiler_params=params,
        cost_estimate=cost(),
        name="pack_first",
    )(offsets, q, k, v)

    far_recv = move(far_send, CORE)
    near_r = move(near_x, PAIR)
    ko, vo = hbm(move(k, CORE)), hbm(move(v, CORE))
    far_pack = pl.pallas_call(
        pack_second,
        out_shape=shape(HEADS, 3, HALF, HD),
        in_specs=[SMEM] + [VMEM] * 2,
        out_specs=VMEM,
        compiler_params=params,
        cost_estimate=cost(),
        name="pack_second",
    )(offsets, far_keep, far_recv)
    far_mine = lax.all_to_all(far_pack, ("x", "y"), 0, 0, tiled=True)
    far_other = move(far_mine, CORE)
    local_out, mass = pl.pallas_call(
        local_kernel,
        out_shape=[shape(ROWS, HEADS * HD), shape(ROWS, HD)],
        in_specs=[SMEM] + [HBM] * 5,
        out_specs=[HBM, VMEM],
        scratch_shapes=[pltpu.VMEM((ROWS, HEADS * HD), BF)] * 6
        + [pltpu.SemaphoreType.DMA((GROUPS, 5)), pltpu.SemaphoreType.DMA((GROUPS,))],
        compiler_params=params,
        cost_estimate=pl.CostEstimate(flops=10**10, bytes_accessed=1000, transcendentals=0),
        name="local",
    )(offsets, q, k, v, ko, vo)

    near_r, mass = lax.optimization_barrier((near_r, mass))
    near_ro = move(near_r, CORE)
    near_out = pl.pallas_call(
        near_kernel,
        out_shape=shape(NSEL, 2 * GW + HD),
        in_specs=[SMEM, VMEM] + [HBM] * 4,
        out_specs=VMEM,
        scratch_shapes=[pltpu.VMEM((ROWS, 2 * GW), BF)] * 2 + [pltpu.SemaphoreType.DMA((16,))],
        compiler_params=params,
        cost_estimate=cost(),
        name="near",
    )(offsets, near_r, k, ko, v, vo)
    near_back = move(near_out, TO_ODD)

    far_out = pl.pallas_call(
        far_kernel,
        out_shape=shape(HEADS, HALF + 16, HD),
        in_specs=[SMEM, VMEM, VMEM, ANY, ANY],
        out_specs=VMEM,
        compiler_params=params,
        cost_estimate=cost(),
        name="far",
    )(offsets, far_mine, far_other, near_out, near_ro)
    far_back = lax.all_to_all(far_out, ("x", "y"), 0, 0, tiled=True)
    far_back_other = move(far_back, CORE)

    return pl.pallas_call(
        merge_kernel,
        out_shape=shape(ROWS, HEADS * HD),
        in_specs=[SMEM, HBM] + [VMEM] * 6 + [HBM],
        out_specs=HBM,
        scratch_shapes=[
            pltpu.VMEM((GROUPS, 2, BLK, GW), BF),
            pltpu.VMEM((GROUPS, BLK, GW), BF),
            pltpu.VMEM((2, 2, BLK, GW), BF),
            pltpu.SemaphoreType.DMA((GROUPS, 2)),
            pltpu.SemaphoreType.DMA((GROUPS,)),
            pltpu.SemaphoreType.DMA((2, 2)),
            pltpu.SemaphoreType.DMA((GROUPS, 2)),
            pltpu.SemaphoreType.DMA((GROUPS,)),
        ],
        input_output_aliases={8: 0},
        compiler_params=params,
        cost_estimate=cost(),
        name="merge",
    )(offsets, q, mass, near_r, near_ro, near_back, far_back, far_back_other, local_out)


def solution(mesh):
    cube = Mesh(mesh.devices.reshape(SIZES), AXES)
    rows = P(AXES, None)
    return jax.shard_map(
        device_part, mesh=cube, in_specs=(rows, rows, rows, P()), out_specs=rows, check_vma=False
    )
```

```python
import functools

import jax
import jax.numpy as jnp
import numpy as np
from jax import lax
from jax.experimental import pallas as pl
from jax.experimental.pallas import tpu as pltpu
from jax.sharding import Mesh
from jax.sharding import PartitionSpec as P

HD = 128
BLK = 128
HALF = 64
HEADS = 16
GROUPS = 4
GH = 4
GW = GH * HD
ROWS = 512
NSEL = 256
AXES = ("x", "y", "z", "c")
SIZES = (4, 4, 4, 2)
SCALE = float(HD**-0.5 * np.log2(np.e))
LOW = -1e30
BF, F32 = jnp.bfloat16, jnp.float32


class Place:
    def __init__(self, offsets):
        self.x, self.y, self.z, self.core = (lax.axis_index(a) for a in AXES)
        self.offsets = offsets
        self.odd = self.z % 2 == 1

    def near(self, g):
        return self.offsets[0, g]

    def far_z(self, g):
        return self.offsets[1, g] // 8

    def far_core(self, g):
        return self.offsets[1, g] // 4 % 2

    def far_block(self, g):
        return self.offsets[1, g] % 4

    def far_here(self, g):
        return (self.far_z(g) == self.z) & (self.far_core(g) == self.core)


def route(step):
    pairs = []
    for index in np.ndindex(*SIZES):
        target = step(*index)
        if target is not None:
            pairs.append((int(np.ravel_multi_index(index, SIZES)), int(np.ravel_multi_index(target, SIZES))))
    return pairs


CORE = route(lambda x, y, z, c: (x, y, z, 1 - c))
PAIR = route(lambda x, y, z, c: (x, y, z ^ 1, c))
TO_ODD = route(lambda x, y, z, c: (x, y, z + 1, c) if z % 2 == 0 else None)


def move(array, pairs):
    return lax.ppermute(array, AXES, pairs)


def cost(flops=1000):
    return pl.CostEstimate(flops=flops, bytes_accessed=1000, transcendentals=0)


ANY = pl.BlockSpec(memory_space=pl.ANY)
SMEM = pl.BlockSpec(memory_space=pltpu.SMEM)
PARAMS = dict(vmem_limit_bytes=28 * 1024 * 1024)


def nt(a, b):
    return lax.dot_general(a, b, (((1,), (1,)), ((), ())), preferred_element_type=F32)


def nn(a, b):
    return lax.dot_general(a, b, (((1,), (0,)), ((), ())), preferred_element_type=F32)


def three(x):
    hi = x.astype(BF).astype(F32)
    rest = x - hi
    mid = rest.astype(BF).astype(F32)
    return hi, mid, rest - mid


def rows_at(first, count):
    return pl.ds(pl.multiple_of(first, count), count)


def group_cols(g):
    return pl.ds(g * GW, GW)


def run_copies(copies):
    for c in copies:
        c.start()
    for c in copies:
        c.wait()


def pack_far(offsets, q, k, v, send, keep, sems):
    here = Place(offsets)
    copies = []
    for g in range(GROUPS):
        for t, source in enumerate((q, k, v)):
            first = here.far_block(g) * BLK
            for half, target in ((1 - here.core, send), (here.core, keep)):
                rows = rows_at(first + half * HALF, HALF)
                copies.append(
                    pltpu.make_async_copy(source.at[rows, group_cols(g)], target.at[g, t], sems.at[len(copies)])
                )
    run_copies(copies)


def pack_near(offsets, q, k, v, near_q, near_kv, sems):
    here = Place(offsets)
    for odd in (False, True):

        @pl.when(here.odd == odd)
        def _():
            copies = []
            for g in range(2):
                for half in range(2):
                    rows = rows_at((here.near(g if odd else g + 2) + 2 * half) * BLK, BLK)
                    to = pl.ds(half * BLK, BLK)
                    for t, source in enumerate((q,) if odd else (k, v)):
                        target = near_q if odd else near_kv.at[t]
                        copies.append(
                            pltpu.make_async_copy(
                                source.at[rows, group_cols(g if odd else g + 2)],
                                target.at[to, group_cols(g)],
                                sems.at[len(copies)],
                            )
                        )
            run_copies(copies)


def pack_second(offsets, kept, received, after_near, out):
    here = Place(offsets)
    for g in range(GROUPS):
        mine = here.far_core(g) == here.core
        for source, flag in ((kept, mine), (received, jnp.logical_not(mine))):

            @pl.when(flag)
            def _():
                for t in range(3):
                    for h in range(GH):
                        out[h * GROUPS + g, t] = source[g, t, :, h * HD : (h + 1) * HD]


def with_ones(val):
    return jnp.concatenate([val, jnp.ones((val.shape[0], HD), BF)], axis=1)


def with_ones(val):
    return jnp.concatenate([val, jnp.ones((val.shape[0], HD), BF)], axis=1)


def softmax_parts(parts, values):
    top = functools.reduce(jnp.maximum, [jnp.max(s, axis=1, keepdims=True) for s in parts]) * SCALE
    both = 0.0
    for s, val in zip(parts, values):
        both = both + nn(jnp.exp2(s * SCALE - top).astype(BF), with_ones(val))
    return both[:, :HD] / both[:, HD:], top + jnp.log2(both[:, HD:])


def head_cols(h):
    return slice(h * HD, (h + 1) * HD)


def near_part(heads, q_of, keys_of, vals_of, out):
    lane = lax.broadcasted_iota(jnp.int32, (NSEL, HD), 1)
    stats = jnp.zeros((NSEL, HD), F32)
    for h in range(heads):
        keys = jnp.concatenate(keys_of(h), axis=0)
        vals = jnp.concatenate(vals_of(h), axis=0)
        o, m = softmax_parts([nt(q_of(h), keys)], [vals])
        out[:, head_cols(h)] = o.astype(BF)
        for n, term in enumerate(three(m)):
            stats = jnp.where(lane == n * heads + h, term, stats)
    out[:, heads * HD :] = stats.astype(BF)


def near_even(offsets, qr, k, ko, v, vo, out, keys, vals, sems):
    here = Place(offsets)

    @pl.when(jnp.logical_not(here.odd))
    def _():
        copies = []
        for g in range(2):
            for n, (source, half) in enumerate([(0, 0), (0, 1), (1, 0), (1, 1)]):
                rows = rows_at((here.near(g) + 2 * half) * BLK, BLK)
                for two, target in (((k, ko), keys), ((v, vo), vals)):
                    copies.append(
                        pltpu.make_async_copy(
                            two[source].at[rows, group_cols(g)],
                            target.at[pl.ds(n * BLK, BLK), group_cols(g)],
                            sems.at[len(copies)],
                        )
                    )
        run_copies(copies)
        near_part(
            2 * GH,
            lambda h: qr[:, head_cols(h)],
            lambda h: [keys[:, head_cols(h)]],
            lambda h: [vals[:, head_cols(h)]],
            out,
        )


def near_odd(offsets, q, kv_a, kv_b, out, queries, sems):
    here = Place(offsets)

    @pl.when(here.odd)
    def _():
        copies = []
        for g in range(2):
            for half in range(2):
                rows = rows_at((here.near(2 + g) + 2 * half) * BLK, BLK)
                copies.append(
                    pltpu.make_async_copy(
                        q.at[rows, group_cols(2 + g)],
                        queries.at[pl.ds(half * BLK, BLK), group_cols(g)],
                        sems.at[len(copies)],
                    )
                )
        run_copies(copies)
        near_part(
            2 * GH,
            lambda h: queries[:, head_cols(h)],
            lambda h: [r[0, :, head_cols(h)] for r in (kv_a, kv_b)],
            lambda h: [r[1, :, head_cols(h)] for r in (kv_a, kv_b)],
            out,
        )


def far_kernel(offsets, mine, other, out):
    here = Place(offsets)

    @pl.when(here.far_z(here.y) == here.z)
    def _():
        late = here.core == 1
        for t in range(4):
            upto = 4 * t + 4
            q = mine[4 * t : upto, 0].reshape(256, HD)
            ri = lax.broadcasted_iota(jnp.int32, (256, 256), 0)
            ci = lax.broadcasted_iota(jnp.int32, (256, 256), 1)
            own_ok = (ci // HALF < ri // HALF) | ((ci // HALF == ri // HALF) & (ci <= ri))
            oth_ok = (ci // HALF < ri // HALF) | ((ci // HALF == ri // HALF) & late)
            parts, vals = [], []
            for source, ok in ((mine, own_ok), (other, oth_ok)):
                s = nt(q, source[0:upto, 1].reshape(upto * HALF, HD))
                d = jnp.where(ok, s[:, t * 256 :], LOW)
                parts.append(d if t == 0 else jnp.concatenate([s[:, : t * 256], d], axis=1))
                vals.append(source[0:upto, 2].reshape(upto * HALF, HD))
            o, m = softmax_parts(parts, vals)
            o = o.astype(BF)
            turned = jnp.transpose(m)[0:16]
            row = lax.broadcasted_iota(jnp.int32, (16, 256), 0)
            stats = jnp.zeros((16, 256), F32)
            for n, term in enumerate(three(turned)):
                stats = jnp.where(row == n, term, stats)
            stats = stats.astype(BF)
            for b in range(4):
                out[4 * t + b, 0:HALF] = o[b * HALF : (b + 1) * HALF]
                out[4 * t + b, HALF:] = stats[:, (b // 2) * 128 : (b // 2) * 128 + 128]


def spread_lanes(stats, places):
    line = lax.broadcasted_iota(jnp.int32, (HD, HD), 0)
    hit = functools.reduce(jnp.logical_or, [line == p for p in places])
    return nn(stats, jnp.where(hit, 1.0, 0.0).astype(BF))


def far_piece(here, far_own, far_oth, g, h):
    outs, masses = [], []
    picks = lax.broadcasted_iota(jnp.int32, (16, HD), 0) < 3
    picks = jnp.where(picks, 1.0, 0.0).astype(BF)
    for source in (far_own, far_oth):
        tile = source[h * GROUPS + g]
        outs.append(tile[0:HALF].astype(F32))
        turned = lax.dot_general(
            tile[HALF:], picks, (((0,), (0,)), ((), ())), preferred_element_type=F32
        )
        masses.append(jnp.where(here.y % 2 == 1, turned[HALF:], turned[:HALF]))
    first = here.core == 0

    def ordered(a, b):
        return jnp.concatenate([jnp.where(first, a, b), jnp.where(first, b, a)], axis=0)

    return ordered(*outs), ordered(*masses)


def local_parts(core):
    if core == 0:
        return [[("own", 256, True)], [("own", 512, False), ("oth", 512, True)]]
    return [[("oth", 512, False), ("own", 256, True)], [("oth", 512, True)]]


def local_weights(near, parts, scores):
    extra = [jnp.where(near == i, 1.0, 0.0).astype(F32) for i in range(2)]
    causal = lax.broadcasted_iota(jnp.int32, (BLK, BLK), 0) >= lax.broadcasted_iota(jnp.int32, (BLK, BLK), 1)
    weights, tops = [[] for _ in scores], []
    for i in range(2):
        blocks = []
        for (_, count, diagonal), sc in zip(parts, scores):
            upto = count // BLK - (1 - i if diagonal else 0)
            mine = [sc[i * BLK : (i + 1) * BLK, j * BLK : (j + 1) * BLK] for j in range(upto)]
            if diagonal:
                mine[-1] = jnp.where(causal, mine[-1], LOW)
            blocks.append(mine)
        top = functools.reduce(jnp.maximum, sum(blocks, []))
        top = jnp.max(top, axis=1, keepdims=True) * SCALE
        raised = top - extra[i]
        for n, mine in enumerate(blocks):
            pieces = [
                jnp.exp2(b * SCALE - (raised if j % 2 == i else top)).astype(BF) for j, b in enumerate(mine)
            ]
            pieces += [jnp.zeros((BLK, BLK), BF)] * (parts[n][1] // BLK - len(pieces))
            weights[n].append(jnp.concatenate(pieces, axis=1))
        tops.append(jnp.broadcast_to(top, (BLK, HD)))
    return [jnp.concatenate(w, axis=0) for w in weights], jnp.concatenate(tops, axis=0)


UNROLL = GH


def local_kernel(offsets, q_in, qo_in, k_in, ko_in, v_in, vo_in, after_near, mine, away, q, qo, k, ko, v, vo, sems):
    here = Place(offsets)
    keys, vals = {"own": k, "oth": ko}, {"own": v, "oth": vo}
    for target in (mine, away):
        target[:, HEADS * HD :] = jnp.zeros((NSEL, HD), BF)

    for core in range(2):
        tiles = local_parts(core)
        own = 512 if core == 0 else 256

        def stage(g, own=own):
            cols = pl.ds(pl.multiple_of(g * GW, GW), GW)
            pieces = (
                (q_in, 0, q, 256),
                (k_in, 0, k, own),
                (ko_in, 0, ko, 512),
                (qo_in, 256, qo, 256),
                (v_in, 0, v, own),
                (vo_in, 0, vo, 512),
            )
            return [
                pltpu.make_async_copy(a.at[pl.ds(first, n), cols], b.at[pl.ds(0, n), cols], sems.at[g, i])
                for i, (a, first, b, n) in enumerate(pieces)
            ]

        @pl.when(here.core == core)
        def _():
            for g in range(GROUPS):
                for c in stage(g):
                    c.start()

            @pl.loop(0, HEADS // UNROLL)
            def _(turn):
                for c in stage(turn):
                    c.wait()
                items = [(h, t) for h in range(UNROLL) for t in range(2)]

                def cols(h):
                    return pl.ds(pl.multiple_of(turn * (UNROLL * HD), HD) + h * HD, HD)

                def score(h, t):
                    queries = (qo if t else q)[:, cols(h)]
                    return [nt(queries, keys[w][0:n, cols(h)]) for w, n, _ in tiles[t]]

                def finish(h, t, weights, top):
                    target = (mine, away)[t]
                    both = 0.0
                    for (w, n, _), p in zip(tiles[t], weights):
                        both = both + nn(p, with_ones(vals[w][0:n, cols(h)]))
                    target[:, cols(h)] = (both[:, :HD] / both[:, HD:]).astype(BF)
                    lane = lax.broadcasted_iota(jnp.int32, (256, HD), 1)
                    stats = target[:, HEADS * HD :].astype(F32)
                    for n, term in enumerate(three(top + jnp.log2(both[:, HD:]))):
                        stats = jnp.where(lane == n * HEADS + turn * UNROLL + h, term, stats)
                    target[:, HEADS * HD :] = stats.astype(BF)

                scores = score(*items[0])
                last = None
                for n, (h, t) in enumerate(items):
                    ahead = score(*items[n + 1]) if n + 1 < len(items) else None
                    current = local_weights(here.near((turn * UNROLL + h) // GH), tiles[t], scores)
                    if last is not None:
                        finish(*last)
                    last = (h, t, *current)
                    scores = ahead
                finish(*last)


def mix(parts):
    top = functools.reduce(jnp.maximum, [m for _, m in parts])
    up = down = 0.0
    for o, m in parts:
        e = jnp.exp2(m - top)
        up, down = up + e * o, down + e
    return (up / down).astype(BF)


def merge_kernel(offsets, mine, back, near_a, near_b, far_own, far_oth, out, done, sems):
    here = Place(offsets)
    nears = (near_a, near_b)
    halves = (mine, back)

    def own_part(half, rows, g, h):
        source = halves[half]
        return (
            source[rows, pl.ds(g * GW + h * HD, HD)].astype(F32),
            spread_lanes(source[rows, HEADS * HD :], [n * HEADS + g * GH + h for n in range(3)]),
        )

    def next_part(half, g, h):
        rows = slice(half * BLK, (half + 1) * BLK)
        source, place = nears[g // 2], (g % 2) * GH + h
        return (
            source[rows, head_cols(place)].astype(F32),
            spread_lanes(source[rows, 2 * GW :], [n * 2 * GH + place for n in range(3)]),
        )

    def put(half, rows, g, h, parts):
        start = rows.start + half * NSEL
        done[pl.ds(pl.multiple_of(start, BLK), BLK), pl.ds(g * GW + h * HD, HD)] = mix(parts)

    copies = []
    for g in range(GROUPS):
        for half in range(2):
            done[half * NSEL : (half + 1) * NSEL, group_cols(g)] = halves[half][:, group_cols(g)]

        near_rows = rows_at(here.near(g) * BLK, BLK)
        far_rows = rows_at(here.far_block(g) % 2 * BLK, BLK)
        near_too = here.odd & (here.far_block(g) % 2 == here.near(g))

        @pl.when(here.odd)
        def _():
            for half in range(2):
                for h in range(GH):
                    put(half, near_rows, g, h, [own_part(half, near_rows, g, h), next_part(half, g, h)])

        for half in range(2):
            for both in (False, True):

                @pl.when(here.far_here(g) & (here.far_block(g) // 2 == half) & (near_too == both))
                def _():
                    for h in range(GH):
                        parts = [own_part(half, far_rows, g, h), far_piece(here, far_own, far_oth, g, h)]
                        if both:
                            parts.append(next_part(half, g, h))
                        put(half, far_rows, g, h, parts)

        copies.append(pltpu.make_async_copy(done.at[:, group_cols(g)], out.at[:, group_cols(g)], sems.at[g]))
        copies[-1].start()
    for c in copies:
        c.wait()


VMEM = pl.BlockSpec(memory_space=pltpu.VMEM)
HBM = pl.BlockSpec(memory_space=pltpu.HBM)


def shape(*dims):
    return jax.ShapeDtypeStruct(dims, BF)


def hbm(array):
    return pltpu.with_memory_space_constraint(array, pltpu.HBM)


def device_part(q, k, v, offsets):
    params = pltpu.CompilerParams(**PARAMS)

    def call(kernel, outs, operands, places, sems=None, scratch=(), out_places=VMEM, flops=1000):
        return pl.pallas_call(
            kernel,
            out_shape=outs,
            in_specs=[SMEM] + places,
            out_specs=out_places,
            scratch_shapes=list(scratch) + ([] if sems is None else [pltpu.SemaphoreType.DMA((sems,))]),
            compiler_params=params,
            cost_estimate=cost(flops),
            name=kernel.__name__,
        )(hbm(offsets), *operands)

    qh, kh, vh = hbm(q), hbm(k), hbm(v)
    half_shape = shape(GROUPS, 3, HALF, GW)
    far_send, far_keep = call(
        pack_far, [half_shape] * 2, (qh, kh, vh), [HBM] * 3, sems=6 * GROUPS, out_places=[VMEM] * 2
    )
    far_recv = move(far_send, CORE)
    near_q, near_kv = call(
        pack_near,
        [shape(NSEL, 2 * GW), shape(2, NSEL, 2 * GW)],
        (qh, kh, vh),
        [HBM] * 3,
        sems=8,
        out_places=[VMEM] * 2,
    )
    near_qr, near_kvr = move(near_q, PAIR), move(near_kv, TO_ODD)
    qo, ko, vo = hbm(move(q, CORE)), hbm(move(k, CORE)), hbm(move(v, CORE))
    far_pack = call(pack_second, shape(HEADS, 3, HALF, HD), (far_keep, far_recv, near_q), [VMEM] * 2 + [ANY])
    far_mine = lax.all_to_all(far_pack, ("x", "y"), 0, 0, tiled=True)

    near_out = call(
        near_even,
        shape(NSEL, 2 * GW + HD),
        (near_qr, kh, ko, vh, vo),
        [VMEM] + [HBM] * 4,
        sems=16,
        scratch=[pltpu.VMEM((ROWS, 2 * GW), BF)] * 2,
    )
    near_back = move(near_out, TO_ODD)
    rows = HEADS * HD
    mine, away = call(
        local_kernel,
        [shape(NSEL, rows + HD)] * 2,
        (qh, qo, kh, ko, vh, vo, near_out),
        [HBM] * 6 + [ANY],
        scratch=[pltpu.VMEM((n, rows), BF) for n in (NSEL, NSEL, ROWS, ROWS, ROWS, ROWS)]
        + [pltpu.SemaphoreType.DMA((GROUPS, 6))],
        out_places=[VMEM] * 2,
        flops=10**10,
    )
    back = move(away, CORE)
    far_mine, near_kvr, mine = lax.optimization_barrier((far_mine, near_kvr, mine))
    far_other = move(far_mine, CORE)
    far_out = call(far_kernel, shape(HEADS, HALF + 16, HD), (far_mine, far_other), [VMEM] * 2)
    far_back = lax.all_to_all(far_out, ("x", "y"), 0, 0, tiled=True)
    near_here = call(
        near_odd,
        shape(NSEL, 2 * GW + HD),
        (qh, near_kvr, move(near_kvr, CORE)),
        [HBM] + [VMEM] * 2,
        sems=4,
        scratch=[pltpu.VMEM((NSEL, 2 * GW), BF)],
    )
    far_back, near_back = lax.optimization_barrier((far_back, near_back))
    far_back_other = move(far_back, CORE)

    return call(
        merge_kernel,
        shape(ROWS, HEADS * HD),
        (mine, back, near_back, near_here, far_back, far_back_other),
        [VMEM] * 6,
        sems=GROUPS,
        scratch=[pltpu.VMEM((ROWS, HEADS * HD), BF)],
        out_places=HBM,
    )


def solution(mesh):
    cube = Mesh(mesh.devices.reshape(SIZES), AXES)
    rows = P(AXES, None)
    return jax.shard_map(
        device_part, mesh=cube, in_specs=(rows, rows, rows, P()), out_specs=rows, check_vma=False
    )
```

```python
import functools

import jax
import jax.numpy as jnp
import numpy as np
from jax import lax
from jax.experimental import pallas as pl
from jax.experimental.pallas import tpu as pltpu
from jax.sharding import Mesh
from jax.sharding import PartitionSpec as P

HD = 128
BLK = 128
HALF = 64
HEADS = 16
GROUPS = 4
GH = 4
GW = GH * HD
ROWS = 512
NSEL = 256
AXES = ("x", "y", "z", "c")
SIZES = (4, 4, 4, 2)
SCALE = float(HD**-0.5 * np.log2(np.e))
LOW = -1e30
BF, F32 = jnp.bfloat16, jnp.float32


class Place:
    def __init__(self, offsets):
        self.x, self.y, self.z, self.core = (lax.axis_index(a) for a in AXES)
        self.offsets = offsets
        self.odd = self.z % 2 == 1

    def near(self, g):
        return self.offsets[0, g]

    def far_z(self, g):
        return self.offsets[1, g] // 8

    def far_core(self, g):
        return self.offsets[1, g] // 4 % 2

    def far_block(self, g):
        return self.offsets[1, g] % 4

    def far_here(self, g):
        return (self.far_z(g) == self.z) & (self.far_core(g) == self.core)


def route(step):
    pairs = []
    for index in np.ndindex(*SIZES):
        target = step(*index)
        if target is not None:
            pairs.append((int(np.ravel_multi_index(index, SIZES)), int(np.ravel_multi_index(target, SIZES))))
    return pairs


CORE = route(lambda x, y, z, c: (x, y, z, 1 - c))
PAIR = route(lambda x, y, z, c: (x, y, z ^ 1, c))
TO_ODD = route(lambda x, y, z, c: (x, y, z + 1, c) if z % 2 == 0 else None)


def move(array, pairs):
    return lax.ppermute(array, AXES, pairs)


def cost(flops=1000):
    return pl.CostEstimate(flops=flops, bytes_accessed=1000, transcendentals=0)


ANY = pl.BlockSpec(memory_space=pl.ANY)
SMEM = pl.BlockSpec(memory_space=pltpu.SMEM)
PARAMS = dict(vmem_limit_bytes=28 * 1024 * 1024)


def nt(a, b):
    return lax.dot_general(a, b, (((1,), (1,)), ((), ())), preferred_element_type=F32)


def nn(a, b):
    return lax.dot_general(a, b, (((1,), (0,)), ((), ())), preferred_element_type=F32)


def three(x):
    hi = x.astype(BF).astype(F32)
    rest = x - hi
    mid = rest.astype(BF).astype(F32)
    return hi, mid, rest - mid


def rows_at(first, count):
    return pl.ds(pl.multiple_of(first, count), count)


def group_cols(g):
    return pl.ds(g * GW, GW)


def run_copies(copies):
    for c in copies:
        c.start()
    for c in copies:
        c.wait()


def pack_first(offsets, q, k, v, near, send, keep, sems):
    here = Place(offsets)
    copies = []
    for g in range(GROUPS):
        for t, source in enumerate((q, k, v)):
            first = here.far_block(g) * BLK
            for half, target in ((1 - here.core, send), (here.core, keep)):
                rows = rows_at(first + half * HALF, HALF)
                copies.append(
                    pltpu.make_async_copy(source.at[rows, group_cols(g)], target.at[g, t], sems.at[len(copies)])
                )
    for odd in (False, True):

        @pl.when(here.odd == odd)
        def _():
            nears = []
            for g in range(2):
                for half in range(2):
                    rows = rows_at((here.near(g if odd else g + 2) + 2 * half) * BLK, BLK)
                    to = pl.ds(half * BLK, BLK)
                    for t, source in enumerate((q,) if odd else (k, v)):
                        nears.append(
                            pltpu.make_async_copy(
                                source.at[rows, group_cols(g if odd else g + 2)],
                                near.at[t, to, group_cols(g)],
                                sems.at[len(copies) + len(nears)],
                            )
                        )
            run_copies(copies + nears)


def pack_second(offsets, kept, received, out):
    here = Place(offsets)
    for g in range(GROUPS):
        mine = here.far_core(g) == here.core
        for source, flag in ((kept, mine), (received, jnp.logical_not(mine))):

            @pl.when(flag)
            def _():
                for t in range(3):
                    for h in range(GH):
                        out[h * GROUPS + g, t] = source[g, t, :, h * HD : (h + 1) * HD]


def with_ones(val):
    return jnp.concatenate([val, jnp.ones((val.shape[0], HD), BF)], axis=1)


def with_ones(val):
    return jnp.concatenate([val, jnp.ones((val.shape[0], HD), BF)], axis=1)


def softmax_parts(parts, values):
    top = functools.reduce(jnp.maximum, [jnp.max(s, axis=1, keepdims=True) for s in parts]) * SCALE
    both = 0.0
    for s, val in zip(parts, values):
        both = both + nn(jnp.exp2(s * SCALE - top).astype(BF), with_ones(val))
    return both[:, :HD] / both[:, HD:], top + jnp.log2(both[:, HD:])


def head_cols(h):
    return slice(h * HD, (h + 1) * HD)


def near_part(heads, q_of, keys_of, vals_of, out):
    lane = lax.broadcasted_iota(jnp.int32, (NSEL, HD), 1)
    stats = jnp.zeros((NSEL, HD), F32)
    for h in range(heads):
        keys = jnp.concatenate(keys_of(h), axis=0)
        vals = jnp.concatenate(vals_of(h), axis=0)
        o, m = softmax_parts([nt(q_of(h), keys)], [vals])
        out[:, head_cols(h)] = o.astype(BF)
        for n, term in enumerate(three(m)):
            stats = jnp.where(lane == n * heads + h, term, stats)
    out[:, heads * HD :] = stats.astype(BF)


def near_even(offsets, qr, k, ko, v, vo, out, keys, vals, sems):
    here = Place(offsets)

    @pl.when(jnp.logical_not(here.odd))
    def _():
        copies = []
        for g in range(2):
            for n, (source, half) in enumerate([(0, 0), (0, 1), (1, 0), (1, 1)]):
                rows = rows_at((here.near(g) + 2 * half) * BLK, BLK)
                for two, target in (((k, ko), keys), ((v, vo), vals)):
                    copies.append(
                        pltpu.make_async_copy(
                            two[source].at[rows, group_cols(g)],
                            target.at[pl.ds(n * BLK, BLK), group_cols(g)],
                            sems.at[len(copies)],
                        )
                    )
        run_copies(copies)
        near_part(
            2 * GH,
            lambda h: qr[0, :, head_cols(h)],
            lambda h: [keys[:, head_cols(h)]],
            lambda h: [vals[:, head_cols(h)]],
            out,
        )


def near_odd(offsets, q, kv_a, kv_b, out, queries, sems):
    here = Place(offsets)

    @pl.when(here.odd)
    def _():
        copies = []
        for g in range(2):
            for half in range(2):
                rows = rows_at((here.near(2 + g) + 2 * half) * BLK, BLK)
                copies.append(
                    pltpu.make_async_copy(
                        q.at[rows, group_cols(2 + g)],
                        queries.at[pl.ds(half * BLK, BLK), group_cols(g)],
                        sems.at[len(copies)],
                    )
                )
        run_copies(copies)
        near_part(
            2 * GH,
            lambda h: queries[:, head_cols(h)],
            lambda h: [r[0, :, head_cols(h)] for r in (kv_a, kv_b)],
            lambda h: [r[1, :, head_cols(h)] for r in (kv_a, kv_b)],
            out,
        )


def far_kernel(offsets, mine, other, out):
    here = Place(offsets)

    @pl.when(here.far_z(here.y) == here.z)
    def _():
        late = here.core == 1
        for t in range(4):
            upto = 4 * t + 4
            q = mine[4 * t : upto, 0].reshape(256, HD)
            ri = lax.broadcasted_iota(jnp.int32, (256, 256), 0)
            ci = lax.broadcasted_iota(jnp.int32, (256, 256), 1)
            own_ok = (ci // HALF < ri // HALF) | ((ci // HALF == ri // HALF) & (ci <= ri))
            oth_ok = (ci // HALF < ri // HALF) | ((ci // HALF == ri // HALF) & late)
            parts, vals = [], []
            for source, ok in ((mine, own_ok), (other, oth_ok)):
                s = nt(q, source[0:upto, 1].reshape(upto * HALF, HD))
                d = jnp.where(ok, s[:, t * 256 :], LOW)
                parts.append(d if t == 0 else jnp.concatenate([s[:, : t * 256], d], axis=1))
                vals.append(source[0:upto, 2].reshape(upto * HALF, HD))
            o, m = softmax_parts(parts, vals)
            o = o.astype(BF)
            turned = jnp.transpose(m)[0:16]
            row = lax.broadcasted_iota(jnp.int32, (16, 256), 0)
            stats = jnp.zeros((16, 256), F32)
            for n, term in enumerate(three(turned)):
                stats = jnp.where(row == n, term, stats)
            stats = stats.astype(BF)
            for b in range(4):
                out[4 * t + b, 0:HALF] = o[b * HALF : (b + 1) * HALF]
                out[4 * t + b, HALF:] = stats[:, (b // 2) * 128 : (b // 2) * 128 + 128]


def spread_lanes(stats, places):
    line = lax.broadcasted_iota(jnp.int32, (HD, HD), 0)
    hit = functools.reduce(jnp.logical_or, [line == p for p in places])
    return nn(stats, jnp.where(hit, 1.0, 0.0).astype(BF))


def far_piece(here, far_own, far_oth, g, h):
    outs, masses = [], []
    picks = lax.broadcasted_iota(jnp.int32, (16, HD), 0) < 3
    picks = jnp.where(picks, 1.0, 0.0).astype(BF)
    for source in (far_own, far_oth):
        tile = source[h * GROUPS + g]
        outs.append(tile[0:HALF].astype(F32))
        turned = lax.dot_general(
            tile[HALF:], picks, (((0,), (0,)), ((), ())), preferred_element_type=F32
        )
        masses.append(jnp.where(here.y % 2 == 1, turned[HALF:], turned[:HALF]))
    first = here.core == 0

    def ordered(a, b):
        return jnp.concatenate([jnp.where(first, a, b), jnp.where(first, b, a)], axis=0)

    return ordered(*outs), ordered(*masses)


def local_parts(core):
    if core == 0:
        return [[("own", 256, True)], [("own", 512, False), ("oth", 512, True)]]
    return [[("oth", 512, False), ("own", 256, True)], [("oth", 512, True)]]


def local_weights(near, parts, scores):
    extra = [jnp.where(near == i, 1.0, 0.0).astype(F32) for i in range(2)]
    causal = lax.broadcasted_iota(jnp.int32, (BLK, BLK), 0) >= lax.broadcasted_iota(jnp.int32, (BLK, BLK), 1)
    weights, tops = [[] for _ in scores], []
    for i in range(2):
        blocks = []
        for (_, count, diagonal), sc in zip(parts, scores):
            upto = count // BLK - (1 - i if diagonal else 0)
            mine = [sc[i * BLK : (i + 1) * BLK, j * BLK : (j + 1) * BLK] for j in range(upto)]
            if diagonal:
                mine[-1] = jnp.where(causal, mine[-1], LOW)
            blocks.append(mine)
        top = functools.reduce(jnp.maximum, sum(blocks, []))
        top = jnp.max(top, axis=1, keepdims=True) * SCALE
        raised = top - extra[i]
        for n, mine in enumerate(blocks):
            pieces = [
                jnp.exp2(b * SCALE - (raised if j % 2 == i else top)).astype(BF) for j, b in enumerate(mine)
            ]
            pieces += [jnp.zeros((BLK, BLK), BF)] * (parts[n][1] // BLK - len(pieces))
            weights[n].append(jnp.concatenate(pieces, axis=1))
        tops.append(jnp.broadcast_to(top, (BLK, HD)))
    return [jnp.concatenate(w, axis=0) for w in weights], jnp.concatenate(tops, axis=0)


UNROLL = GH


def local_kernel(offsets, q_in, qo_in, k_in, ko_in, v_in, vo_in, mine, away, q, qo, k, ko, v, vo, sems):
    here = Place(offsets)
    keys, vals = {"own": k, "oth": ko}, {"own": v, "oth": vo}
    for target in (mine, away):
        target[:, HEADS * HD :] = jnp.zeros((NSEL, HD), BF)

    for core in range(2):
        tiles = local_parts(core)
        own = 512 if core == 0 else 256

        def stage(g, own=own):
            cols = pl.ds(pl.multiple_of(g * GW, GW), GW)
            pieces = (
                (q_in, 0, q, 256),
                (k_in, 0, k, own),
                (ko_in, 0, ko, 512),
                (qo_in, 256, qo, 256),
                (v_in, 0, v, own),
                (vo_in, 0, vo, 512),
            )
            return [
                pltpu.make_async_copy(a.at[pl.ds(first, n), cols], b.at[pl.ds(0, n), cols], sems.at[g, i])
                for i, (a, first, b, n) in enumerate(pieces)
            ]

        @pl.when(here.core == core)
        def _():
            for g in range(GROUPS):
                for c in stage(g):
                    c.start()

            @pl.loop(0, HEADS // UNROLL)
            def _(turn):
                for c in stage(turn):
                    c.wait()
                items = [(h, t) for h in range(UNROLL) for t in range(2)]

                def cols(h):
                    return pl.ds(pl.multiple_of(turn * (UNROLL * HD), HD) + h * HD, HD)

                def score(h, t):
                    queries = (qo if t else q)[:, cols(h)]
                    return [nt(queries, keys[w][0:n, cols(h)]) for w, n, _ in tiles[t]]

                def finish(h, t, weights, top):
                    target = (mine, away)[t]
                    both = 0.0
                    for (w, n, _), p in zip(tiles[t], weights):
                        both = both + nn(p, with_ones(vals[w][0:n, cols(h)]))
                    target[:, cols(h)] = (both[:, :HD] / both[:, HD:]).astype(BF)
                    lane = lax.broadcasted_iota(jnp.int32, (256, HD), 1)
                    stats = target[:, HEADS * HD :].astype(F32)
                    for n, term in enumerate(three(top + jnp.log2(both[:, HD:]))):
                        stats = jnp.where(lane == n * HEADS + turn * UNROLL + h, term, stats)
                    target[:, HEADS * HD :] = stats.astype(BF)

                scores = score(*items[0])
                last = None
                for n, (h, t) in enumerate(items):
                    ahead = score(*items[n + 1]) if n + 1 < len(items) else None
                    current = local_weights(here.near((turn * UNROLL + h) // GH), tiles[t], scores)
                    if last is not None:
                        finish(*last)
                    last = (h, t, *current)
                    scores = ahead
                finish(*last)


def mix(parts):
    top = functools.reduce(jnp.maximum, [m for _, m in parts])
    up = down = 0.0
    for o, m in parts:
        e = jnp.exp2(m - top)
        up, down = up + e * o, down + e
    return (up / down).astype(BF)


def merge_kernel(offsets, mine, back, near_a, near_b, far_own, far_oth, out, done, sems):
    here = Place(offsets)
    nears = (near_a, near_b)
    halves = (mine, back)

    def own_part(half, rows, g, h):
        source = halves[half]
        return (
            source[rows, pl.ds(g * GW + h * HD, HD)].astype(F32),
            spread_lanes(source[rows, HEADS * HD :], [n * HEADS + g * GH + h for n in range(3)]),
        )

    def next_part(half, g, h):
        rows = slice(half * BLK, (half + 1) * BLK)
        source, place = nears[g // 2], (g % 2) * GH + h
        return (
            source[rows, head_cols(place)].astype(F32),
            spread_lanes(source[rows, 2 * GW :], [n * 2 * GH + place for n in range(3)]),
        )

    def put(half, rows, g, h, parts):
        start = rows.start + half * NSEL
        done[pl.ds(pl.multiple_of(start, BLK), BLK), pl.ds(g * GW + h * HD, HD)] = mix(parts)

    copies = []
    for g in range(GROUPS):
        for half in range(2):
            done[half * NSEL : (half + 1) * NSEL, group_cols(g)] = halves[half][:, group_cols(g)]

        near_rows = rows_at(here.near(g) * BLK, BLK)
        far_rows = rows_at(here.far_block(g) % 2 * BLK, BLK)
        near_too = here.odd & (here.far_block(g) % 2 == here.near(g))

        @pl.when(here.odd)
        def _():
            for half in range(2):
                for h in range(GH):
                    put(half, near_rows, g, h, [own_part(half, near_rows, g, h), next_part(half, g, h)])

        for half in range(2):
            for both in (False, True):

                @pl.when(here.far_here(g) & (here.far_block(g) // 2 == half) & (near_too == both))
                def _():
                    for h in range(GH):
                        parts = [own_part(half, far_rows, g, h), far_piece(here, far_own, far_oth, g, h)]
                        if both:
                            parts.append(next_part(half, g, h))
                        put(half, far_rows, g, h, parts)

        copies.append(pltpu.make_async_copy(done.at[:, group_cols(g)], out.at[:, group_cols(g)], sems.at[g]))
        copies[-1].start()
    for c in copies:
        c.wait()


VMEM = pl.BlockSpec(memory_space=pltpu.VMEM)
HBM = pl.BlockSpec(memory_space=pltpu.HBM)


def shape(*dims):
    return jax.ShapeDtypeStruct(dims, BF)


def hbm(array):
    return pltpu.with_memory_space_constraint(array, pltpu.HBM)


def device_part(q, k, v, offsets):
    params = pltpu.CompilerParams(**PARAMS)

    def call(kernel, outs, operands, places, sems=None, scratch=(), out_places=VMEM, flops=1000):
        return pl.pallas_call(
            kernel,
            out_shape=outs,
            in_specs=[SMEM] + places,
            out_specs=out_places,
            scratch_shapes=list(scratch) + ([] if sems is None else [pltpu.SemaphoreType.DMA((sems,))]),
            compiler_params=params,
            cost_estimate=cost(flops),
            name=kernel.__name__,
        )(hbm(offsets), *operands)

    qh, kh, vh = hbm(q), hbm(k), hbm(v)
    half_shape = shape(GROUPS, 3, HALF, GW)
    near_x, far_send, far_keep = call(
        pack_first,
        [pltpu.HBM((2, NSEL, 2 * GW), BF), half_shape, half_shape],
        (qh, kh, vh),
        [HBM] * 3,
        sems=6 * GROUPS + 8,
        out_places=[HBM] + [VMEM] * 2,
    )
    far_recv = move(far_send, CORE)
    near_r = move(near_x, PAIR)
    qo, ko, vo = hbm(move(q, CORE)), hbm(move(k, CORE)), hbm(move(v, CORE))
    far_pack = call(pack_second, shape(HEADS, 3, HALF, HD), (far_keep, far_recv), [VMEM] * 2)
    far_mine = lax.all_to_all(far_pack, ("x", "y"), 0, 0, tiled=True)

    rows = HEADS * HD
    mine, away = call(
        local_kernel,
        [shape(NSEL, rows + HD), pltpu.HBM((NSEL, rows + HD), BF)],
        (qh, qo, kh, ko, vh, vo),
        [HBM] * 6,
        scratch=[pltpu.VMEM((n, rows), BF) for n in (NSEL, NSEL, ROWS, ROWS, ROWS, ROWS)]
        + [pltpu.SemaphoreType.DMA((GROUPS, 6))],
        out_places=[VMEM] * 2,
        flops=10**10,
    )
    back = move(away, CORE)
    far_mine, mine = lax.optimization_barrier((far_mine, mine))
    far_other = move(far_mine, CORE)
    far_out = call(far_kernel, shape(HEADS, HALF + 16, HD), (far_mine, far_other), [VMEM] * 2)
    near_r, far_out = lax.optimization_barrier((near_r, far_out))
    near_ro = move(near_r, CORE)
    near_out = call(
        near_even,
        shape(NSEL, 2 * GW + HD),
        (near_r, kh, ko, vh, vo),
        [VMEM] + [HBM] * 4,
        sems=16,
        scratch=[pltpu.VMEM((ROWS, 2 * GW), BF)] * 2,
    )
    near_back = move(near_out, TO_ODD)
    far_out, near_out = lax.optimization_barrier((far_out, near_out))
    far_back = lax.all_to_all(far_out, ("x", "y"), 0, 0, tiled=True)
    near_here = call(
        near_odd,
        shape(NSEL, 2 * GW + HD),
        (qh, near_r, near_ro),
        [HBM] + [VMEM] * 2,
        sems=4,
        scratch=[pltpu.VMEM((NSEL, 2 * GW), BF)],
    )
    far_back, near_back, near_here = lax.optimization_barrier((far_back, near_back, near_here))
    far_back_other = move(far_back, CORE)

    return call(
        merge_kernel,
        shape(ROWS, HEADS * HD),
        (mine, back, near_back, near_here, far_back, far_back_other),
        [VMEM] * 6,
        sems=GROUPS,
        scratch=[pltpu.VMEM((ROWS, HEADS * HD), BF)],
        out_places=HBM,
    )


def solution(mesh):
    cube = Mesh(mesh.devices.reshape(SIZES), AXES)
    rows = P(AXES, None)
    return jax.shard_map(
        device_part, mesh=cube, in_specs=(rows, rows, rows, P()), out_specs=rows, check_vma=False
    )
```

```python
import functools

import jax
import jax.numpy as jnp
import numpy as np
from jax import lax
from jax.experimental import pallas as pl
from jax.experimental.pallas import tpu as pltpu
from jax.sharding import Mesh
from jax.sharding import PartitionSpec as P

HD = 128
BLK = 128
HALF = 64
HEADS = 16
GROUPS = 4
GH = 4
GW = GH * HD
ROWS = 512
NSEL = 256
AXES = ("x", "y", "z", "c")
SIZES = (4, 4, 4, 2)
SCALE = float(HD**-0.5 * np.log2(np.e))
LOW = -1e30
BF, F32 = jnp.bfloat16, jnp.float32


class Place:
    def __init__(self, offsets):
        self.x, self.y, self.z, self.core = (lax.axis_index(a) for a in AXES)
        self.offsets = offsets
        self.odd = self.z % 2 == 1

    def near(self, g):
        return self.offsets[0, g]

    def far_z(self, g):
        return self.offsets[1, g] // 8

    def far_core(self, g):
        return self.offsets[1, g] // 4 % 2

    def far_block(self, g):
        return self.offsets[1, g] % 4

    def far_here(self, g):
        return (self.far_z(g) == self.z) & (self.far_core(g) == self.core)


def route(step):
    pairs = []
    for index in np.ndindex(*SIZES):
        target = step(*index)
        if target is not None:
            pairs.append((int(np.ravel_multi_index(index, SIZES)), int(np.ravel_multi_index(target, SIZES))))
    return pairs


CORE = route(lambda x, y, z, c: (x, y, z, 1 - c))
PAIR = route(lambda x, y, z, c: (x, y, z ^ 1, c))
TO_ODD = route(lambda x, y, z, c: (x, y, z + 1, c) if z % 2 == 0 else None)


def move(array, pairs):
    return lax.ppermute(array, AXES, pairs)


def cost(flops=1000):
    return pl.CostEstimate(flops=flops, bytes_accessed=1000, transcendentals=0)


ANY = pl.BlockSpec(memory_space=pl.ANY)
SMEM = pl.BlockSpec(memory_space=pltpu.SMEM)
PARAMS = dict(vmem_limit_bytes=28 * 1024 * 1024)


def nt(a, b):
    return lax.dot_general(a, b, (((1,), (1,)), ((), ())), preferred_element_type=F32)


def nn(a, b):
    return lax.dot_general(a, b, (((1,), (0,)), ((), ())), preferred_element_type=F32)


def three(x):
    hi = x.astype(BF).astype(F32)
    rest = x - hi
    mid = rest.astype(BF).astype(F32)
    return hi, mid, rest - mid


def rows_at(first, count):
    return pl.ds(pl.multiple_of(first, count), count)


def group_cols(g):
    return pl.ds(g * GW, GW)


def run_copies(copies):
    for c in copies:
        c.start()
    for c in copies:
        c.wait()


def pack_first(offsets, q, k, v, near, send, keep, sems):
    here = Place(offsets)
    copies = []
    for g in range(GROUPS):
        for t, source in enumerate((q, k, v)):
            first = here.far_block(g) * BLK
            for half, target in ((1 - here.core, send), (here.core, keep)):
                rows = rows_at(first + half * HALF, HALF)
                copies.append(
                    pltpu.make_async_copy(source.at[rows, group_cols(g)], target.at[g, t], sems.at[len(copies)])
                )
    for odd in (False, True):

        @pl.when(here.odd == odd)
        def _():
            nears = []
            for g in range(2):
                for half in range(2):
                    rows = rows_at((here.near(g if odd else g + 2) + 2 * half) * BLK, BLK)
                    to = pl.ds(half * BLK, BLK)
                    for t, source in enumerate((q,) if odd else (k, v)):
                        nears.append(
                            pltpu.make_async_copy(
                                source.at[rows, group_cols(g if odd else g + 2)],
                                near.at[t, to, group_cols(g)],
                                sems.at[len(copies) + len(nears)],
                            )
                        )
            run_copies(copies + nears)


def pack_second(offsets, kept, received, out):
    here = Place(offsets)
    for g in range(GROUPS):
        mine = here.far_core(g) == here.core
        for source, flag in ((kept, mine), (received, jnp.logical_not(mine))):

            @pl.when(flag)
            def _():
                for t in range(3):
                    for h in range(GH):
                        out[h * GROUPS + g, t] = source[g, t, :, h * HD : (h + 1) * HD]


def with_ones(val):
    return jnp.concatenate([val, jnp.ones((val.shape[0], HD), BF)], axis=1)


def with_ones(val):
    return jnp.concatenate([val, jnp.ones((val.shape[0], HD), BF)], axis=1)


def softmax_parts(parts, values):
    top = functools.reduce(jnp.maximum, [jnp.max(s, axis=1, keepdims=True) for s in parts]) * SCALE
    both = 0.0
    for s, val in zip(parts, values):
        both = both + nn(jnp.exp2(s * SCALE - top).astype(BF), with_ones(val))
    return both[:, :HD] / both[:, HD:], top + jnp.log2(both[:, HD:])


def head_cols(h):
    return slice(h * HD, (h + 1) * HD)


def near_part(heads, q_of, keys_of, vals_of, out):
    lane = lax.broadcasted_iota(jnp.int32, (NSEL, HD), 1)
    stats = jnp.zeros((NSEL, HD), F32)
    for h in range(heads):
        keys = jnp.concatenate(keys_of(h), axis=0)
        vals = jnp.concatenate(vals_of(h), axis=0)
        o, m = softmax_parts([nt(q_of(h), keys)], [vals])
        out[:, head_cols(h)] = o.astype(BF)
        for n, term in enumerate(three(m)):
            stats = jnp.where(lane == n * heads + h, term, stats)
    out[:, heads * HD :] = stats.astype(BF)


def near_even(offsets, qr, k, ko, v, vo, out, keys, vals, sems):
    here = Place(offsets)

    @pl.when(jnp.logical_not(here.odd))
    def _():
        copies = []
        for g in range(2):
            for n, (source, half) in enumerate([(0, 0), (0, 1), (1, 0), (1, 1)]):
                rows = rows_at((here.near(g) + 2 * half) * BLK, BLK)
                for two, target in (((k, ko), keys), ((v, vo), vals)):
                    copies.append(
                        pltpu.make_async_copy(
                            two[source].at[rows, group_cols(g)],
                            target.at[pl.ds(n * BLK, BLK), group_cols(g)],
                            sems.at[len(copies)],
                        )
                    )
        run_copies(copies)
        near_part(
            2 * GH,
            lambda h: qr[0, :, head_cols(h)],
            lambda h: [keys[:, head_cols(h)]],
            lambda h: [vals[:, head_cols(h)]],
            out,
        )


def near_odd(offsets, q, kv_a, kv_b, out, queries, sems):
    here = Place(offsets)

    @pl.when(here.odd)
    def _():
        copies = []
        for g in range(2):
            for half in range(2):
                rows = rows_at((here.near(2 + g) + 2 * half) * BLK, BLK)
                copies.append(
                    pltpu.make_async_copy(
                        q.at[rows, group_cols(2 + g)],
                        queries.at[pl.ds(half * BLK, BLK), group_cols(g)],
                        sems.at[len(copies)],
                    )
                )
        run_copies(copies)
        near_part(
            2 * GH,
            lambda h: queries[:, head_cols(h)],
            lambda h: [r[0, :, head_cols(h)] for r in (kv_a, kv_b)],
            lambda h: [r[1, :, head_cols(h)] for r in (kv_a, kv_b)],
            out,
        )


def far_kernel(offsets, mine, other, out):
    here = Place(offsets)

    @pl.when(here.far_z(here.y) == here.z)
    def _():
        late = here.core == 1
        for t in range(4):
            upto = 4 * t + 4
            q = mine[4 * t : upto, 0].reshape(256, HD)
            ri = lax.broadcasted_iota(jnp.int32, (256, 256), 0)
            ci = lax.broadcasted_iota(jnp.int32, (256, 256), 1)
            own_ok = (ci // HALF < ri // HALF) | ((ci // HALF == ri // HALF) & (ci <= ri))
            oth_ok = (ci // HALF < ri // HALF) | ((ci // HALF == ri // HALF) & late)
            parts, vals = [], []
            for source, ok in ((mine, own_ok), (other, oth_ok)):
                s = nt(q, source[0:upto, 1].reshape(upto * HALF, HD))
                d = jnp.where(ok, s[:, t * 256 :], LOW)
                parts.append(d if t == 0 else jnp.concatenate([s[:, : t * 256], d], axis=1))
                vals.append(source[0:upto, 2].reshape(upto * HALF, HD))
            o, m = softmax_parts(parts, vals)
            o = o.astype(BF)
            turned = jnp.transpose(m)[0:16]
            row = lax.broadcasted_iota(jnp.int32, (16, 256), 0)
            stats = jnp.zeros((16, 256), F32)
            for n, term in enumerate(three(turned)):
                stats = jnp.where(row == n, term, stats)
            stats = stats.astype(BF)
            for b in range(4):
                out[4 * t + b, 0:HALF] = o[b * HALF : (b + 1) * HALF]
                out[4 * t + b, HALF:] = stats[:, (b // 2) * 128 : (b // 2) * 128 + 128]


def spread_lanes(stats, places):
    line = lax.broadcasted_iota(jnp.int32, (HD, HD), 0)
    hit = functools.reduce(jnp.logical_or, [line == p for p in places])
    return nn(stats, jnp.where(hit, 1.0, 0.0).astype(BF))


def far_piece(here, far_own, far_oth, g, h):
    outs, masses = [], []
    picks = lax.broadcasted_iota(jnp.int32, (16, HD), 0) < 3
    picks = jnp.where(picks, 1.0, 0.0).astype(BF)
    for source in (far_own, far_oth):
        tile = source[h * GROUPS + g]
        outs.append(tile[0:HALF].astype(F32))
        turned = lax.dot_general(
            tile[HALF:], picks, (((0,), (0,)), ((), ())), preferred_element_type=F32
        )
        masses.append(jnp.where(here.y % 2 == 1, turned[HALF:], turned[:HALF]))
    first = here.core == 0

    def ordered(a, b):
        return jnp.concatenate([jnp.where(first, a, b), jnp.where(first, b, a)], axis=0)

    return ordered(*outs), ordered(*masses)


def local_parts(core):
    if core == 0:
        return [[("own", 256, True)], [("own", 512, False), ("oth", 512, True)]]
    return [[("oth", 512, False), ("own", 256, True)], [("oth", 512, True)]]


def local_weights(near, parts, scores):
    extra = [jnp.where(near == i, 1.0, 0.0).astype(F32) for i in range(2)]
    causal = lax.broadcasted_iota(jnp.int32, (BLK, BLK), 0) >= lax.broadcasted_iota(jnp.int32, (BLK, BLK), 1)
    weights, tops = [[] for _ in scores], []
    for i in range(2):
        blocks = []
        for (_, count, diagonal), sc in zip(parts, scores):
            upto = count // BLK - (1 - i if diagonal else 0)
            mine = [sc[i * BLK : (i + 1) * BLK, j * BLK : (j + 1) * BLK] for j in range(upto)]
            if diagonal:
                mine[-1] = jnp.where(causal, mine[-1], LOW)
            blocks.append(mine)
        top = functools.reduce(jnp.maximum, sum(blocks, []))
        top = jnp.max(top, axis=1, keepdims=True) * SCALE
        raised = top - extra[i]
        for n, mine in enumerate(blocks):
            pieces = [
                jnp.exp2(b * SCALE - (raised if j % 2 == i else top)).astype(BF) for j, b in enumerate(mine)
            ]
            pieces += [jnp.zeros((BLK, BLK), BF)] * (parts[n][1] // BLK - len(pieces))
            weights[n].append(jnp.concatenate(pieces, axis=1))
        tops.append(jnp.broadcast_to(top, (BLK, HD)))
    return [jnp.concatenate(w, axis=0) for w in weights], jnp.concatenate(tops, axis=0)


UNROLL = GH


def local_kernel(offsets, q_in, qo_in, k_in, ko_in, v_in, vo_in, mine, away, q, qo, k, ko, v, vo, sems):
    here = Place(offsets)
    keys, vals = {"own": k, "oth": ko}, {"own": v, "oth": vo}
    for target in (mine, away):
        target[:, HEADS * HD :] = jnp.zeros((NSEL, HD), BF)

    for core in range(2):
        tiles = local_parts(core)
        own = 512 if core == 0 else 256

        def stage(g, own=own):
            cols = pl.ds(pl.multiple_of(g * GW, GW), GW)
            pieces = (
                (q_in, 0, q, 256),
                (k_in, 0, k, own),
                (ko_in, 0, ko, 512),
                (qo_in, 256, qo, 256),
                (v_in, 0, v, own),
                (vo_in, 0, vo, 512),
            )
            return [
                pltpu.make_async_copy(a.at[pl.ds(first, n), cols], b.at[pl.ds(0, n), cols], sems.at[g, i])
                for i, (a, first, b, n) in enumerate(pieces)
            ]

        @pl.when(here.core == core)
        def _():
            for g in range(GROUPS):
                for c in stage(g):
                    c.start()

            @pl.loop(0, HEADS // UNROLL)
            def _(turn):
                for c in stage(turn):
                    c.wait()
                items = [(h, t) for h in range(UNROLL) for t in range(2)]

                def cols(h):
                    return pl.ds(pl.multiple_of(turn * (UNROLL * HD), HD) + h * HD, HD)

                def score(h, t):
                    queries = (qo if t else q)[:, cols(h)]
                    return [nt(queries, keys[w][0:n, cols(h)]) for w, n, _ in tiles[t]]

                def finish(h, t, weights, top):
                    target = (mine, away)[t]
                    both = 0.0
                    for (w, n, _), p in zip(tiles[t], weights):
                        both = both + nn(p, with_ones(vals[w][0:n, cols(h)]))
                    target[:, cols(h)] = (both[:, :HD] / both[:, HD:]).astype(BF)
                    lane = lax.broadcasted_iota(jnp.int32, (256, HD), 1)
                    stats = target[:, HEADS * HD :].astype(F32)
                    for n, term in enumerate(three(top + jnp.log2(both[:, HD:]))):
                        stats = jnp.where(lane == n * HEADS + turn * UNROLL + h, term, stats)
                    target[:, HEADS * HD :] = stats.astype(BF)

                scores = score(*items[0])
                last = None
                for n, (h, t) in enumerate(items):
                    ahead = score(*items[n + 1]) if n + 1 < len(items) else None
                    current = local_weights(here.near((turn * UNROLL + h) // GH), tiles[t], scores)
                    if last is not None:
                        finish(*last)
                    last = (h, t, *current)
                    scores = ahead
                finish(*last)


def mix(parts):
    top = functools.reduce(jnp.maximum, [m for _, m in parts])
    up = down = 0.0
    for o, m in parts:
        e = jnp.exp2(m - top)
        up, down = up + e * o, down + e
    return (up / down).astype(BF)


def merge_kernel(offsets, mine, back, near_a, near_b, far_own, far_oth, out, done, sems):
    here = Place(offsets)
    nears = (near_a, near_b)
    halves = (mine, back)

    def own_part(half, rows, g, h):
        source = halves[half]
        return (
            source[rows, pl.ds(g * GW + h * HD, HD)].astype(F32),
            spread_lanes(source[rows, HEADS * HD :], [n * HEADS + g * GH + h for n in range(3)]),
        )

    def next_part(half, g, h):
        rows = slice(half * BLK, (half + 1) * BLK)
        source, place = nears[g // 2], (g % 2) * GH + h
        return (
            source[rows, head_cols(place)].astype(F32),
            spread_lanes(source[rows, 2 * GW :], [n * 2 * GH + place for n in range(3)]),
        )

    def put(half, rows, g, h, parts):
        start = rows.start + half * NSEL
        done[pl.ds(pl.multiple_of(start, BLK), BLK), pl.ds(g * GW + h * HD, HD)] = mix(parts)

    copies = []
    for g in range(GROUPS):
        for half in range(2):
            done[half * NSEL : (half + 1) * NSEL, group_cols(g)] = halves[half][:, group_cols(g)]

        near_rows = rows_at(here.near(g) * BLK, BLK)
        far_rows = rows_at(here.far_block(g) % 2 * BLK, BLK)
        near_too = here.odd & (here.far_block(g) % 2 == here.near(g))

        @pl.when(here.odd)
        def _():
            for half in range(2):
                for h in range(GH):
                    put(half, near_rows, g, h, [own_part(half, near_rows, g, h), next_part(half, g, h)])

        for half in range(2):
            for both in (False, True):

                @pl.when(here.far_here(g) & (here.far_block(g) // 2 == half) & (near_too == both))
                def _():
                    for h in range(GH):
                        parts = [own_part(half, far_rows, g, h), far_piece(here, far_own, far_oth, g, h)]
                        if both:
                            parts.append(next_part(half, g, h))
                        put(half, far_rows, g, h, parts)

        copies.append(pltpu.make_async_copy(done.at[:, group_cols(g)], out.at[:, group_cols(g)], sems.at[g]))
        copies[-1].start()
    for c in copies:
        c.wait()


VMEM = pl.BlockSpec(memory_space=pltpu.VMEM)
HBM = pl.BlockSpec(memory_space=pltpu.HBM)


def shape(*dims):
    return jax.ShapeDtypeStruct(dims, BF)


def hbm(array):
    return pltpu.with_memory_space_constraint(array, pltpu.HBM)


def device_part(q, k, v, offsets):
    params = pltpu.CompilerParams(**PARAMS)

    def call(kernel, outs, operands, places, sems=None, scratch=(), out_places=VMEM, flops=1000):
        return pl.pallas_call(
            kernel,
            out_shape=outs,
            in_specs=[SMEM] + places,
            out_specs=out_places,
            scratch_shapes=list(scratch) + ([] if sems is None else [pltpu.SemaphoreType.DMA((sems,))]),
            compiler_params=params,
            cost_estimate=cost(flops),
            name=kernel.__name__,
        )(hbm(offsets), *operands)

    qh, kh, vh = hbm(q), hbm(k), hbm(v)
    half_shape = shape(GROUPS, 3, HALF, GW)
    near_x, far_send, far_keep = call(
        pack_first,
        [shape(2, NSEL, 2 * GW), half_shape, half_shape],
        (qh, kh, vh),
        [HBM] * 3,
        sems=6 * GROUPS + 8,
        out_places=[VMEM] * 3,
    )
    far_recv = move(far_send, CORE)
    near_r = move(near_x, PAIR)
    qo, ko, vo = hbm(move(q, CORE)), hbm(move(k, CORE)), hbm(move(v, CORE))
    far_pack = call(pack_second, shape(HEADS, 3, HALF, HD), (far_keep, far_recv), [VMEM] * 2)
    far_mine = lax.all_to_all(far_pack, ("x", "y"), 0, 0, tiled=True)

    rows = HEADS * HD
    mine, away = call(
        local_kernel,
        [shape(NSEL, rows + HD), pltpu.HBM((NSEL, rows + HD), BF)],
        (qh, qo, kh, ko, vh, vo),
        [HBM] * 6,
        scratch=[pltpu.VMEM((n, rows), BF) for n in (NSEL, NSEL, ROWS, ROWS, ROWS, ROWS)]
        + [pltpu.SemaphoreType.DMA((GROUPS, 6))],
        out_places=[VMEM] * 2,
        flops=10**10,
    )
    back = move(away, CORE)
    near_r, far_mine, mine = lax.optimization_barrier((near_r, far_mine, mine))
    far_other, near_ro = move(far_mine, CORE), move(near_r, CORE)
    near_out = call(
        near_even,
        shape(NSEL, 2 * GW + HD),
        (near_r, kh, ko, vh, vo),
        [VMEM] + [HBM] * 4,
        sems=16,
        scratch=[pltpu.VMEM((ROWS, 2 * GW), BF)] * 2,
    )
    near_back = move(near_out, TO_ODD)
    far_other, near_out = lax.optimization_barrier((far_other, near_out))
    far_out = call(far_kernel, shape(HEADS, HALF + 16, HD), (far_mine, far_other), [VMEM] * 2)
    far_back = lax.all_to_all(far_out, ("x", "y"), 0, 0, tiled=True)
    near_here = call(
        near_odd,
        shape(NSEL, 2 * GW + HD),
        (qh, near_r, near_ro),
        [HBM] + [VMEM] * 2,
        sems=4,
        scratch=[pltpu.VMEM((NSEL, 2 * GW), BF)],
    )
    far_back, near_back, near_here = lax.optimization_barrier((far_back, near_back, near_here))
    far_back_other = move(far_back, CORE)

    return call(
        merge_kernel,
        shape(ROWS, HEADS * HD),
        (mine, back, near_back, near_here, far_back, far_back_other),
        [VMEM] * 6,
        sems=GROUPS,
        scratch=[pltpu.VMEM((ROWS, HEADS * HD), BF)],
        out_places=HBM,
    )


def solution(mesh):
    cube = Mesh(mesh.devices.reshape(SIZES), AXES)
    rows = P(AXES, None)
    return jax.shard_map(
        device_part, mesh=cube, in_specs=(rows, rows, rows, P()), out_specs=rows, check_vma=False
    )
```

```python
import functools

import jax
import jax.numpy as jnp
import numpy as np
from jax import lax
from jax.experimental import pallas as pl
from jax.experimental.pallas import tpu as pltpu
from jax.sharding import Mesh
from jax.sharding import PartitionSpec as P

HD = 128
BLK = 128
HALF = 64
HEADS = 16
GROUPS = 4
GH = 4
GW = GH * HD
ROWS = 512
NSEL = 256
AXES = ("x", "y", "z", "c")
SIZES = (4, 4, 4, 2)
SCALE = float(HD**-0.5 * np.log2(np.e))
LOW = -1e30
BF, F32 = jnp.bfloat16, jnp.float32


class Place:
    def __init__(self, offsets):
        self.x, self.y, self.z, self.core = (lax.axis_index(a) for a in AXES)
        self.offsets = offsets
        self.odd = self.z % 2 == 1

    def near(self, g):
        return self.offsets[0, g]

    def far_z(self, g):
        return self.offsets[1, g] // 8

    def far_core(self, g):
        return self.offsets[1, g] // 4 % 2

    def far_block(self, g):
        return self.offsets[1, g] % 4

    def far_here(self, g):
        return (self.far_z(g) == self.z) & (self.far_core(g) == self.core)


def route(step):
    pairs = []
    for index in np.ndindex(*SIZES):
        target = step(*index)
        if target is not None:
            pairs.append((int(np.ravel_multi_index(index, SIZES)), int(np.ravel_multi_index(target, SIZES))))
    return pairs


CORE = route(lambda x, y, z, c: (x, y, z, 1 - c))
PAIR = route(lambda x, y, z, c: (x, y, z ^ 1, c))
TO_ODD = route(lambda x, y, z, c: (x, y, z + 1, c) if z % 2 == 0 else None)


def move(array, pairs):
    return lax.ppermute(array, AXES, pairs)


def cost(flops=1000):
    return pl.CostEstimate(flops=flops, bytes_accessed=1000, transcendentals=0)


ANY = pl.BlockSpec(memory_space=pl.ANY)
SMEM = pl.BlockSpec(memory_space=pltpu.SMEM)
PARAMS = dict(vmem_limit_bytes=28 * 1024 * 1024)


def nt(a, b):
    return lax.dot_general(a, b, (((1,), (1,)), ((), ())), preferred_element_type=F32)


def nn(a, b):
    return lax.dot_general(a, b, (((1,), (0,)), ((), ())), preferred_element_type=F32)


def three(x):
    hi = x.astype(BF).astype(F32)
    rest = x - hi
    mid = rest.astype(BF).astype(F32)
    return hi, mid, rest - mid


def in_three(stats, lane, heads):
    hi, mid, low = three(stats)
    return jnp.where(lane < heads, hi, jnp.where(lane < 2 * heads, mid, low)).astype(BF)


def rows_at(first, count):
    return pl.ds(pl.multiple_of(first, count), count)


def group_cols(g):
    return pl.ds(g * GW, GW)


def run_copies(copies):
    for c in copies:
        c.start()
    for c in copies:
        c.wait()


def pack_first(offsets, q, k, v, near, send, keep, sems):
    here = Place(offsets)
    copies = []
    for g in range(GROUPS):
        for t, source in enumerate((q, k, v)):
            first = here.far_block(g) * BLK
            for half, target in ((1 - here.core, send), (here.core, keep)):
                rows = rows_at(first + half * HALF, HALF)
                copies.append(
                    pltpu.make_async_copy(source.at[rows, group_cols(g)], target.at[g, t], sems.at[len(copies)])
                )
    for odd in (False, True):

        @pl.when(here.odd == odd)
        def _():
            nears = []
            for g in range(2):
                for half in range(2):
                    rows = rows_at((here.near(g if odd else g + 2) + 2 * half) * BLK, BLK)
                    to = pl.ds(half * BLK, BLK)
                    for t, source in enumerate((q,) if odd else (k, v)):
                        nears.append(
                            pltpu.make_async_copy(
                                source.at[rows, group_cols(g if odd else g + 2)],
                                near.at[t, to, group_cols(g)],
                                sems.at[len(copies) + len(nears)],
                            )
                        )
            run_copies(copies + nears)


def pack_second(offsets, kept, received, out):
    here = Place(offsets)
    for g in range(GROUPS):
        mine = here.far_core(g) == here.core
        for source, flag in ((kept, mine), (received, jnp.logical_not(mine))):

            @pl.when(flag)
            def _():
                for t in range(3):
                    for h in range(GH):
                        out[h * GROUPS + g, t] = source[g, t, :, h * HD : (h + 1) * HD]


def with_ones(val):
    return jnp.concatenate([val, jnp.ones((val.shape[0], HD), BF)], axis=1)


def with_ones(val):
    return jnp.concatenate([val, jnp.ones((val.shape[0], HD), BF)], axis=1)


def softmax_parts(parts, values):
    top = functools.reduce(jnp.maximum, [jnp.max(s, axis=1, keepdims=True) for s in parts]) * SCALE
    both = 0.0
    for s, val in zip(parts, values):
        both = both + nn(jnp.exp2(s * SCALE - top).astype(BF), with_ones(val))
    return both[:, :HD] / both[:, HD:], top + jnp.log2(both[:, HD:])


def head_cols(h):
    return slice(h * HD, (h + 1) * HD)


def near_part(heads, q_of, keys_of, vals_of, out):
    lane = lax.broadcasted_iota(jnp.int32, (NSEL, HD), 1)
    stats = jnp.zeros((NSEL, HD), F32)
    for h in range(heads):
        keys = jnp.concatenate(keys_of(h), axis=0)
        vals = jnp.concatenate(vals_of(h), axis=0)
        o, m = softmax_parts([nt(q_of(h), keys)], [vals])
        out[:, head_cols(h)] = o.astype(BF)
        stats = jnp.where(lane % heads == h, m, stats)
    out[:, heads * HD :] = in_three(stats, lane, heads)


def near_even(offsets, qr, k, ko, v, vo, out, keys, vals, sems):
    here = Place(offsets)

    @pl.when(jnp.logical_not(here.odd))
    def _():
        copies = []
        for g in range(2):
            for n, (source, half) in enumerate([(0, 0), (0, 1), (1, 0), (1, 1)]):
                rows = rows_at((here.near(g) + 2 * half) * BLK, BLK)
                for two, target in (((k, ko), keys), ((v, vo), vals)):
                    copies.append(
                        pltpu.make_async_copy(
                            two[source].at[rows, group_cols(g)],
                            target.at[pl.ds(n * BLK, BLK), group_cols(g)],
                            sems.at[len(copies)],
                        )
                    )
        run_copies(copies)
        near_part(
            2 * GH,
            lambda h: qr[0, :, head_cols(h)],
            lambda h: [keys[:, head_cols(h)]],
            lambda h: [vals[:, head_cols(h)]],
            out,
        )


def far_kernel(offsets, mine, other, out):
    here = Place(offsets)

    @pl.when(here.far_z(here.y) == here.z)
    def _():
        late = here.core == 1
        for t in range(4):
            upto = 4 * t + 4
            q = mine[4 * t : upto, 0].reshape(256, HD)
            ri = lax.broadcasted_iota(jnp.int32, (256, 256), 0)
            ci = lax.broadcasted_iota(jnp.int32, (256, 256), 1)
            own_ok = (ci // HALF < ri // HALF) | ((ci // HALF == ri // HALF) & (ci <= ri))
            oth_ok = (ci // HALF < ri // HALF) | ((ci // HALF == ri // HALF) & late)
            parts, vals = [], []
            for source, ok in ((mine, own_ok), (other, oth_ok)):
                s = nt(q, source[0:upto, 1].reshape(upto * HALF, HD))
                d = jnp.where(ok, s[:, t * 256 :], LOW)
                parts.append(d if t == 0 else jnp.concatenate([s[:, : t * 256], d], axis=1))
                vals.append(source[0:upto, 2].reshape(upto * HALF, HD))
            o, m = softmax_parts(parts, vals)
            o = o.astype(BF)
            turned = jnp.transpose(m)[0:16]
            row = lax.broadcasted_iota(jnp.int32, (16, 256), 0)
            stats = jnp.zeros((16, 256), F32)
            for n, term in enumerate(three(turned)):
                stats = jnp.where(row == n, term, stats)
            stats = stats.astype(BF)
            for b in range(4):
                out[4 * t + b, 0:HALF] = o[b * HALF : (b + 1) * HALF]
                out[4 * t + b, HALF:] = stats[:, (b // 2) * 128 : (b // 2) * 128 + 128]


def spread_lanes(stats, places):
    line = lax.broadcasted_iota(jnp.int32, (HD, HD), 0)
    hit = functools.reduce(jnp.logical_or, [line == p for p in places])
    return nn(stats, jnp.where(hit, 1.0, 0.0).astype(BF))


def far_piece(here, far_own, far_oth, g, h):
    outs, masses = [], []
    picks = lax.broadcasted_iota(jnp.int32, (16, HD), 0) < 3
    picks = jnp.where(picks, 1.0, 0.0).astype(BF)
    for source in (far_own, far_oth):
        tile = source[h * GROUPS + g]
        outs.append(tile[0:HALF].astype(F32))
        turned = lax.dot_general(
            tile[HALF:], picks, (((0,), (0,)), ((), ())), preferred_element_type=F32
        )
        masses.append(jnp.where(here.y % 2 == 1, turned[HALF:], turned[:HALF]))
    first = here.core == 0

    def ordered(a, b):
        return jnp.concatenate([jnp.where(first, a, b), jnp.where(first, b, a)], axis=0)

    return ordered(*outs), ordered(*masses)


def local_parts(core):
    if core == 0:
        return [[("own", 256, True)], [("own", 512, False), ("oth", 512, True)]]
    return [[("oth", 512, False), ("own", 256, True)], [("oth", 512, True)]]


def local_weights(near, parts, scores):
    extra = [jnp.where(near == i, 1.0, 0.0).astype(F32) for i in range(2)]
    causal = lax.broadcasted_iota(jnp.int32, (BLK, BLK), 0) >= lax.broadcasted_iota(jnp.int32, (BLK, BLK), 1)
    weights, tops = [[] for _ in scores], []
    for i in range(2):
        blocks = []
        for (_, count, diagonal), sc in zip(parts, scores):
            upto = count // BLK - (1 - i if diagonal else 0)
            mine = [sc[i * BLK : (i + 1) * BLK, j * BLK : (j + 1) * BLK] for j in range(upto)]
            if diagonal:
                mine[-1] = jnp.where(causal, mine[-1], LOW)
            blocks.append(mine)
        top = functools.reduce(jnp.maximum, sum(blocks, []))
        top = jnp.max(top, axis=1, keepdims=True) * SCALE
        raised = top - extra[i]
        for n, mine in enumerate(blocks):
            pieces = [
                jnp.exp2(b * SCALE - (raised if j % 2 == i else top)).astype(BF) for j, b in enumerate(mine)
            ]
            pieces += [jnp.zeros((BLK, BLK), BF)] * (parts[n][1] // BLK - len(pieces))
            weights[n].append(jnp.concatenate(pieces, axis=1))
        tops.append(jnp.broadcast_to(top, (BLK, HD)))
    return [jnp.concatenate(w, axis=0) for w in weights], jnp.concatenate(tops, axis=0)


UNROLL = GH


def local_kernel(offsets, q_in, qo_in, k_in, ko_in, v_in, vo_in, mine, away, q, qo, k, ko, v, vo, stats, sems):
    here = Place(offsets)
    keys, vals = {"own": k, "oth": ko}, {"own": v, "oth": vo}
    lane = lax.broadcasted_iota(jnp.int32, (NSEL, HD), 1)
    stats[...] = jnp.zeros_like(stats)

    for core in range(2):
        tiles = local_parts(core)
        own = 512 if core == 0 else 256

        def stage(g, own=own):
            cols = pl.ds(pl.multiple_of(g * GW, GW), GW)
            pieces = (
                (q_in, 0, q, 256),
                (k_in, 0, k, own),
                (ko_in, 0, ko, 512),
                (qo_in, 256, qo, 256),
                (v_in, 0, v, own),
                (vo_in, 0, vo, 512),
            )
            return [
                pltpu.make_async_copy(a.at[pl.ds(first, n), cols], b.at[pl.ds(0, n), cols], sems.at[g, i])
                for i, (a, first, b, n) in enumerate(pieces)
            ]

        @pl.when(here.core == core)
        def _():
            for g in range(GROUPS):
                for c in stage(g):
                    c.start()

            @pl.loop(0, HEADS // UNROLL)
            def _(turn):
                for c in stage(turn):
                    c.wait()
                items = [(h, t) for h in range(UNROLL) for t in range(2)]

                def cols(h):
                    return pl.ds(pl.multiple_of(turn * (UNROLL * HD), HD) + h * HD, HD)

                def score(h, t):
                    queries = (qo if t else q)[:, cols(h)]
                    return [nt(queries, keys[w][0:n, cols(h)]) for w, n, _ in tiles[t]]

                def finish(h, t, weights, top):
                    target = (mine, away)[t]
                    both = 0.0
                    for (w, n, _), p in zip(tiles[t], weights):
                        both = both + nn(p, with_ones(vals[w][0:n, cols(h)]))
                    target[:, cols(h)] = (both[:, :HD] / both[:, HD:]).astype(BF)
                    here_lane = lane % HEADS == turn * UNROLL + h
                    stats[t] = jnp.where(here_lane, top + jnp.log2(both[:, HD:]), stats[t])

                scores = score(*items[0])
                last = None
                for n, (h, t) in enumerate(items):
                    ahead = score(*items[n + 1]) if n + 1 < len(items) else None
                    current = local_weights(here.near((turn * UNROLL + h) // GH), tiles[t], scores)
                    if last is not None:
                        finish(*last)
                    last = (h, t, *current)
                    scores = ahead
                finish(*last)

    for t, target in enumerate((mine, away)):
        target[:, HEADS * HD :] = in_three(stats[t], lane, HEADS)


def mix(parts):
    top = functools.reduce(jnp.maximum, [m for _, m in parts])
    up = down = 0.0
    for o, m in parts:
        e = jnp.exp2(m - top)
        up, down = up + e * o, down + e
    return (up / down).astype(BF)


def own_part(halves, half, rows, g, h):
    source = halves[half]
    return (
        source[rows, pl.ds(g * GW + h * HD, HD)].astype(F32),
        spread_lanes(source[rows, HEADS * HD :], [n * HEADS + g * GH + h for n in range(3)]),
    )


def next_part(nears, half, g, h):
    rows = slice(half * BLK, (half + 1) * BLK)
    source, place = nears[g // 2], (g % 2) * GH + h
    return (
        source[rows, head_cols(place)].astype(F32),
        spread_lanes(source[rows, 2 * GW :], [n * 2 * GH + place for n in range(3)]),
    )


def settle(offsets, q, kv_a, kv_b, mine, back, out, near, queries, done, sems, out_sems):
    here = Place(offsets)
    halves = (mine, back)
    copies = []
    for g in range(2):
        for half in range(2):
            rows = rows_at((here.near(2 + g) + 2 * half) * BLK, BLK)
            copies.append(
                pltpu.make_async_copy(
                    q.at[rows, group_cols(2 + g)],
                    queries.at[pl.ds(half * BLK, BLK), group_cols(g)],
                    sems.at[len(copies)],
                )
            )

    @pl.when(here.odd)
    def _():
        for c in copies:
            c.start()

    for half in range(2):
        done[half * NSEL : (half + 1) * NSEL, :] = halves[half][:, : HEADS * HD]

    def leave(g):
        return pltpu.make_async_copy(done.at[:, group_cols(g)], out.at[:, group_cols(g)], out_sems.at[g])

    leave(0).start()
    leave(1).start()

    @pl.when(here.odd)
    def _():
        for c in copies:
            c.wait()
        near_part(
            2 * GH,
            lambda h: queries[:, head_cols(h)],
            lambda h: [r[0, :, head_cols(h)] for r in (kv_a, kv_b)],
            lambda h: [r[1, :, head_cols(h)] for r in (kv_a, kv_b)],
            near,
        )
        for g in (2, 3):
            rows = rows_at(here.near(g) * BLK, BLK)
            for half in range(2):
                to = rows_at(here.near(g) * BLK + half * NSEL, BLK)
                for h in range(GH):
                    parts = [own_part(halves, half, rows, g, h), next_part((None, near), half, g, h)]
                    done[to, pl.ds(g * GW + h * HD, HD)] = mix(parts)

    leave(2).start()
    leave(3).start()
    for g in range(GROUPS):
        leave(g).wait()


def finish_kernel(offsets, mine, back, near_a, near_b, far_own, far_oth, before, out, near_o, far_o, near_sems, far_sems):
    here = Place(offsets)
    nears, halves = (near_a, near_b), (mine, back)

    def near_copy(g, half):
        rows = rows_at((here.near(g) + 2 * half) * BLK, BLK)
        return pltpu.make_async_copy(near_o.at[g, half], out.at[rows, group_cols(g)], near_sems.at[g, half])

    def far_copy(g):
        rows = rows_at(here.far_block(g) * BLK, BLK)
        return pltpu.make_async_copy(far_o.at[g], out.at[rows, group_cols(g)], far_sems.at[g])

    def near_here(g, half):
        return here.odd & jnp.logical_not(here.far_here(g) & (here.far_block(g) == here.near(g) + 2 * half))

    for g in range(2):
        rows = rows_at(here.near(g) * BLK, BLK)
        for half in range(2):

            @pl.when(near_here(g, half))
            def _():
                for h in range(GH):
                    parts = [own_part(halves, half, rows, g, h), next_part(nears, half, g, h)]
                    near_o[g, half, :, head_cols(h)] = mix(parts)
                near_copy(g, half).start()

    for g in range(GROUPS):
        rows = rows_at(here.far_block(g) % 2 * BLK, BLK)
        near_too = here.odd & (here.far_block(g) % 2 == here.near(g))
        for half in range(2):
            for both in (False, True):

                @pl.when(here.far_here(g) & (here.far_block(g) // 2 == half) & (near_too == both))
                def _():
                    for h in range(GH):
                        parts = [own_part(halves, half, rows, g, h), far_piece(here, far_own, far_oth, g, h)]
                        if both:
                            parts.append(next_part(nears, half, g, h))
                        far_o[g, :, head_cols(h)] = mix(parts)
                    far_copy(g).start()

    for g in range(GROUPS):

        @pl.when(here.far_here(g))
        def _():
            far_copy(g).wait()

    for g in range(2):
        for half in range(2):

            @pl.when(near_here(g, half))
            def _():
                near_copy(g, half).wait()


VMEM = pl.BlockSpec(memory_space=pltpu.VMEM)
HBM = pl.BlockSpec(memory_space=pltpu.HBM)


def shape(*dims):
    return jax.ShapeDtypeStruct(dims, BF)


def hbm(array):
    return pltpu.with_memory_space_constraint(array, pltpu.HBM)


def device_part(q, k, v, offsets):
    params = pltpu.CompilerParams(**PARAMS)

    def call(kernel, outs, operands, places, sems=None, scratch=(), out_places=VMEM, flops=1000, aliases=None):
        return pl.pallas_call(
            kernel,
            out_shape=outs,
            in_specs=[SMEM] + places,
            out_specs=out_places,
            scratch_shapes=list(scratch) + ([] if sems is None else [pltpu.SemaphoreType.DMA((sems,))]),
            input_output_aliases=aliases or {},
            compiler_params=params,
            cost_estimate=cost(flops),
            name=kernel.__name__,
        )(hbm(offsets), *operands)

    qh, kh, vh = hbm(q), hbm(k), hbm(v)
    half_shape = shape(GROUPS, 3, HALF, GW)
    near_x, far_send, far_keep = call(
        pack_first,
        [pltpu.VMEM((2, NSEL, 2 * GW), BF), half_shape, half_shape],
        (qh, kh, vh),
        [HBM] * 3,
        sems=6 * GROUPS + 8,
        out_places=[VMEM] * 3,
    )
    far_recv = move(far_send, CORE)
    near_r = move(near_x, PAIR)
    qo, ko, vo = hbm(move(q, CORE)), hbm(move(k, CORE)), hbm(move(v, CORE))
    far_pack = call(pack_second, shape(HEADS, 3, HALF, HD), (far_keep, far_recv), [VMEM] * 2)
    far_mine = lax.all_to_all(far_pack, ("x", "y"), 0, 0, tiled=True)

    rows = HEADS * HD
    mine, away = call(
        local_kernel,
        [shape(NSEL, rows + HD), pltpu.HBM((NSEL, rows + HD), BF)],
        (qh, qo, kh, ko, vh, vo),
        [HBM] * 6,
        scratch=[pltpu.VMEM((n, rows), BF) for n in (NSEL, NSEL, ROWS, ROWS, ROWS, ROWS)]
        + [pltpu.VMEM((2, NSEL, HD), F32), pltpu.SemaphoreType.DMA((GROUPS, 6))],
        out_places=[VMEM] * 2,
        flops=10**10,
    )
    back = move(away, CORE)
    near_r, far_mine, mine = lax.optimization_barrier((near_r, far_mine, mine))
    far_other, near_ro = move(far_mine, CORE), move(near_r, CORE)
    near_out = call(
        near_even,
        shape(NSEL, 2 * GW + HD),
        (near_r, kh, ko, vh, vo),
        [VMEM] + [HBM] * 4,
        sems=16,
        scratch=[pltpu.VMEM((ROWS, 2 * GW), BF)] * 2,
    )
    near_back = move(near_out, TO_ODD)
    far_other, near_out = lax.optimization_barrier((far_other, near_out))
    far_out = call(far_kernel, pltpu.HBM((HEADS, HALF + 16, HD), BF), (far_mine, far_other), [VMEM] * 2)
    far_back = lax.all_to_all(far_out, ("x", "y"), 0, 0, tiled=True)
    out, near_here = call(
        settle,
        [shape(ROWS, HEADS * HD), pltpu.HBM((NSEL, 2 * GW + HD), BF)],
        (qh, near_r, near_ro, mine, back),
        [HBM] + [VMEM] * 4,
        scratch=[
            pltpu.VMEM((NSEL, 2 * GW), BF),
            pltpu.VMEM((ROWS, HEADS * HD), BF),
            pltpu.SemaphoreType.DMA((4,)),
            pltpu.SemaphoreType.DMA((GROUPS,)),
        ],
        out_places=[HBM, VMEM],
    )
    far_back, near_back, out = lax.optimization_barrier((far_back, near_back, out))
    far_back_other = move(far_back, CORE)
    return call(
        finish_kernel,
        shape(ROWS, HEADS * HD),
        (mine, back, near_back, near_here, far_back, far_back_other, out),
        [VMEM] * 6 + [HBM],
        scratch=[
            pltpu.VMEM((2, 2, BLK, GW), BF),
            pltpu.VMEM((GROUPS, BLK, GW), BF),
            pltpu.SemaphoreType.DMA((2, 2)),
            pltpu.SemaphoreType.DMA((GROUPS,)),
        ],
        out_places=HBM,
        aliases={7: 0},
    )


def solution(mesh):
    cube = Mesh(mesh.devices.reshape(SIZES), AXES)
    rows = P(AXES, None)
    return jax.shard_map(
        device_part, mesh=cube, in_specs=(rows, rows, rows, P()), out_specs=rows, check_vma=False
    )
```

```python
import functools

import jax
import jax.numpy as jnp
import numpy as np
from jax import lax
from jax.experimental import pallas as pl
from jax.experimental.pallas import tpu as pltpu
from jax.sharding import Mesh
from jax.sharding import PartitionSpec as P

HD = 128
BLK = 128
HALF = 64
HEADS = 16
GROUPS = 4
GH = 4
GW = GH * HD
ROWS = 512
NSEL = 256
AXES = ("x", "y", "z", "c")
SIZES = (4, 4, 4, 2)
SCALE = float(HD**-0.5 * np.log2(np.e))
LOW = -1e30
BF, F32 = jnp.bfloat16, jnp.float32


class Place:
    def __init__(self, offsets):
        self.x, self.y, self.z, self.core = (lax.axis_index(a) for a in AXES)
        self.offsets = offsets
        self.odd = self.z % 2 == 1

    def near(self, g):
        return self.offsets[0, g]

    def far_z(self, g):
        return self.offsets[1, g] // 8

    def far_core(self, g):
        return self.offsets[1, g] // 4 % 2

    def far_block(self, g):
        return self.offsets[1, g] % 4

    def far_here(self, g):
        return (self.far_z(g) == self.z) & (self.far_core(g) == self.core)


def route(step):
    pairs = []
    for index in np.ndindex(*SIZES):
        target = step(*index)
        if target is not None:
            pairs.append((int(np.ravel_multi_index(index, SIZES)), int(np.ravel_multi_index(target, SIZES))))
    return pairs


CORE = route(lambda x, y, z, c: (x, y, z, 1 - c))
PAIR = route(lambda x, y, z, c: (x, y, z ^ 1, c))
TO_ODD = route(lambda x, y, z, c: (x, y, z + 1, c) if z % 2 == 0 else None)


def move(array, pairs):
    return lax.ppermute(array, AXES, pairs)


def cost(flops=1000):
    return pl.CostEstimate(flops=flops, bytes_accessed=1000, transcendentals=0)


ANY = pl.BlockSpec(memory_space=pl.ANY)
SMEM = pl.BlockSpec(memory_space=pltpu.SMEM)
PARAMS = dict(vmem_limit_bytes=28 * 1024 * 1024)


def nt(a, b):
    return lax.dot_general(a, b, (((1,), (1,)), ((), ())), preferred_element_type=F32)


def nn(a, b):
    return lax.dot_general(a, b, (((1,), (0,)), ((), ())), preferred_element_type=F32)


def three(x):
    hi = x.astype(BF).astype(F32)
    rest = x - hi
    mid = rest.astype(BF).astype(F32)
    return hi, mid, rest - mid


def in_three(stats, lane, heads):
    hi, mid, low = three(stats)
    return jnp.where(lane < heads, hi, jnp.where(lane < 2 * heads, mid, low)).astype(BF)


def rows_at(first, count):
    return pl.ds(pl.multiple_of(first, count), count)


def group_cols(g):
    return pl.ds(g * GW, GW)


def run_copies(copies):
    for c in copies:
        c.start()
    for c in copies:
        c.wait()


def pack_first(offsets, q, k, v, near, send, keep, sems):
    here = Place(offsets)
    copies = []
    for g in range(GROUPS):
        for t, source in enumerate((q, k, v)):
            first = here.far_block(g) * BLK
            for half, target in ((1 - here.core, send), (here.core, keep)):
                rows = rows_at(first + half * HALF, HALF)
                copies.append(
                    pltpu.make_async_copy(source.at[rows, group_cols(g)], target.at[g, t], sems.at[len(copies)])
                )
    for odd in (False, True):

        @pl.when(here.odd == odd)
        def _():
            nears = []
            for g in range(2):
                for half in range(2):
                    rows = rows_at((here.near(g if odd else g + 2) + 2 * half) * BLK, BLK)
                    to = pl.ds(half * BLK, BLK)
                    for t, source in enumerate((q,) if odd else (k, v)):
                        nears.append(
                            pltpu.make_async_copy(
                                source.at[rows, group_cols(g if odd else g + 2)],
                                near.at[t, to, group_cols(g)],
                                sems.at[len(copies) + len(nears)],
                            )
                        )
            run_copies(copies + nears)


def pack_second(offsets, kept, received, out):
    here = Place(offsets)
    for g in range(GROUPS):
        mine = here.far_core(g) == here.core
        for source, flag in ((kept, mine), (received, jnp.logical_not(mine))):

            @pl.when(flag)
            def _():
                for t in range(3):
                    for h in range(GH):
                        out[h * GROUPS + g, t] = source[g, t, :, h * HD : (h + 1) * HD]


def with_ones(val):
    return jnp.concatenate([val, jnp.ones((val.shape[0], HD), BF)], axis=1)


def with_ones(val):
    return jnp.concatenate([val, jnp.ones((val.shape[0], HD), BF)], axis=1)


def softmax_parts(parts, values):
    top = functools.reduce(jnp.maximum, [jnp.max(s, axis=1, keepdims=True) for s in parts]) * SCALE
    both = 0.0
    for s, val in zip(parts, values):
        both = both + nn(jnp.exp2(s * SCALE - top).astype(BF), with_ones(val))
    return both[:, :HD] / both[:, HD:], top + jnp.log2(both[:, HD:])


def head_cols(h):
    return slice(h * HD, (h + 1) * HD)


def near_part(heads, q_of, keys_of, vals_of, out):
    lane = lax.broadcasted_iota(jnp.int32, (NSEL, HD), 1)
    stats = jnp.zeros((NSEL, HD), F32)
    for h in range(heads):
        keys = jnp.concatenate(keys_of(h), axis=0)
        vals = jnp.concatenate(vals_of(h), axis=0)
        o, m = softmax_parts([nt(q_of(h), keys)], [vals])
        out[:, head_cols(h)] = o.astype(BF)
        stats = jnp.where(lane % heads == h, m, stats)
    out[:, heads * HD :] = in_three(stats, lane, heads)


def near_even(offsets, qr, k, ko, v, vo, out, keys, vals, sems):
    here = Place(offsets)

    @pl.when(jnp.logical_not(here.odd))
    def _():
        copies = []
        for g in range(2):
            for n, (source, half) in enumerate([(0, 0), (0, 1), (1, 0), (1, 1)]):
                rows = rows_at((here.near(g) + 2 * half) * BLK, BLK)
                for two, target in (((k, ko), keys), ((v, vo), vals)):
                    copies.append(
                        pltpu.make_async_copy(
                            two[source].at[rows, group_cols(g)],
                            target.at[pl.ds(n * BLK, BLK), group_cols(g)],
                            sems.at[len(copies)],
                        )
                    )
        run_copies(copies)
        near_part(
            2 * GH,
            lambda h: qr[0, :, head_cols(h)],
            lambda h: [keys[:, head_cols(h)]],
            lambda h: [vals[:, head_cols(h)]],
            out,
        )


def far_kernel(offsets, mine, other, out):
    here = Place(offsets)

    @pl.when(here.far_z(here.y) == here.z)
    def _():
        late = here.core == 1
        for t in range(4):
            upto = 4 * t + 4
            q = mine[4 * t : upto, 0].reshape(256, HD)
            ri = lax.broadcasted_iota(jnp.int32, (256, 256), 0)
            ci = lax.broadcasted_iota(jnp.int32, (256, 256), 1)
            own_ok = (ci // HALF < ri // HALF) | ((ci // HALF == ri // HALF) & (ci <= ri))
            oth_ok = (ci // HALF < ri // HALF) | ((ci // HALF == ri // HALF) & late)
            parts, vals = [], []
            for source, ok in ((mine, own_ok), (other, oth_ok)):
                s = nt(q, source[0:upto, 1].reshape(upto * HALF, HD))
                d = jnp.where(ok, s[:, t * 256 :], LOW)
                parts.append(d if t == 0 else jnp.concatenate([s[:, : t * 256], d], axis=1))
                vals.append(source[0:upto, 2].reshape(upto * HALF, HD))
            o, m = softmax_parts(parts, vals)
            o = o.astype(BF)
            turned = jnp.transpose(m)[0:16]
            row = lax.broadcasted_iota(jnp.int32, (16, 256), 0)
            stats = jnp.zeros((16, 256), F32)
            for n, term in enumerate(three(turned)):
                stats = jnp.where(row == n, term, stats)
            stats = stats.astype(BF)
            for b in range(4):
                out[4 * t + b, 0:HALF] = o[b * HALF : (b + 1) * HALF]
                out[4 * t + b, HALF:] = stats[:, (b // 2) * 128 : (b // 2) * 128 + 128]


def spread_lanes(stats, places):
    line = lax.broadcasted_iota(jnp.int32, (HD, HD), 0)
    hit = functools.reduce(jnp.logical_or, [line == p for p in places])
    return nn(stats, jnp.where(hit, 1.0, 0.0).astype(BF))


def far_piece(here, far_own, far_oth, g, h):
    outs, masses = [], []
    picks = lax.broadcasted_iota(jnp.int32, (16, HD), 0) < 3
    picks = jnp.where(picks, 1.0, 0.0).astype(BF)
    for source in (far_own, far_oth):
        tile = source[h * GROUPS + g]
        outs.append(tile[0:HALF].astype(F32))
        turned = lax.dot_general(
            tile[HALF:], picks, (((0,), (0,)), ((), ())), preferred_element_type=F32
        )
        masses.append(jnp.where(here.y % 2 == 1, turned[HALF:], turned[:HALF]))
    first = here.core == 0

    def ordered(a, b):
        return jnp.concatenate([jnp.where(first, a, b), jnp.where(first, b, a)], axis=0)

    return ordered(*outs), ordered(*masses)


def local_parts(core):
    if core == 0:
        return [[("own", 256, True)], [("own", 512, False), ("oth", 512, True)]]
    return [[("oth", 512, False), ("own", 256, True)], [("oth", 512, True)]]


def local_weights(near, parts, scores):
    extra = [jnp.where(near == i, 1.0, 0.0).astype(F32) for i in range(2)]
    causal = lax.broadcasted_iota(jnp.int32, (BLK, BLK), 0) >= lax.broadcasted_iota(jnp.int32, (BLK, BLK), 1)
    weights, tops = [[] for _ in scores], []
    for i in range(2):
        blocks = []
        for (_, count, diagonal), sc in zip(parts, scores):
            upto = count // BLK - (1 - i if diagonal else 0)
            mine = [sc[i * BLK : (i + 1) * BLK, j * BLK : (j + 1) * BLK] for j in range(upto)]
            if diagonal:
                mine[-1] = jnp.where(causal, mine[-1], LOW)
            blocks.append(mine)
        top = functools.reduce(jnp.maximum, sum(blocks, []))
        top = jnp.max(top, axis=1, keepdims=True) * SCALE
        raised = top - extra[i]
        for n, mine in enumerate(blocks):
            pieces = [
                jnp.exp2(b * SCALE - (raised if j % 2 == i else top)).astype(BF) for j, b in enumerate(mine)
            ]
            pieces += [jnp.zeros((BLK, BLK), BF)] * (parts[n][1] // BLK - len(pieces))
            weights[n].append(jnp.concatenate(pieces, axis=1))
        tops.append(jnp.broadcast_to(top, (BLK, HD)))
    return [jnp.concatenate(w, axis=0) for w in weights], jnp.concatenate(tops, axis=0)


UNROLL = GH


def local_kernel(offsets, q_in, qo_in, k_in, ko_in, v_in, vo_in, mine, away, q, qo, k, ko, v, vo, stats, sems):
    here = Place(offsets)
    keys, vals = {"own": k, "oth": ko}, {"own": v, "oth": vo}
    lane = lax.broadcasted_iota(jnp.int32, (NSEL, HD), 1)
    stats[...] = jnp.zeros_like(stats)

    for core in range(2):
        tiles = local_parts(core)
        own = 512 if core == 0 else 256

        def stage(g, own=own):
            cols = pl.ds(pl.multiple_of(g * GW, GW), GW)
            pieces = (
                (q_in, 0, q, 256),
                (k_in, 0, k, own),
                (ko_in, 0, ko, 512),
                (qo_in, 256, qo, 256),
                (v_in, 0, v, own),
                (vo_in, 0, vo, 512),
            )
            return [
                pltpu.make_async_copy(a.at[pl.ds(first, n), cols], b.at[pl.ds(0, n), cols], sems.at[g, i])
                for i, (a, first, b, n) in enumerate(pieces)
            ]

        @pl.when(here.core == core)
        def _():
            for g in range(GROUPS):
                for c in stage(g):
                    c.start()

            @pl.loop(0, HEADS // UNROLL)
            def _(turn):
                for c in stage(turn):
                    c.wait()
                items = [(h, t) for h in range(UNROLL) for t in range(2)]

                def cols(h):
                    return pl.ds(pl.multiple_of(turn * (UNROLL * HD), HD) + h * HD, HD)

                def score(h, t):
                    queries = (qo if t else q)[:, cols(h)]
                    return [nt(queries, keys[w][0:n, cols(h)]) for w, n, _ in tiles[t]]

                def finish(h, t, weights, top):
                    target = (mine, away)[t]
                    both = 0.0
                    for (w, n, _), p in zip(tiles[t], weights):
                        both = both + nn(p, with_ones(vals[w][0:n, cols(h)]))
                    target[:, cols(h)] = (both[:, :HD] / both[:, HD:]).astype(BF)
                    here_lane = lane % HEADS == turn * UNROLL + h
                    stats[t] = jnp.where(here_lane, top + jnp.log2(both[:, HD:]), stats[t])

                scores = score(*items[0])
                last = None
                for n, (h, t) in enumerate(items):
                    ahead = score(*items[n + 1]) if n + 1 < len(items) else None
                    current = local_weights(here.near((turn * UNROLL + h) // GH), tiles[t], scores)
                    if last is not None:
                        finish(*last)
                    last = (h, t, *current)
                    scores = ahead
                finish(*last)

    for t, target in enumerate((mine, away)):
        target[:, HEADS * HD :] = in_three(stats[t], lane, HEADS)


def mix(parts):
    top = functools.reduce(jnp.maximum, [m for _, m in parts])
    up = down = 0.0
    for o, m in parts:
        e = jnp.exp2(m - top)
        up, down = up + e * o, down + e
    return (up / down).astype(BF)


def own_part(halves, half, rows, g, h):
    source = halves[half]
    return (
        source[rows, pl.ds(g * GW + h * HD, HD)].astype(F32),
        spread_lanes(source[rows, HEADS * HD :], [n * HEADS + g * GH + h for n in range(3)]),
    )


def next_part(nears, half, g, h):
    rows = slice(half * BLK, (half + 1) * BLK)
    source, place = nears[g // 2], (g % 2) * GH + h
    return (
        source[rows, head_cols(place)].astype(F32),
        spread_lanes(source[rows, 2 * GW :], [n * 2 * GH + place for n in range(3)]),
    )


def settle(offsets, q, kv_a, kv_b, mine, back, out, near, queries, done, sems, out_sems):
    here = Place(offsets)
    halves = (mine, back)
    copies = []
    for g in range(2):
        for half in range(2):
            rows = rows_at((here.near(2 + g) + 2 * half) * BLK, BLK)
            copies.append(
                pltpu.make_async_copy(
                    q.at[rows, group_cols(2 + g)],
                    queries.at[pl.ds(half * BLK, BLK), group_cols(g)],
                    sems.at[len(copies)],
                )
            )

    @pl.when(here.odd)
    def _():
        for c in copies:
            c.start()

    for half in range(2):
        done[half * NSEL : (half + 1) * NSEL, :] = halves[half][:, : HEADS * HD]

    def leave(g):
        return pltpu.make_async_copy(done.at[:, group_cols(g)], out.at[:, group_cols(g)], out_sems.at[g])

    leave(0).start()
    leave(1).start()

    @pl.when(here.odd)
    def _():
        for c in copies:
            c.wait()
        near_part(
            2 * GH,
            lambda h: queries[:, head_cols(h)],
            lambda h: [r[0, :, head_cols(h)] for r in (kv_a, kv_b)],
            lambda h: [r[1, :, head_cols(h)] for r in (kv_a, kv_b)],
            near,
        )
        for g in (2, 3):
            rows = rows_at(here.near(g) * BLK, BLK)
            for half in range(2):
                to = rows_at(here.near(g) * BLK + half * NSEL, BLK)
                for h in range(GH):
                    parts = [own_part(halves, half, rows, g, h), next_part((None, near), half, g, h)]
                    done[to, pl.ds(g * GW + h * HD, HD)] = mix(parts)

    leave(2).start()
    leave(3).start()
    for g in range(GROUPS):
        leave(g).wait()


def finish_kernel(
    offsets, mine, back, near_a, far_own, far_oth, near_in, before, out, near_o, far_o, near_b, near_sems, far_sems, sem
):
    here = Place(offsets)
    nears, halves = (near_a, near_b), (mine, back)
    want_near_b = here.odd & (here.far_here(2) | here.far_here(3))
    fetch = pltpu.make_async_copy(near_in, near_b, sem)

    @pl.when(want_near_b)
    def _():
        fetch.start()

    def near_copy(g, half):
        rows = rows_at((here.near(g) + 2 * half) * BLK, BLK)
        return pltpu.make_async_copy(near_o.at[g, half], out.at[rows, group_cols(g)], near_sems.at[g, half])

    def far_copy(g):
        rows = rows_at(here.far_block(g) * BLK, BLK)
        return pltpu.make_async_copy(far_o.at[g], out.at[rows, group_cols(g)], far_sems.at[g])

    def near_here(g, half):
        return here.odd & jnp.logical_not(here.far_here(g) & (here.far_block(g) == here.near(g) + 2 * half))

    for g in range(2):
        rows = rows_at(here.near(g) * BLK, BLK)
        for half in range(2):

            @pl.when(near_here(g, half))
            def _():
                for h in range(GH):
                    parts = [own_part(halves, half, rows, g, h), next_part(nears, half, g, h)]
                    near_o[g, half, :, head_cols(h)] = mix(parts)
                near_copy(g, half).start()

    @pl.when(want_near_b)
    def _():
        fetch.wait()

    for g in range(GROUPS):
        rows = rows_at(here.far_block(g) % 2 * BLK, BLK)
        near_too = here.odd & (here.far_block(g) % 2 == here.near(g))
        for half in range(2):
            for both in (False, True):

                @pl.when(here.far_here(g) & (here.far_block(g) // 2 == half) & (near_too == both))
                def _():
                    for h in range(GH):
                        parts = [own_part(halves, half, rows, g, h), far_piece(here, far_own, far_oth, g, h)]
                        if both:
                            parts.append(next_part(nears, half, g, h))
                        far_o[g, :, head_cols(h)] = mix(parts)
                    far_copy(g).start()

    for g in range(GROUPS):

        @pl.when(here.far_here(g))
        def _():
            far_copy(g).wait()

    for g in range(2):
        for half in range(2):

            @pl.when(near_here(g, half))
            def _():
                near_copy(g, half).wait()


VMEM = pl.BlockSpec(memory_space=pltpu.VMEM)
HBM = pl.BlockSpec(memory_space=pltpu.HBM)


def shape(*dims):
    return jax.ShapeDtypeStruct(dims, BF)


def hbm(array):
    return pltpu.with_memory_space_constraint(array, pltpu.HBM)


def device_part(q, k, v, offsets):
    params = pltpu.CompilerParams(**PARAMS)

    def call(kernel, outs, operands, places, sems=None, scratch=(), out_places=VMEM, flops=1000, aliases=None):
        return pl.pallas_call(
            kernel,
            out_shape=outs,
            in_specs=[SMEM] + places,
            out_specs=out_places,
            scratch_shapes=list(scratch) + ([] if sems is None else [pltpu.SemaphoreType.DMA((sems,))]),
            input_output_aliases=aliases or {},
            compiler_params=params,
            cost_estimate=cost(flops),
            name=kernel.__name__,
        )(hbm(offsets), *operands)

    qh, kh, vh = hbm(q), hbm(k), hbm(v)
    half_shape = shape(GROUPS, 3, HALF, GW)
    near_x, far_send, far_keep = call(
        pack_first,
        [pltpu.VMEM((2, NSEL, 2 * GW), BF), half_shape, half_shape],
        (qh, kh, vh),
        [HBM] * 3,
        sems=6 * GROUPS + 8,
        out_places=[VMEM] * 3,
    )
    far_recv = move(far_send, CORE)
    near_r = move(near_x, PAIR)
    qm, far_recv = lax.optimization_barrier((q, far_recv))
    qo, ko, vo = hbm(move(qm, CORE)), hbm(move(k, CORE)), hbm(move(v, CORE))
    far_pack = call(pack_second, shape(HEADS, 3, HALF, HD), (far_keep, far_recv), [VMEM] * 2)
    far_mine = lax.all_to_all(far_pack, ("x", "y"), 0, 0, tiled=True)

    rows = HEADS * HD
    mine, away = call(
        local_kernel,
        [shape(NSEL, rows + HD), pltpu.HBM((NSEL, rows + HD), BF)],
        (qh, qo, kh, ko, vh, vo),
        [HBM] * 6,
        scratch=[pltpu.VMEM((n, rows), BF) for n in (NSEL, NSEL, ROWS, ROWS, ROWS, ROWS)]
        + [pltpu.VMEM((2, NSEL, HD), F32), pltpu.SemaphoreType.DMA((GROUPS, 6))],
        out_places=[VMEM] * 2,
        flops=10**10,
    )
    back = move(away, CORE)
    far_mine, mine = lax.optimization_barrier((far_mine, mine))
    far_other = move(far_mine, CORE)
    far_out = call(far_kernel, pltpu.HBM((HEADS, HALF + 16, HD), BF), (far_mine, far_other), [VMEM] * 2)
    near_r, far_out = lax.optimization_barrier((near_r, far_out))
    near_ro = move(near_r, CORE)
    near_out = call(
        near_even,
        shape(NSEL, 2 * GW + HD),
        (near_r, kh, ko, vh, vo),
        [VMEM] + [HBM] * 4,
        sems=16,
        scratch=[pltpu.VMEM((ROWS, 2 * GW), BF)] * 2,
    )
    near_back = move(near_out, TO_ODD)
    far_out, near_out = lax.optimization_barrier((far_out, near_out))
    far_back = lax.all_to_all(far_out, ("x", "y"), 0, 0, tiled=True)
    out, near_here = call(
        settle,
        [shape(ROWS, HEADS * HD), pltpu.HBM((NSEL, 2 * GW + HD), BF)],
        (qh, near_r, near_ro, mine, back),
        [HBM] + [VMEM] * 4,
        scratch=[
            pltpu.VMEM((NSEL, 2 * GW), BF),
            pltpu.VMEM((ROWS, HEADS * HD), BF),
            pltpu.SemaphoreType.DMA((4,)),
            pltpu.SemaphoreType.DMA((GROUPS,)),
        ],
        out_places=[HBM, VMEM],
    )
    near_here = hbm(near_here)
    far_back, near_back, out = lax.optimization_barrier((far_back, near_back, out))
    far_back_other = move(far_back, CORE)
    return call(
        finish_kernel,
        shape(ROWS, HEADS * HD),
        (mine, back, near_back, far_back, far_back_other, near_here, out),
        [VMEM] * 5 + [HBM] * 2,
        scratch=[
            pltpu.VMEM((2, 2, BLK, GW), BF),
            pltpu.VMEM((GROUPS, BLK, GW), BF),
            pltpu.VMEM((NSEL, 2 * GW + HD), BF),
            pltpu.SemaphoreType.DMA((2, 2)),
            pltpu.SemaphoreType.DMA((GROUPS,)),
            pltpu.SemaphoreType.DMA,
        ],
        out_places=HBM,
        aliases={7: 0},
    )


def solution(mesh):
    cube = Mesh(mesh.devices.reshape(SIZES), AXES)
    rows = P(AXES, None)
    return jax.shard_map(
        device_part, mesh=cube, in_specs=(rows, rows, rows, P()), out_specs=rows, check_vma=False
    )
```

```python
import functools

import jax
import jax.numpy as jnp
import numpy as np
from jax import lax
from jax.experimental import pallas as pl
from jax.experimental.pallas import tpu as pltpu
from jax.sharding import Mesh
from jax.sharding import PartitionSpec as P

HD = 128
BLK = 128
HALF = 64
HEADS = 16
GROUPS = 4
GH = 4
GW = GH * HD
ROWS = 512
NSEL = 256
ASK = 3
AXES = ("x", "y", "z", "c")
SIZES = (4, 4, 4, 2)
SCALE = float(HD**-0.5 * np.log2(np.e))
LOW = -1e30
BF, F32 = jnp.bfloat16, jnp.float32


class Place:
    def __init__(self, offsets):
        self.x, self.y, self.z, self.core = (lax.axis_index(a) for a in AXES)
        self.offsets = offsets
        self.odd = self.z % 2 == 1

    def near(self, g):
        return self.offsets[0, g]

    def far_z(self, g):
        return self.offsets[1, g] // 8

    def far_core(self, g):
        return self.offsets[1, g] // 4 % 2

    def far_block(self, g):
        return self.offsets[1, g] % 4

    def far_here(self, g):
        return (self.far_z(g) == self.z) & (self.far_core(g) == self.core)


def route(step):
    pairs = []
    for index in np.ndindex(*SIZES):
        target = step(*index)
        if target is not None:
            pairs.append((int(np.ravel_multi_index(index, SIZES)), int(np.ravel_multi_index(target, SIZES))))
    return pairs


CORE = route(lambda x, y, z, c: (x, y, z, 1 - c))
PAIR = route(lambda x, y, z, c: (x, y, z ^ 1, c))
TO_ODD = route(lambda x, y, z, c: (x, y, z + 1, c) if z % 2 == 0 else None)


def move(array, pairs):
    return lax.ppermute(array, AXES, pairs)


def cost(flops=1000):
    return pl.CostEstimate(flops=flops, bytes_accessed=1000, transcendentals=0)


ANY = pl.BlockSpec(memory_space=pl.ANY)
SMEM = pl.BlockSpec(memory_space=pltpu.SMEM)
PARAMS = dict(vmem_limit_bytes=28 * 1024 * 1024)


def nt(a, b):
    return lax.dot_general(a, b, (((1,), (1,)), ((), ())), preferred_element_type=F32)


def nn(a, b):
    return lax.dot_general(a, b, (((1,), (0,)), ((), ())), preferred_element_type=F32)


def three(x):
    hi = x.astype(BF).astype(F32)
    rest = x - hi
    mid = rest.astype(BF).astype(F32)
    return hi, mid, rest - mid


def in_three(stats, lane, heads):
    hi, mid, low = three(stats)
    return jnp.where(lane < heads, hi, jnp.where(lane < 2 * heads, mid, low)).astype(BF)


def rows_at(first, count):
    return pl.ds(pl.multiple_of(first, count), count)


def group_cols(g):
    return pl.ds(g * GW, GW)


def run_copies(copies):
    for c in copies:
        c.start()
    for c in copies:
        c.wait()


def pack_first(offsets, q, k, v, near, send, keep, sems):
    here = Place(offsets)
    copies = []
    for g in range(GROUPS):
        for t, source in enumerate((q, k, v)):
            first = here.far_block(g) * BLK
            for half, target in ((1 - here.core, send), (here.core, keep)):
                rows = rows_at(first + half * HALF, HALF)
                copies.append(
                    pltpu.make_async_copy(source.at[rows, group_cols(g)], target.at[g, t], sems.at[len(copies)])
                )
    for odd in (False, True):

        @pl.when(here.odd == odd)
        def _():
            nears = []
            pieces = [(q, g, g) for g in range(ASK)] if odd else [(k, ASK, 0), (v, ASK, 1)]
            for source, g, place in pieces:
                for half in range(2):
                    rows = rows_at((here.near(g) + 2 * half) * BLK, BLK)
                    nears.append(
                        pltpu.make_async_copy(
                            source.at[rows, group_cols(g)],
                            near.at[pl.ds(half * BLK, BLK), group_cols(place)],
                            sems.at[len(copies) + len(nears)],
                        )
                    )
            run_copies(copies + nears)


def pack_second(offsets, kept, received, out):
    here = Place(offsets)
    for g in range(GROUPS):
        mine = here.far_core(g) == here.core
        for source, flag in ((kept, mine), (received, jnp.logical_not(mine))):

            @pl.when(flag)
            def _():
                for t in range(3):
                    for h in range(GH):
                        out[h * GROUPS + g, t] = source[g, t, :, h * HD : (h + 1) * HD]


def with_ones(val):
    return jnp.concatenate([val, jnp.ones((val.shape[0], HD), BF)], axis=1)


def with_ones(val):
    return jnp.concatenate([val, jnp.ones((val.shape[0], HD), BF)], axis=1)


def softmax_parts(parts, values):
    top = functools.reduce(jnp.maximum, [jnp.max(s, axis=1, keepdims=True) for s in parts]) * SCALE
    both = 0.0
    for s, val in zip(parts, values):
        both = both + nn(jnp.exp2(s * SCALE - top).astype(BF), with_ones(val))
    return both[:, :HD] / both[:, HD:], top + jnp.log2(both[:, HD:])


def head_cols(h):
    return slice(h * HD, (h + 1) * HD)


def near_part(heads, q_of, keys_of, vals_of, out):
    lane = lax.broadcasted_iota(jnp.int32, (NSEL, HD), 1)
    stats = jnp.zeros((NSEL, HD), F32)
    for h in range(heads):
        keys = jnp.concatenate(keys_of(h), axis=0)
        vals = jnp.concatenate(vals_of(h), axis=0)
        o, m = softmax_parts([nt(q_of(h), keys)], [vals])
        out[:, head_cols(h)] = o.astype(BF)
        stats = jnp.where(lane % heads == h, m, stats)
    out[:, heads * HD :] = in_three(stats, lane, heads)


def near_even(offsets, qr, k, ko, v, vo, out, keys, vals, sems):
    here = Place(offsets)

    @pl.when(jnp.logical_not(here.odd))
    def _():
        copies = []
        for g in range(ASK):
            for n, (source, half) in enumerate([(0, 0), (0, 1), (1, 0), (1, 1)]):
                rows = rows_at((here.near(g) + 2 * half) * BLK, BLK)
                for two, target in (((k, ko), keys), ((v, vo), vals)):
                    copies.append(
                        pltpu.make_async_copy(
                            two[source].at[rows, group_cols(g)],
                            target.at[pl.ds(n * BLK, BLK), group_cols(g)],
                            sems.at[len(copies)],
                        )
                    )
        run_copies(copies)
        near_part(
            ASK * GH,
            lambda h: qr[:, head_cols(h)],
            lambda h: [keys[:, head_cols(h)]],
            lambda h: [vals[:, head_cols(h)]],
            out,
        )


def far_kernel(offsets, mine, other, out):
    here = Place(offsets)

    @pl.when(here.far_z(here.y) == here.z)
    def _():
        late = here.core == 1
        for t in range(4):
            upto = 4 * t + 4
            q = mine[4 * t : upto, 0].reshape(256, HD)
            ri = lax.broadcasted_iota(jnp.int32, (256, 256), 0)
            ci = lax.broadcasted_iota(jnp.int32, (256, 256), 1)
            own_ok = (ci // HALF < ri // HALF) | ((ci // HALF == ri // HALF) & (ci <= ri))
            oth_ok = (ci // HALF < ri // HALF) | ((ci // HALF == ri // HALF) & late)
            parts, vals = [], []
            for source, ok in ((mine, own_ok), (other, oth_ok)):
                s = nt(q, source[0:upto, 1].reshape(upto * HALF, HD))
                d = jnp.where(ok, s[:, t * 256 :], LOW)
                parts.append(d if t == 0 else jnp.concatenate([s[:, : t * 256], d], axis=1))
                vals.append(source[0:upto, 2].reshape(upto * HALF, HD))
            o, m = softmax_parts(parts, vals)
            o = o.astype(BF)
            turned = jnp.transpose(m)[0:16]
            row = lax.broadcasted_iota(jnp.int32, (16, 256), 0)
            stats = jnp.zeros((16, 256), F32)
            for n, term in enumerate(three(turned)):
                stats = jnp.where(row == n, term, stats)
            stats = stats.astype(BF)
            for b in range(4):
                out[4 * t + b, 0:HALF] = o[b * HALF : (b + 1) * HALF]
                out[4 * t + b, HALF:] = stats[:, (b // 2) * 128 : (b // 2) * 128 + 128]


def spread_lanes(stats, places):
    line = lax.broadcasted_iota(jnp.int32, (HD, HD), 0)
    hit = functools.reduce(jnp.logical_or, [line == p for p in places])
    return nn(stats, jnp.where(hit, 1.0, 0.0).astype(BF))


def far_piece(here, far_own, far_oth, g, h):
    outs, masses = [], []
    picks = lax.broadcasted_iota(jnp.int32, (16, HD), 0) < 3
    picks = jnp.where(picks, 1.0, 0.0).astype(BF)
    for source in (far_own, far_oth):
        tile = source[h * GROUPS + g]
        outs.append(tile[0:HALF].astype(F32))
        turned = lax.dot_general(
            tile[HALF:], picks, (((0,), (0,)), ((), ())), preferred_element_type=F32
        )
        masses.append(jnp.where(here.y % 2 == 1, turned[HALF:], turned[:HALF]))
    first = here.core == 0

    def ordered(a, b):
        return jnp.concatenate([jnp.where(first, a, b), jnp.where(first, b, a)], axis=0)

    return ordered(*outs), ordered(*masses)


def local_parts(core):
    if core == 0:
        return [[("own", 256, True)], [("own", 512, False), ("oth", 512, True)]]
    return [[("oth", 512, False), ("own", 256, True)], [("oth", 512, True)]]


def local_weights(near, parts, scores):
    extra = [jnp.where(near == i, 1.0, 0.0).astype(F32) for i in range(2)]
    causal = lax.broadcasted_iota(jnp.int32, (BLK, BLK), 0) >= lax.broadcasted_iota(jnp.int32, (BLK, BLK), 1)
    weights, tops = [[] for _ in scores], []
    for i in range(2):
        blocks = []
        for (_, count, diagonal), sc in zip(parts, scores):
            upto = count // BLK - (1 - i if diagonal else 0)
            mine = [sc[i * BLK : (i + 1) * BLK, j * BLK : (j + 1) * BLK] for j in range(upto)]
            if diagonal:
                mine[-1] = jnp.where(causal, mine[-1], LOW)
            blocks.append(mine)
        top = functools.reduce(jnp.maximum, sum(blocks, []))
        top = jnp.max(top, axis=1, keepdims=True) * SCALE
        raised = top - extra[i]
        for n, mine in enumerate(blocks):
            pieces = [
                jnp.exp2(b * SCALE - (raised if j % 2 == i else top)).astype(BF) for j, b in enumerate(mine)
            ]
            pieces += [jnp.zeros((BLK, BLK), BF)] * (parts[n][1] // BLK - len(pieces))
            weights[n].append(jnp.concatenate(pieces, axis=1))
        tops.append(jnp.broadcast_to(top, (BLK, HD)))
    return [jnp.concatenate(w, axis=0) for w in weights], jnp.concatenate(tops, axis=0)


UNROLL = GH


def local_kernel(offsets, q_in, qo_in, k_in, ko_in, v_in, vo_in, mine, away, q, qo, k, ko, v, vo, stats, sems):
    here = Place(offsets)
    keys, vals = {"own": k, "oth": ko}, {"own": v, "oth": vo}
    lane = lax.broadcasted_iota(jnp.int32, (NSEL, HD), 1)
    stats[...] = jnp.zeros_like(stats)

    for core in range(2):
        tiles = local_parts(core)
        own = 512 if core == 0 else 256

        def stage(g, own=own):
            cols = pl.ds(pl.multiple_of(g * GW, GW), GW)
            pieces = (
                (q_in, 0, q, 256),
                (k_in, 0, k, own),
                (ko_in, 0, ko, 512),
                (qo_in, 256, qo, 256),
                (v_in, 0, v, own),
                (vo_in, 0, vo, 512),
            )
            return [
                pltpu.make_async_copy(a.at[pl.ds(first, n), cols], b.at[pl.ds(0, n), cols], sems.at[g, i])
                for i, (a, first, b, n) in enumerate(pieces)
            ]

        @pl.when(here.core == core)
        def _():
            for g in range(GROUPS):
                for c in stage(g):
                    c.start()

            @pl.loop(0, HEADS // UNROLL)
            def _(turn):
                for c in stage(turn):
                    c.wait()
                items = [(h, t) for h in range(UNROLL) for t in range(2)]

                def cols(h):
                    return pl.ds(pl.multiple_of(turn * (UNROLL * HD), HD) + h * HD, HD)

                def score(h, t):
                    queries = (qo if t else q)[:, cols(h)]
                    return [nt(queries, keys[w][0:n, cols(h)]) for w, n, _ in tiles[t]]

                def finish(h, t, weights, top):
                    target = (mine, away)[t]
                    both = 0.0
                    for (w, n, _), p in zip(tiles[t], weights):
                        both = both + nn(p, with_ones(vals[w][0:n, cols(h)]))
                    target[:, cols(h)] = (both[:, :HD] / both[:, HD:]).astype(BF)
                    here_lane = lane % HEADS == turn * UNROLL + h
                    stats[t] = jnp.where(here_lane, top + jnp.log2(both[:, HD:]), stats[t])

                scores = score(*items[0])
                last = None
                for n, (h, t) in enumerate(items):
                    ahead = score(*items[n + 1]) if n + 1 < len(items) else None
                    current = local_weights(here.near((turn * UNROLL + h) // GH), tiles[t], scores)
                    if last is not None:
                        finish(*last)
                    last = (h, t, *current)
                    scores = ahead
                finish(*last)

    for t, target in enumerate((mine, away)):
        target[:, HEADS * HD :] = in_three(stats[t], lane, HEADS)


def mix(parts):
    top = functools.reduce(jnp.maximum, [m for _, m in parts])
    up = down = 0.0
    for o, m in parts:
        e = jnp.exp2(m - top)
        up, down = up + e * o, down + e
    return (up / down).astype(BF)


def own_part(halves, half, rows, g, h):
    source = halves[half]
    return (
        source[rows, pl.ds(g * GW + h * HD, HD)].astype(F32),
        spread_lanes(source[rows, HEADS * HD :], [n * HEADS + g * GH + h for n in range(3)]),
    )


def next_part(nears, half, g, h):
    rows = slice(half * BLK, (half + 1) * BLK)
    source, place, heads = (nears[0], g * GH + h, ASK * GH) if g < ASK else (nears[1], h, GH)
    return (
        source[rows, head_cols(place)].astype(F32),
        spread_lanes(source[rows, heads * HD :], [n * heads + place for n in range(3)]),
    )


def settle(offsets, q, kv_a, kv_b, mine, back, out, near, queries, done, sems, out_sems):
    here = Place(offsets)
    halves = (mine, back)
    copies = []
    for half in range(2):
        rows = rows_at((here.near(ASK) + 2 * half) * BLK, BLK)
        copies.append(
            pltpu.make_async_copy(
                q.at[rows, group_cols(ASK)], queries.at[pl.ds(half * BLK, BLK)], sems.at[len(copies)]
            )
        )

    @pl.when(here.odd)
    def _():
        for c in copies:
            c.start()

    for half in range(2):
        done[half * NSEL : (half + 1) * NSEL, :] = halves[half][:, : HEADS * HD]

    def leave(g):
        return pltpu.make_async_copy(done.at[:, group_cols(g)], out.at[:, group_cols(g)], out_sems.at[g])

    for g in range(ASK):
        leave(g).start()

    @pl.when(here.odd)
    def _():
        for c in copies:
            c.wait()
        near_part(
            GH,
            lambda h: queries[:, head_cols(h)],
            lambda h: [r[:, head_cols(h)] for r in (kv_a, kv_b)],
            lambda h: [r[:, head_cols(GH + h)] for r in (kv_a, kv_b)],
            near,
        )
        rows = rows_at(here.near(ASK) * BLK, BLK)
        for half in range(2):
            to = rows_at(here.near(ASK) * BLK + half * NSEL, BLK)
            for h in range(GH):
                parts = [own_part(halves, half, rows, ASK, h), next_part((None, near), half, ASK, h)]
                done[to, pl.ds(ASK * GW + h * HD, HD)] = mix(parts)

    leave(ASK).start()
    for g in range(GROUPS):
        leave(g).wait()


def finish_kernel(
    offsets, mine, back, near_a, far_own, far_oth, near_in, before, out, near_o, far_o, near_b, near_sems, far_sems, sem
):
    here = Place(offsets)
    nears, halves = (near_a, near_b), (mine, back)
    want_near_b = here.odd & here.far_here(ASK)
    fetch = pltpu.make_async_copy(near_in, near_b, sem)

    @pl.when(want_near_b)
    def _():
        fetch.start()

    def near_copy(g, half):
        rows = rows_at((here.near(g) + 2 * half) * BLK, BLK)
        return pltpu.make_async_copy(near_o.at[g, half], out.at[rows, group_cols(g)], near_sems.at[g, half])

    def far_copy(g):
        rows = rows_at(here.far_block(g) * BLK, BLK)
        return pltpu.make_async_copy(far_o.at[g], out.at[rows, group_cols(g)], far_sems.at[g])

    def near_here(g, half):
        return here.odd & jnp.logical_not(here.far_here(g) & (here.far_block(g) == here.near(g) + 2 * half))

    for g in range(ASK):
        rows = rows_at(here.near(g) * BLK, BLK)
        for half in range(2):

            @pl.when(near_here(g, half))
            def _():
                for h in range(GH):
                    parts = [own_part(halves, half, rows, g, h), next_part(nears, half, g, h)]
                    near_o[g, half, :, head_cols(h)] = mix(parts)
                near_copy(g, half).start()

    @pl.when(want_near_b)
    def _():
        fetch.wait()

    for g in range(GROUPS):
        rows = rows_at(here.far_block(g) % 2 * BLK, BLK)
        near_too = here.odd & (here.far_block(g) % 2 == here.near(g))
        for half in range(2):
            for both in (False, True):

                @pl.when(here.far_here(g) & (here.far_block(g) // 2 == half) & (near_too == both))
                def _():
                    for h in range(GH):
                        parts = [own_part(halves, half, rows, g, h), far_piece(here, far_own, far_oth, g, h)]
                        if both:
                            parts.append(next_part(nears, half, g, h))
                        far_o[g, :, head_cols(h)] = mix(parts)
                    far_copy(g).start()

    for g in range(GROUPS):

        @pl.when(here.far_here(g))
        def _():
            far_copy(g).wait()

    for g in range(ASK):
        for half in range(2):

            @pl.when(near_here(g, half))
            def _():
                near_copy(g, half).wait()


VMEM = pl.BlockSpec(memory_space=pltpu.VMEM)
HBM = pl.BlockSpec(memory_space=pltpu.HBM)


def shape(*dims):
    return jax.ShapeDtypeStruct(dims, BF)


def hbm(array):
    return pltpu.with_memory_space_constraint(array, pltpu.HBM)


def device_part(q, k, v, offsets):
    params = pltpu.CompilerParams(**PARAMS)

    def call(kernel, outs, operands, places, sems=None, scratch=(), out_places=VMEM, flops=1000, aliases=None):
        return pl.pallas_call(
            kernel,
            out_shape=outs,
            in_specs=[SMEM] + places,
            out_specs=out_places,
            scratch_shapes=list(scratch) + ([] if sems is None else [pltpu.SemaphoreType.DMA((sems,))]),
            input_output_aliases=aliases or {},
            compiler_params=params,
            cost_estimate=cost(flops),
            name=kernel.__name__,
        )(hbm(offsets), *operands)

    qh, kh, vh = hbm(q), hbm(k), hbm(v)
    half_shape = shape(GROUPS, 3, HALF, GW)
    near_x, far_send, far_keep = call(
        pack_first,
        [shape(NSEL, ASK * GW), half_shape, half_shape],
        (qh, kh, vh),
        [HBM] * 3,
        sems=6 * GROUPS + 2 * ASK,
        out_places=[VMEM] * 3,
    )
    far_recv = move(far_send, CORE)
    near_r = move(near_x, PAIR)
    qm, far_recv = lax.optimization_barrier((q, far_recv))
    qo, ko, vo = hbm(move(qm, CORE)), hbm(move(k, CORE)), hbm(move(v, CORE))
    far_pack = call(pack_second, shape(HEADS, 3, HALF, HD), (far_keep, far_recv), [VMEM] * 2)
    far_mine = lax.all_to_all(far_pack, ("x", "y"), 0, 0, tiled=True)

    rows = HEADS * HD
    mine, away = call(
        local_kernel,
        [shape(NSEL, rows + HD), pltpu.HBM((NSEL, rows + HD), BF)],
        (qh, qo, kh, ko, vh, vo),
        [HBM] * 6,
        scratch=[pltpu.VMEM((n, rows), BF) for n in (NSEL, NSEL, ROWS, ROWS, ROWS, ROWS)]
        + [pltpu.VMEM((2, NSEL, HD), F32), pltpu.SemaphoreType.DMA((GROUPS, 6))],
        out_places=[VMEM] * 2,
        flops=10**10,
    )
    back = move(away, CORE)
    near_r, far_mine, mine = lax.optimization_barrier((near_r, far_mine, mine))
    far_other, near_ro = move(far_mine, CORE), move(near_r, CORE)
    near_out = call(
        near_even,
        shape(NSEL, ASK * GW + HD),
        (near_r, kh, ko, vh, vo),
        [VMEM] + [HBM] * 4,
        sems=8 * ASK,
        scratch=[pltpu.VMEM((ROWS, ASK * GW), BF)] * 2,
    )
    near_back = move(near_out, TO_ODD)
    far_other, near_out = lax.optimization_barrier((far_other, near_out))
    far_out = call(far_kernel, pltpu.HBM((HEADS, HALF + 16, HD), BF), (far_mine, far_other), [VMEM] * 2)
    far_back = lax.all_to_all(far_out, ("x", "y"), 0, 0, tiled=True)
    out, near_here = call(
        settle,
        [shape(ROWS, HEADS * HD), pltpu.HBM((NSEL, GW + HD), BF)],
        (qh, near_r, near_ro, mine, back),
        [HBM] + [VMEM] * 4,
        scratch=[
            pltpu.VMEM((NSEL, GW), BF),
            pltpu.VMEM((ROWS, HEADS * HD), BF),
            pltpu.SemaphoreType.DMA((2,)),
            pltpu.SemaphoreType.DMA((GROUPS,)),
        ],
        out_places=[HBM, VMEM],
    )
    near_here = hbm(near_here)
    far_back, near_back, out = lax.optimization_barrier((far_back, near_back, out))
    far_back_other = move(far_back, CORE)
    return call(
        finish_kernel,
        shape(ROWS, HEADS * HD),
        (mine, back, near_back, far_back, far_back_other, near_here, out),
        [VMEM] * 5 + [HBM] * 2,
        scratch=[
            pltpu.VMEM((ASK, 2, BLK, GW), BF),
            pltpu.VMEM((GROUPS, BLK, GW), BF),
            pltpu.VMEM((NSEL, GW + HD), BF),
            pltpu.SemaphoreType.DMA((ASK, 2)),
            pltpu.SemaphoreType.DMA((GROUPS,)),
            pltpu.SemaphoreType.DMA,
        ],
        out_places=HBM,
        aliases={7: 0},
    )


def solution(mesh):
    cube = Mesh(mesh.devices.reshape(SIZES), AXES)
    rows = P(AXES, None)
    return jax.shard_map(
        device_part, mesh=cube, in_specs=(rows, rows, rows, P()), out_specs=rows, check_vma=False
    )
```

```python
import functools

import jax
import jax.numpy as jnp
import numpy as np
from jax import lax
from jax.experimental import pallas as pl
from jax.experimental.pallas import tpu as pltpu
from jax.sharding import Mesh
from jax.sharding import PartitionSpec as P

HD = 128
BLK = 128
HALF = 64
HEADS = 16
GROUPS = 4
GH = 4
GW = GH * HD
ROWS = 512
NSEL = 256
ASK = 3
AXES = ("x", "y", "z", "c")
SIZES = (4, 4, 4, 2)
SCALE = float(HD**-0.5 * np.log2(np.e))
LOW = -1e30
BF, F32 = jnp.bfloat16, jnp.float32


class Place:
    def __init__(self, offsets):
        self.x, self.y, self.z, self.core = (lax.axis_index(a) for a in AXES)
        self.offsets = offsets
        self.odd = self.z % 2 == 1

    def near(self, g):
        return self.offsets[0, g]

    def far_z(self, g):
        return self.offsets[1, g] // 8

    def far_core(self, g):
        return self.offsets[1, g] // 4 % 2

    def far_block(self, g):
        return self.offsets[1, g] % 4

    def far_here(self, g):
        return (self.far_z(g) == self.z) & (self.far_core(g) == self.core)


def route(step):
    pairs = []
    for index in np.ndindex(*SIZES):
        target = step(*index)
        if target is not None:
            pairs.append((int(np.ravel_multi_index(index, SIZES)), int(np.ravel_multi_index(target, SIZES))))
    return pairs


CORE = route(lambda x, y, z, c: (x, y, z, 1 - c))
PAIR = route(lambda x, y, z, c: (x, y, z ^ 1, c))
TO_ODD = route(lambda x, y, z, c: (x, y, z + 1, c) if z % 2 == 0 else None)


def move(array, pairs):
    return lax.ppermute(array, AXES, pairs)


def cost(flops=1000):
    return pl.CostEstimate(flops=flops, bytes_accessed=1000, transcendentals=0)


ANY = pl.BlockSpec(memory_space=pl.ANY)
SMEM = pl.BlockSpec(memory_space=pltpu.SMEM)
PARAMS = dict(vmem_limit_bytes=28 * 1024 * 1024)


def nt(a, b):
    return lax.dot_general(a, b, (((1,), (1,)), ((), ())), preferred_element_type=F32)


def nn(a, b):
    return lax.dot_general(a, b, (((1,), (0,)), ((), ())), preferred_element_type=F32)


def three(x):
    hi = x.astype(BF).astype(F32)
    rest = x - hi
    mid = rest.astype(BF).astype(F32)
    return hi, mid, rest - mid


def in_three(stats, lane, heads):
    hi, mid, low = three(stats)
    return jnp.where(lane < heads, hi, jnp.where(lane < 2 * heads, mid, low)).astype(BF)


def rows_at(first, count):
    return pl.ds(pl.multiple_of(first, count), count)


def group_cols(g):
    return pl.ds(g * GW, GW)


def run_copies(copies):
    for c in copies:
        c.start()
    for c in copies:
        c.wait()


def pack_first(offsets, q, k, v, near, send, keep, sems):
    here = Place(offsets)
    copies = []
    for g in range(GROUPS):
        for t, source in enumerate((q, k, v)):
            first = here.far_block(g) * BLK
            for half, target in ((1 - here.core, send), (here.core, keep)):
                rows = rows_at(first + half * HALF, HALF)
                copies.append(
                    pltpu.make_async_copy(source.at[rows, group_cols(g)], target.at[g, t], sems.at[len(copies)])
                )
    for odd in (False, True):

        @pl.when(here.odd == odd)
        def _():
            nears = []
            pieces = [(q, g, g) for g in range(ASK)] if odd else [(k, ASK, 0), (v, ASK, 1)]
            for source, g, place in pieces:
                for half in range(2):
                    rows = rows_at((here.near(g) + 2 * half) * BLK, BLK)
                    nears.append(
                        pltpu.make_async_copy(
                            source.at[rows, group_cols(g)],
                            near.at[pl.ds(half * BLK, BLK), group_cols(place)],
                            sems.at[len(copies) + len(nears)],
                        )
                    )
            run_copies(copies + nears)


def pack_second(offsets, kept, received, out):
    here = Place(offsets)
    for g in range(GROUPS):
        mine = here.far_core(g) == here.core
        for source, flag in ((kept, mine), (received, jnp.logical_not(mine))):

            @pl.when(flag)
            def _():
                for t in range(3):
                    for h in range(GH):
                        out[h * GROUPS + g, t] = source[g, t, :, h * HD : (h + 1) * HD]


def with_ones(val):
    return jnp.concatenate([val, jnp.ones((val.shape[0], HD), BF)], axis=1)


def with_ones(val):
    return jnp.concatenate([val, jnp.ones((val.shape[0], HD), BF)], axis=1)


def softmax_parts(parts, values):
    top = functools.reduce(jnp.maximum, [jnp.max(s, axis=1, keepdims=True) for s in parts]) * SCALE
    both = 0.0
    for s, val in zip(parts, values):
        both = both + nn(jnp.exp2(s * SCALE - top).astype(BF), with_ones(val))
    return both[:, :HD] / both[:, HD:], top + jnp.log2(both[:, HD:])


def head_cols(h):
    return slice(h * HD, (h + 1) * HD)


def near_part(heads, q_of, keys_of, vals_of, out, ready=lambda h: None):
    lane = lax.broadcasted_iota(jnp.int32, (NSEL, HD), 1)

    def score(h):
        ready(h)
        return [nt(q_of(h), keys) for keys in keys_of(h)]

    def finish(h, weights, top, stats):
        both = sum(nn(p, with_ones(vals)) for p, vals in zip(weights, vals_of(h)))
        out[:, head_cols(h)] = (both[:, :HD] / both[:, HD:]).astype(BF)
        return jnp.where(lane % heads == h, top + jnp.log2(both[:, HD:]), stats)

    stats, last, scores = jnp.zeros((NSEL, HD), F32), None, score(0)
    for h in range(heads):
        ahead = score(h + 1) if h + 1 < heads else None
        top = functools.reduce(jnp.maximum, [jnp.max(s, axis=1, keepdims=True) for s in scores]) * SCALE
        weights = [jnp.exp2(s * SCALE - top).astype(BF) for s in scores]
        if last is not None:
            stats = finish(*last, stats)
        last, scores = (h, weights, top), ahead
    stats = finish(*last, stats)
    out[:, heads * HD :] = in_three(stats, lane, heads)


def near_even(offsets, qr, k, ko, v, vo, out, keys, vals, sems):
    here = Place(offsets)

    @pl.when(jnp.logical_not(here.odd))
    def _():
        copies = []
        for g in range(ASK):
            for n, (source, half) in enumerate([(0, 0), (0, 1), (1, 0), (1, 1)]):
                rows = rows_at((here.near(g) + 2 * half) * BLK, BLK)
                for two, target in (((k, ko), keys), ((v, vo), vals)):
                    copies.append(
                        pltpu.make_async_copy(
                            two[source].at[rows, group_cols(g)],
                            target.at[pl.ds(n * BLK, BLK), group_cols(g)],
                            sems.at[len(copies)],
                        )
                    )
        for c in copies:
            c.start()

        def ready(h):
            if h % GH == 0:
                for c in copies[8 * (h // GH) : 8 * (h // GH) + 8]:
                    c.wait()

        near_part(
            ASK * GH,
            lambda h: qr[:, head_cols(h)],
            lambda h: [keys[:, head_cols(h)]],
            lambda h: [vals[:, head_cols(h)]],
            out,
            ready,
        )


def far_kernel(offsets, mine, other, out):
    here = Place(offsets)

    @pl.when(here.far_z(here.y) == here.z)
    def _():
        late = here.core == 1
        for t in range(4):
            upto = 4 * t + 4
            q = mine[4 * t : upto, 0].reshape(256, HD)
            ri = lax.broadcasted_iota(jnp.int32, (256, 256), 0)
            ci = lax.broadcasted_iota(jnp.int32, (256, 256), 1)
            own_ok = (ci // HALF < ri // HALF) | ((ci // HALF == ri // HALF) & (ci <= ri))
            oth_ok = (ci // HALF < ri // HALF) | ((ci // HALF == ri // HALF) & late)
            parts, vals = [], []
            for source, ok in ((mine, own_ok), (other, oth_ok)):
                s = nt(q, source[0:upto, 1].reshape(upto * HALF, HD))
                d = jnp.where(ok, s[:, t * 256 :], LOW)
                parts.append(d if t == 0 else jnp.concatenate([s[:, : t * 256], d], axis=1))
                vals.append(source[0:upto, 2].reshape(upto * HALF, HD))
            o, m = softmax_parts(parts, vals)
            o = o.astype(BF)
            turned = jnp.transpose(m)[0:16]
            row = lax.broadcasted_iota(jnp.int32, (16, 256), 0)
            stats = jnp.zeros((16, 256), F32)
            for n, term in enumerate(three(turned)):
                stats = jnp.where(row == n, term, stats)
            stats = stats.astype(BF)
            for b in range(4):
                out[4 * t + b, 0:HALF] = o[b * HALF : (b + 1) * HALF]
                out[4 * t + b, HALF:] = stats[:, (b // 2) * 128 : (b // 2) * 128 + 128]


def spread_lanes(stats, places):
    line = lax.broadcasted_iota(jnp.int32, (HD, HD), 0)
    hit = functools.reduce(jnp.logical_or, [line == p for p in places])
    return nn(stats, jnp.where(hit, 1.0, 0.0).astype(BF))


def far_piece(here, far_own, far_oth, g, h):
    outs, masses = [], []
    picks = lax.broadcasted_iota(jnp.int32, (16, HD), 0) < 3
    picks = jnp.where(picks, 1.0, 0.0).astype(BF)
    for source in (far_own, far_oth):
        tile = source[h * GROUPS + g]
        outs.append(tile[0:HALF].astype(F32))
        turned = lax.dot_general(
            tile[HALF:], picks, (((0,), (0,)), ((), ())), preferred_element_type=F32
        )
        masses.append(jnp.where(here.y % 2 == 1, turned[HALF:], turned[:HALF]))
    first = here.core == 0

    def ordered(a, b):
        return jnp.concatenate([jnp.where(first, a, b), jnp.where(first, b, a)], axis=0)

    return ordered(*outs), ordered(*masses)


def local_parts(core):
    if core == 0:
        return [[("own", 256, True)], [("own", 512, False), ("oth", 512, True)]]
    return [[("oth", 512, False), ("own", 256, True)], [("oth", 512, True)]]


def local_weights(near, parts, scores):
    extra = [jnp.where(near == i, 1.0, 0.0).astype(F32) for i in range(2)]
    causal = lax.broadcasted_iota(jnp.int32, (BLK, BLK), 0) >= lax.broadcasted_iota(jnp.int32, (BLK, BLK), 1)
    weights, tops = [[] for _ in scores], []
    for i in range(2):
        blocks = []
        for (_, count, diagonal), sc in zip(parts, scores):
            upto = count // BLK - (1 - i if diagonal else 0)
            mine = [sc[i * BLK : (i + 1) * BLK, j * BLK : (j + 1) * BLK] for j in range(upto)]
            if diagonal:
                mine[-1] = jnp.where(causal, mine[-1], LOW)
            blocks.append(mine)
        top = functools.reduce(jnp.maximum, sum(blocks, []))
        top = jnp.max(top, axis=1, keepdims=True) * SCALE
        raised = top - extra[i]
        for n, mine in enumerate(blocks):
            pieces = [
                jnp.exp2(b * SCALE - (raised if j % 2 == i else top)).astype(BF) for j, b in enumerate(mine)
            ]
            pieces += [jnp.zeros((BLK, BLK), BF)] * (parts[n][1] // BLK - len(pieces))
            weights[n].append(jnp.concatenate(pieces, axis=1))
        tops.append(jnp.broadcast_to(top, (BLK, HD)))
    return [jnp.concatenate(w, axis=0) for w in weights], jnp.concatenate(tops, axis=0)


UNROLL = GH


def local_kernel(offsets, q_in, qo_in, k_in, ko_in, v_in, vo_in, mine, away, q, qo, k, ko, v, vo, stats, sems):
    here = Place(offsets)
    keys, vals = {"own": k, "oth": ko}, {"own": v, "oth": vo}
    lane = lax.broadcasted_iota(jnp.int32, (NSEL, HD), 1)
    stats[...] = jnp.zeros_like(stats)

    for core in range(2):
        tiles = local_parts(core)
        own = 512 if core == 0 else 256

        def stage(g, own=own):
            cols = pl.ds(pl.multiple_of(g * GW, GW), GW)
            pieces = (
                (q_in, 0, q, 256),
                (k_in, 0, k, own),
                (ko_in, 0, ko, 512),
                (qo_in, 256, qo, 256),
                (v_in, 0, v, own),
                (vo_in, 0, vo, 512),
            )
            return [
                pltpu.make_async_copy(a.at[pl.ds(first, n), cols], b.at[pl.ds(0, n), cols], sems.at[g, i])
                for i, (a, first, b, n) in enumerate(pieces)
            ]

        @pl.when(here.core == core)
        def _():
            for g in range(GROUPS):
                for c in stage(g):
                    c.start()

            @pl.loop(0, HEADS // UNROLL)
            def _(turn):
                for c in stage(turn):
                    c.wait()
                items = [(h, t) for h in range(UNROLL) for t in range(2)]

                def cols(h):
                    return pl.ds(pl.multiple_of(turn * (UNROLL * HD), HD) + h * HD, HD)

                def score(h, t):
                    queries = (qo if t else q)[:, cols(h)]
                    return [nt(queries, keys[w][0:n, cols(h)]) for w, n, _ in tiles[t]]

                def finish(h, t, weights, top):
                    target = (mine, away)[t]
                    both = 0.0
                    for (w, n, _), p in zip(tiles[t], weights):
                        both = both + nn(p, with_ones(vals[w][0:n, cols(h)]))
                    target[:, cols(h)] = (both[:, :HD] / both[:, HD:]).astype(BF)
                    here_lane = lane % HEADS == turn * UNROLL + h
                    stats[t] = jnp.where(here_lane, top + jnp.log2(both[:, HD:]), stats[t])

                scores = score(*items[0])
                last = None
                for n, (h, t) in enumerate(items):
                    ahead = score(*items[n + 1]) if n + 1 < len(items) else None
                    current = local_weights(here.near((turn * UNROLL + h) // GH), tiles[t], scores)
                    if last is not None:
                        finish(*last)
                    last = (h, t, *current)
                    scores = ahead
                finish(*last)

    for t, target in enumerate((mine, away)):
        target[:, HEADS * HD :] = in_three(stats[t], lane, HEADS)


def mix(parts):
    top = functools.reduce(jnp.maximum, [m for _, m in parts])
    up = down = 0.0
    for o, m in parts:
        e = jnp.exp2(m - top)
        up, down = up + e * o, down + e
    return (up / down).astype(BF)


def own_part(halves, half, rows, g, h):
    source = halves[half]
    return (
        source[rows, pl.ds(g * GW + h * HD, HD)].astype(F32),
        spread_lanes(source[rows, HEADS * HD :], [n * HEADS + g * GH + h for n in range(3)]),
    )


def next_part(nears, half, g, h):
    rows = slice(half * BLK, (half + 1) * BLK)
    source, place, heads = (nears[0], g * GH + h, ASK * GH) if g < ASK else (nears[1], h, GH)
    return (
        source[rows, head_cols(place)].astype(F32),
        spread_lanes(source[rows, heads * HD :], [n * heads + place for n in range(3)]),
    )


def settle(offsets, q, kv_a, kv_b, mine, back, out, near, queries, done, sems, out_sems):
    here = Place(offsets)
    halves = (mine, back)
    copies = []
    for half in range(2):
        rows = rows_at((here.near(ASK) + 2 * half) * BLK, BLK)
        copies.append(
            pltpu.make_async_copy(
                q.at[rows, group_cols(ASK)], queries.at[pl.ds(half * BLK, BLK)], sems.at[len(copies)]
            )
        )

    @pl.when(here.odd)
    def _():
        for c in copies:
            c.start()

    for half in range(2):
        done[half * NSEL : (half + 1) * NSEL, :] = halves[half][:, : HEADS * HD]

    def leave(g):
        return pltpu.make_async_copy(done.at[:, group_cols(g)], out.at[:, group_cols(g)], out_sems.at[g])

    for g in range(ASK):
        leave(g).start()

    @pl.when(here.odd)
    def _():
        for c in copies:
            c.wait()
        near_part(
            GH,
            lambda h: queries[:, head_cols(h)],
            lambda h: [r[:, head_cols(h)] for r in (kv_a, kv_b)],
            lambda h: [r[:, head_cols(GH + h)] for r in (kv_a, kv_b)],
            near,
        )
        rows = rows_at(here.near(ASK) * BLK, BLK)
        for half in range(2):
            to = rows_at(here.near(ASK) * BLK + half * NSEL, BLK)
            for h in range(GH):
                parts = [own_part(halves, half, rows, ASK, h), next_part((None, near), half, ASK, h)]
                done[to, pl.ds(ASK * GW + h * HD, HD)] = mix(parts)

    leave(ASK).start()
    for g in range(GROUPS):
        leave(g).wait()


def finish_kernel(
    offsets, mine, back, near_a, far_own, far_oth, near_in, before, out, near_o, far_o, near_b, near_sems, far_sems, sem
):
    here = Place(offsets)
    nears, halves = (near_a, near_b), (mine, back)
    want_near_b = here.odd & here.far_here(ASK)
    fetch = pltpu.make_async_copy(near_in, near_b, sem)

    @pl.when(want_near_b)
    def _():
        fetch.start()

    def near_copy(g, half):
        rows = rows_at((here.near(g) + 2 * half) * BLK, BLK)
        return pltpu.make_async_copy(near_o.at[g, half], out.at[rows, group_cols(g)], near_sems.at[g, half])

    def far_copy(g):
        rows = rows_at(here.far_block(g) * BLK, BLK)
        return pltpu.make_async_copy(far_o.at[g], out.at[rows, group_cols(g)], far_sems.at[g])

    def near_here(g, half):
        return here.odd & jnp.logical_not(here.far_here(g) & (here.far_block(g) == here.near(g) + 2 * half))

    for g in range(ASK):
        rows = rows_at(here.near(g) * BLK, BLK)
        for half in range(2):

            @pl.when(near_here(g, half))
            def _():
                for h in range(GH):
                    parts = [own_part(halves, half, rows, g, h), next_part(nears, half, g, h)]
                    near_o[g, half, :, head_cols(h)] = mix(parts)
                near_copy(g, half).start()

    @pl.when(want_near_b)
    def _():
        fetch.wait()

    for g in range(GROUPS):
        rows = rows_at(here.far_block(g) % 2 * BLK, BLK)
        near_too = here.odd & (here.far_block(g) % 2 == here.near(g))
        for half in range(2):
            for both in (False, True):

                @pl.when(here.far_here(g) & (here.far_block(g) // 2 == half) & (near_too == both))
                def _():
                    for h in range(GH):
                        parts = [own_part(halves, half, rows, g, h), far_piece(here, far_own, far_oth, g, h)]
                        if both:
                            parts.append(next_part(nears, half, g, h))
                        far_o[g, :, head_cols(h)] = mix(parts)
                    far_copy(g).start()

    for g in range(GROUPS):

        @pl.when(here.far_here(g))
        def _():
            far_copy(g).wait()

    for g in range(ASK):
        for half in range(2):

            @pl.when(near_here(g, half))
            def _():
                near_copy(g, half).wait()


VMEM = pl.BlockSpec(memory_space=pltpu.VMEM)
HBM = pl.BlockSpec(memory_space=pltpu.HBM)


def shape(*dims):
    return jax.ShapeDtypeStruct(dims, BF)


def hbm(array):
    return pltpu.with_memory_space_constraint(array, pltpu.HBM)


def device_part(q, k, v, offsets):
    params = pltpu.CompilerParams(**PARAMS)

    def call(kernel, outs, operands, places, sems=None, scratch=(), out_places=VMEM, flops=1000, aliases=None):
        return pl.pallas_call(
            kernel,
            out_shape=outs,
            in_specs=[SMEM] + places,
            out_specs=out_places,
            scratch_shapes=list(scratch) + ([] if sems is None else [pltpu.SemaphoreType.DMA((sems,))]),
            input_output_aliases=aliases or {},
            compiler_params=params,
            cost_estimate=cost(flops),
            name=kernel.__name__,
        )(hbm(offsets), *operands)

    qh, kh, vh = hbm(q), hbm(k), hbm(v)
    half_shape = shape(GROUPS, 3, HALF, GW)
    near_x, far_send, far_keep = call(
        pack_first,
        [shape(NSEL, ASK * GW), half_shape, half_shape],
        (qh, kh, vh),
        [HBM] * 3,
        sems=6 * GROUPS + 2 * ASK,
        out_places=[VMEM] * 3,
    )
    far_recv = move(far_send, CORE)
    near_r = move(near_x, PAIR)
    qm, far_recv = lax.optimization_barrier((q, far_recv))
    qo, ko, vo = hbm(move(qm, CORE)), hbm(move(k, CORE)), hbm(move(v, CORE))
    far_pack = call(pack_second, shape(HEADS, 3, HALF, HD), (far_keep, far_recv), [VMEM] * 2)
    far_mine = lax.all_to_all(far_pack, ("x", "y"), 0, 0, tiled=True)

    rows = HEADS * HD
    mine, away = call(
        local_kernel,
        [shape(NSEL, rows + HD), pltpu.HBM((NSEL, rows + HD), BF)],
        (qh, qo, kh, ko, vh, vo),
        [HBM] * 6,
        scratch=[pltpu.VMEM((n, rows), BF) for n in (NSEL, NSEL, ROWS, ROWS, ROWS, ROWS)]
        + [pltpu.VMEM((2, NSEL, HD), F32), pltpu.SemaphoreType.DMA((GROUPS, 6))],
        out_places=[VMEM] * 2,
        flops=10**10,
    )
    back = move(away, CORE)
    near_r, far_mine, mine = lax.optimization_barrier((near_r, far_mine, mine))
    far_other, near_ro = move(far_mine, CORE), move(near_r, CORE)
    near_out = call(
        near_even,
        shape(NSEL, ASK * GW + HD),
        (near_r, kh, ko, vh, vo),
        [VMEM] + [HBM] * 4,
        sems=8 * ASK,
        scratch=[pltpu.VMEM((ROWS, ASK * GW), BF)] * 2,
    )
    near_back = move(near_out, TO_ODD)
    far_other, near_out = lax.optimization_barrier((far_other, near_out))
    far_out = call(far_kernel, pltpu.HBM((HEADS, HALF + 16, HD), BF), (far_mine, far_other), [VMEM] * 2)
    far_back = lax.all_to_all(far_out, ("x", "y"), 0, 0, tiled=True)
    out, near_here = call(
        settle,
        [shape(ROWS, HEADS * HD), pltpu.HBM((NSEL, GW + HD), BF)],
        (qh, near_r, near_ro, mine, back),
        [HBM] + [VMEM] * 4,
        scratch=[
            pltpu.VMEM((NSEL, GW), BF),
            pltpu.VMEM((ROWS, HEADS * HD), BF),
            pltpu.SemaphoreType.DMA((2,)),
            pltpu.SemaphoreType.DMA((GROUPS,)),
        ],
        out_places=[HBM, VMEM],
    )
    near_here = hbm(near_here)
    far_back, out = lax.optimization_barrier((far_back, out))
    far_back_other = move(far_back, CORE)
    return call(
        finish_kernel,
        shape(ROWS, HEADS * HD),
        (mine, back, near_back, far_back, far_back_other, near_here, out),
        [VMEM] * 5 + [HBM] * 2,
        scratch=[
            pltpu.VMEM((ASK, 2, BLK, GW), BF),
            pltpu.VMEM((GROUPS, BLK, GW), BF),
            pltpu.VMEM((NSEL, GW + HD), BF),
            pltpu.SemaphoreType.DMA((ASK, 2)),
            pltpu.SemaphoreType.DMA((GROUPS,)),
            pltpu.SemaphoreType.DMA,
        ],
        out_places=HBM,
        aliases={7: 0},
    )


def solution(mesh):
    cube = Mesh(mesh.devices.reshape(SIZES), AXES)
    rows = P(AXES, None)
    return jax.shard_map(
        device_part, mesh=cube, in_specs=(rows, rows, rows, P()), out_specs=rows, check_vma=False
    )
```

```python
import functools

import jax
import jax.numpy as jnp
import numpy as np
from jax import lax
from jax.experimental import pallas as pl
from jax.experimental.pallas import tpu as pltpu
from jax.sharding import Mesh
from jax.sharding import PartitionSpec as P

HD = 128
BLK = 128
HALF = 64
HEADS = 16
GROUPS = 4
GH = 4
GW = GH * HD
ROWS = 512
NSEL = 256
ASK = 3
AXES = ("x", "y", "z", "c")
SIZES = (4, 4, 4, 2)
SCALE = float(HD**-0.5 * np.log2(np.e))
LOW = -1e30
BF, F32 = jnp.bfloat16, jnp.float32


class Place:
    def __init__(self, offsets):
        self.x, self.y, self.z, self.core = (lax.axis_index(a) for a in AXES)
        self.offsets = offsets
        self.odd = self.z % 2 == 1

    def near(self, g):
        return self.offsets[0, g]

    def far_z(self, g):
        return self.offsets[1, g] // 8

    def far_core(self, g):
        return self.offsets[1, g] // 4 % 2

    def far_block(self, g):
        return self.offsets[1, g] % 4

    def far_here(self, g):
        return (self.far_z(g) == self.z) & (self.far_core(g) == self.core)


def route(step):
    pairs = []
    for index in np.ndindex(*SIZES):
        target = step(*index)
        if target is not None:
            pairs.append((int(np.ravel_multi_index(index, SIZES)), int(np.ravel_multi_index(target, SIZES))))
    return pairs


CORE = route(lambda x, y, z, c: (x, y, z, 1 - c))
PAIR = route(lambda x, y, z, c: (x, y, z ^ 1, c))
TO_ODD = route(lambda x, y, z, c: (x, y, z + 1, c) if z % 2 == 0 else None)


def move(array, pairs):
    return lax.ppermute(array, AXES, pairs)


def cost(flops=1000):
    return pl.CostEstimate(flops=flops, bytes_accessed=1000, transcendentals=0)


ANY = pl.BlockSpec(memory_space=pl.ANY)
SMEM = pl.BlockSpec(memory_space=pltpu.SMEM)
PARAMS = dict(vmem_limit_bytes=28 * 1024 * 1024)


def nt(a, b):
    return lax.dot_general(a, b, (((1,), (1,)), ((), ())), preferred_element_type=F32)


def nn(a, b):
    return lax.dot_general(a, b, (((1,), (0,)), ((), ())), preferred_element_type=F32)


def three(x):
    hi = x.astype(BF).astype(F32)
    rest = x - hi
    mid = rest.astype(BF).astype(F32)
    return hi, mid, rest - mid


def in_three(stats, lane, heads):
    hi, mid, low = three(stats)
    return jnp.where(lane < heads, hi, jnp.where(lane < 2 * heads, mid, low)).astype(BF)


def rows_at(first, count):
    return pl.ds(pl.multiple_of(first, count), count)


def group_cols(g):
    return pl.ds(g * GW, GW)


def run_copies(copies):
    for c in copies:
        c.start()
    for c in copies:
        c.wait()


def pack_first(offsets, q, k, v, near, send, keep, sems):
    here = Place(offsets)
    copies = []
    for g in range(GROUPS):
        for t, source in enumerate((q, k, v)):
            first = here.far_block(g) * BLK
            for half, target in ((1 - here.core, send), (here.core, keep)):
                rows = rows_at(first + half * HALF, HALF)
                copies.append(
                    pltpu.make_async_copy(source.at[rows, group_cols(g)], target.at[g, t], sems.at[len(copies)])
                )
    for odd in (False, True):

        @pl.when(here.odd == odd)
        def _():
            nears = []
            pieces = [(q, g, g) for g in range(ASK)] if odd else [(k, ASK, 0), (v, ASK, 1)]
            for source, g, place in pieces:
                for half in range(2):
                    rows = rows_at((here.near(g) + 2 * half) * BLK, BLK)
                    nears.append(
                        pltpu.make_async_copy(
                            source.at[rows, group_cols(g)],
                            near.at[pl.ds(half * BLK, BLK), group_cols(place)],
                            sems.at[len(copies) + len(nears)],
                        )
                    )
            run_copies(copies + nears)


def pack_second(offsets, kept, received, out):
    here = Place(offsets)
    for g in range(GROUPS):
        mine = here.far_core(g) == here.core
        for source, flag in ((kept, mine), (received, jnp.logical_not(mine))):

            @pl.when(flag)
            def _():
                for t in range(3):
                    for h in range(GH):
                        out[h * GROUPS + g, t] = source[g, t, :, h * HD : (h + 1) * HD]


def with_ones(val):
    return jnp.concatenate([val, jnp.ones((val.shape[0], HD), BF)], axis=1)


def with_ones(val):
    return jnp.concatenate([val, jnp.ones((val.shape[0], HD), BF)], axis=1)


def softmax_parts(parts, values):
    top = functools.reduce(jnp.maximum, [jnp.max(s, axis=1, keepdims=True) for s in parts]) * SCALE
    both = 0.0
    for s, val in zip(parts, values):
        both = both + nn(jnp.exp2(s * SCALE - top).astype(BF), with_ones(val))
    return both[:, :HD] / both[:, HD:], top + jnp.log2(both[:, HD:])


def head_cols(h):
    return slice(h * HD, (h + 1) * HD)


def near_part(heads, q_of, keys_of, vals_of, out, ready=lambda h: None, left=lambda h: None):
    lane = lax.broadcasted_iota(jnp.int32, (NSEL, HD), 1)

    def score(h):
        ready(h)
        return [nt(q_of(h), keys) for keys in keys_of(h)]

    def finish(h, weights, top, stats):
        both = sum(nn(p, with_ones(vals)) for p, vals in zip(weights, vals_of(h)))
        out[:, head_cols(h)] = (both[:, :HD] / both[:, HD:]).astype(BF)
        left(h)
        return jnp.where(lane % heads == h, top + jnp.log2(both[:, HD:]), stats)

    stats, last, scores = jnp.zeros((NSEL, HD), F32), None, score(0)
    for h in range(heads):
        ahead = score(h + 1) if h + 1 < heads else None
        top = functools.reduce(jnp.maximum, [jnp.max(s, axis=1, keepdims=True) for s in scores]) * SCALE
        weights = [jnp.exp2(s * SCALE - top).astype(BF) for s in scores]
        if last is not None:
            stats = finish(*last, stats)
        last, scores = (h, weights, top), ahead
    stats = finish(*last, stats)
    out[:, heads * HD :] = in_three(stats, lane, heads)


def near_even(offsets, qr_in, k, ko, v, vo, out, keys, vals, qr, done, sems, out_sems):
    here = Place(offsets)

    @pl.when(jnp.logical_not(here.odd))
    def _():
        copies = []
        for g in range(ASK):
            pieces = [(qr_in.at[:, group_cols(g)], qr.at[:, group_cols(g)])]
            for n, (source, half) in enumerate([(0, 0), (0, 1), (1, 0), (1, 1)]):
                rows = rows_at((here.near(g) + 2 * half) * BLK, BLK)
                for two, target in (((k, ko), keys), ((v, vo), vals)):
                    pieces.append(
                        (two[source].at[rows, group_cols(g)], target.at[pl.ds(n * BLK, BLK), group_cols(g)])
                    )
            copies.append(
                [pltpu.make_async_copy(x, y, sems.at[g, i]) for i, (x, y) in enumerate(pieces)]
            )
        for c in sum(copies, []):
            c.start()

        def ready(h):
            if h % GH == 0:
                for c in copies[h // GH]:
                    c.wait()

        def leave(g):
            cols = group_cols(g) if g < ASK else pl.ds(ASK * GW, HD)
            return pltpu.make_async_copy(done.at[:, cols], out.at[:, cols], out_sems.at[g])

        def left(h):
            if h % GH == GH - 1:
                leave(h // GH).start()

        near_part(
            ASK * GH,
            lambda h: qr[:, head_cols(h)],
            lambda h: [keys[:, head_cols(h)]],
            lambda h: [vals[:, head_cols(h)]],
            done,
            ready,
            left,
        )
        leave(ASK).start()
        for g in range(ASK + 1):
            leave(g).wait()


def far_kernel(offsets, mine, other, out):
    here = Place(offsets)

    @pl.when(here.far_z(here.y) == here.z)
    def _():
        late = here.core == 1
        for t in range(4):
            upto = 4 * t + 4
            q = mine[4 * t : upto, 0].reshape(256, HD)
            ri = lax.broadcasted_iota(jnp.int32, (256, 256), 0)
            ci = lax.broadcasted_iota(jnp.int32, (256, 256), 1)
            own_ok = (ci // HALF < ri // HALF) | ((ci // HALF == ri // HALF) & (ci <= ri))
            oth_ok = (ci // HALF < ri // HALF) | ((ci // HALF == ri // HALF) & late)
            parts, vals = [], []
            for source, ok in ((mine, own_ok), (other, oth_ok)):
                s = nt(q, source[0:upto, 1].reshape(upto * HALF, HD))
                d = jnp.where(ok, s[:, t * 256 :], LOW)
                parts.append(d if t == 0 else jnp.concatenate([s[:, : t * 256], d], axis=1))
                vals.append(source[0:upto, 2].reshape(upto * HALF, HD))
            o, m = softmax_parts(parts, vals)
            o = o.astype(BF)
            turned = jnp.transpose(m)[0:16]
            row = lax.broadcasted_iota(jnp.int32, (16, 256), 0)
            stats = jnp.zeros((16, 256), F32)
            for n, term in enumerate(three(turned)):
                stats = jnp.where(row == n, term, stats)
            stats = stats.astype(BF)
            for b in range(4):
                out[4 * t + b, 0:HALF] = o[b * HALF : (b + 1) * HALF]
                out[4 * t + b, HALF:] = stats[:, (b // 2) * 128 : (b // 2) * 128 + 128]


def spread_lanes(stats, places):
    line = lax.broadcasted_iota(jnp.int32, (HD, HD), 0)
    hit = functools.reduce(jnp.logical_or, [line == p for p in places])
    return nn(stats, jnp.where(hit, 1.0, 0.0).astype(BF))


def far_piece(here, far_own, far_oth, g, h):
    outs, masses = [], []
    picks = lax.broadcasted_iota(jnp.int32, (16, HD), 0) < 3
    picks = jnp.where(picks, 1.0, 0.0).astype(BF)
    for source in (far_own, far_oth):
        tile = source[h * GROUPS + g]
        outs.append(tile[0:HALF].astype(F32))
        turned = lax.dot_general(
            tile[HALF:], picks, (((0,), (0,)), ((), ())), preferred_element_type=F32
        )
        masses.append(jnp.where(here.y % 2 == 1, turned[HALF:], turned[:HALF]))
    first = here.core == 0

    def ordered(a, b):
        return jnp.concatenate([jnp.where(first, a, b), jnp.where(first, b, a)], axis=0)

    return ordered(*outs), ordered(*masses)


def local_parts(core):
    if core == 0:
        return [[("own", 256, True)], [("own", 512, False), ("oth", 512, True)]]
    return [[("oth", 512, False), ("own", 256, True)], [("oth", 512, True)]]


def local_weights(near, parts, scores):
    extra = [jnp.where(near == i, 1.0, 0.0).astype(F32) for i in range(2)]
    causal = lax.broadcasted_iota(jnp.int32, (BLK, BLK), 0) >= lax.broadcasted_iota(jnp.int32, (BLK, BLK), 1)
    weights, tops = [[] for _ in scores], []
    for i in range(2):
        blocks = []
        for (_, count, diagonal), sc in zip(parts, scores):
            upto = count // BLK - (1 - i if diagonal else 0)
            mine = [sc[i * BLK : (i + 1) * BLK, j * BLK : (j + 1) * BLK] for j in range(upto)]
            if diagonal:
                mine[-1] = jnp.where(causal, mine[-1], LOW)
            blocks.append(mine)
        top = functools.reduce(jnp.maximum, sum(blocks, []))
        top = jnp.max(top, axis=1, keepdims=True) * SCALE
        raised = top - extra[i]
        for n, mine in enumerate(blocks):
            pieces = [
                jnp.exp2(b * SCALE - (raised if j % 2 == i else top)).astype(BF) for j, b in enumerate(mine)
            ]
            pieces += [jnp.zeros((BLK, BLK), BF)] * (parts[n][1] // BLK - len(pieces))
            weights[n].append(jnp.concatenate(pieces, axis=1))
        tops.append(jnp.broadcast_to(top, (BLK, HD)))
    return [jnp.concatenate(w, axis=0) for w in weights], jnp.concatenate(tops, axis=0)


UNROLL = GH


def local_kernel(offsets, q_in, qo_in, k_in, ko_in, v_in, vo_in, mine, away, q, qo, k, ko, v, vo, stats, sems):
    here = Place(offsets)
    keys, vals = {"own": k, "oth": ko}, {"own": v, "oth": vo}
    lane = lax.broadcasted_iota(jnp.int32, (NSEL, HD), 1)
    stats[...] = jnp.zeros_like(stats)

    for core in range(2):
        tiles = local_parts(core)
        own = 512 if core == 0 else 256

        def stage(g, own=own):
            cols = pl.ds(pl.multiple_of(g * GW, GW), GW)
            pieces = (
                (q_in, 0, q, 256),
                (k_in, 0, k, own),
                (ko_in, 0, ko, 512),
                (qo_in, 256, qo, 256),
                (v_in, 0, v, own),
                (vo_in, 0, vo, 512),
            )
            return [
                pltpu.make_async_copy(a.at[pl.ds(first, n), cols], b.at[pl.ds(0, n), cols], sems.at[g, i])
                for i, (a, first, b, n) in enumerate(pieces)
            ]

        @pl.when(here.core == core)
        def _():
            for g in range(GROUPS):
                for c in stage(g):
                    c.start()

            @pl.loop(0, HEADS // UNROLL)
            def _(turn):
                for c in stage(turn):
                    c.wait()
                items = [(h, t) for h in range(UNROLL) for t in range(2)]

                def cols(h):
                    return pl.ds(pl.multiple_of(turn * (UNROLL * HD), HD) + h * HD, HD)

                def score(h, t):
                    queries = (qo if t else q)[:, cols(h)]
                    return [nt(queries, keys[w][0:n, cols(h)]) for w, n, _ in tiles[t]]

                def finish(h, t, weights, top):
                    target = (mine, away)[t]
                    both = 0.0
                    for (w, n, _), p in zip(tiles[t], weights):
                        both = both + nn(p, with_ones(vals[w][0:n, cols(h)]))
                    target[:, cols(h)] = (both[:, :HD] / both[:, HD:]).astype(BF)
                    here_lane = lane % HEADS == turn * UNROLL + h
                    stats[t] = jnp.where(here_lane, top + jnp.log2(both[:, HD:]), stats[t])

                scores = score(*items[0])
                last = None
                for n, (h, t) in enumerate(items):
                    ahead = score(*items[n + 1]) if n + 1 < len(items) else None
                    current = local_weights(here.near((turn * UNROLL + h) // GH), tiles[t], scores)
                    if last is not None:
                        finish(*last)
                    last = (h, t, *current)
                    scores = ahead
                finish(*last)

    for t, target in enumerate((mine, away)):
        target[:, HEADS * HD :] = in_three(stats[t], lane, HEADS)


def mix(parts):
    top = functools.reduce(jnp.maximum, [m for _, m in parts])
    up = down = 0.0
    for o, m in parts:
        e = jnp.exp2(m - top)
        up, down = up + e * o, down + e
    return (up / down).astype(BF)


def own_part(halves, half, rows, g, h):
    source = halves[half]
    return (
        source[rows, pl.ds(g * GW + h * HD, HD)].astype(F32),
        spread_lanes(source[rows, HEADS * HD :], [n * HEADS + g * GH + h for n in range(3)]),
    )


def next_part(nears, half, g, h):
    rows = slice(half * BLK, (half + 1) * BLK)
    source, place, heads = (nears[0], g * GH + h, ASK * GH) if g < ASK else (nears[1], h, GH)
    return (
        source[rows, head_cols(place)].astype(F32),
        spread_lanes(source[rows, heads * HD :], [n * heads + place for n in range(3)]),
    )


def settle(offsets, q, kv_a, kv_b, mine, back, out, near, queries, done, sems, out_sems):
    here = Place(offsets)
    halves = (mine, back)
    copies = []
    for half in range(2):
        rows = rows_at((here.near(ASK) + 2 * half) * BLK, BLK)
        copies.append(
            pltpu.make_async_copy(
                q.at[rows, group_cols(ASK)], queries.at[pl.ds(half * BLK, BLK)], sems.at[len(copies)]
            )
        )

    @pl.when(here.odd)
    def _():
        for c in copies:
            c.start()

    for half in range(2):
        done[half * NSEL : (half + 1) * NSEL, :] = halves[half][:, : HEADS * HD]

    def leave(g):
        return pltpu.make_async_copy(done.at[:, group_cols(g)], out.at[:, group_cols(g)], out_sems.at[g])

    for g in range(ASK):
        leave(g).start()

    @pl.when(here.odd)
    def _():
        for c in copies:
            c.wait()
        near_part(
            GH,
            lambda h: queries[:, head_cols(h)],
            lambda h: [r[:, head_cols(h)] for r in (kv_a, kv_b)],
            lambda h: [r[:, head_cols(GH + h)] for r in (kv_a, kv_b)],
            near,
        )
        rows = rows_at(here.near(ASK) * BLK, BLK)
        for half in range(2):
            to = rows_at(here.near(ASK) * BLK + half * NSEL, BLK)
            for h in range(GH):
                parts = [own_part(halves, half, rows, ASK, h), next_part((None, near), half, ASK, h)]
                done[to, pl.ds(ASK * GW + h * HD, HD)] = mix(parts)

    leave(ASK).start()
    for g in range(GROUPS):
        leave(g).wait()


def finish_kernel(
    offsets, mine, back, far_own, far_oth, ask_in, near_in, before, out, *rest
):
    here = Place(offsets)
    near_o, far_o, near_a, near_b, near_sems, far_sems, ask_sems, sem = rest
    nears, halves = (near_a, near_b), (mine, back)

    def ask_copy(g):
        cols = group_cols(g) if g < ASK else pl.ds(ASK * GW, HD)
        return pltpu.make_async_copy(ask_in.at[:, cols], near_a.at[:, cols], ask_sems.at[g])

    @pl.when(here.odd)
    def _():
        for g in (ASK, *range(ASK)):
            ask_copy(g).start()

    want_near_b = here.odd & here.far_here(ASK)
    fetch = pltpu.make_async_copy(near_in, near_b, sem)

    @pl.when(want_near_b)
    def _():
        fetch.start()

    def near_copy(g, half):
        rows = rows_at((here.near(g) + 2 * half) * BLK, BLK)
        return pltpu.make_async_copy(near_o.at[g, half], out.at[rows, group_cols(g)], near_sems.at[g, half])

    def far_copy(g):
        rows = rows_at(here.far_block(g) * BLK, BLK)
        return pltpu.make_async_copy(far_o.at[g], out.at[rows, group_cols(g)], far_sems.at[g])

    def near_here(g, half):
        return here.odd & jnp.logical_not(here.far_here(g) & (here.far_block(g) == here.near(g) + 2 * half))

    for g in range(ASK):
        rows = rows_at(here.near(g) * BLK, BLK)

        @pl.when(here.odd)
        def _():
            if g == 0:
                ask_copy(ASK).wait()
            ask_copy(g).wait()

        for half in range(2):

            @pl.when(near_here(g, half))
            def _():
                for h in range(GH):
                    parts = [own_part(halves, half, rows, g, h), next_part(nears, half, g, h)]
                    near_o[g, half, :, head_cols(h)] = mix(parts)
                near_copy(g, half).start()

    @pl.when(want_near_b)
    def _():
        fetch.wait()

    for g in range(GROUPS):
        rows = rows_at(here.far_block(g) % 2 * BLK, BLK)
        near_too = here.odd & (here.far_block(g) % 2 == here.near(g))
        for half in range(2):
            for both in (False, True):

                @pl.when(here.far_here(g) & (here.far_block(g) // 2 == half) & (near_too == both))
                def _():
                    for h in range(GH):
                        parts = [own_part(halves, half, rows, g, h), far_piece(here, far_own, far_oth, g, h)]
                        if both:
                            parts.append(next_part(nears, half, g, h))
                        far_o[g, :, head_cols(h)] = mix(parts)
                    far_copy(g).start()

    for g in range(GROUPS):

        @pl.when(here.far_here(g))
        def _():
            far_copy(g).wait()

    for g in range(ASK):
        for half in range(2):

            @pl.when(near_here(g, half))
            def _():
                near_copy(g, half).wait()


VMEM = pl.BlockSpec(memory_space=pltpu.VMEM)
HBM = pl.BlockSpec(memory_space=pltpu.HBM)


def shape(*dims):
    return jax.ShapeDtypeStruct(dims, BF)


def hbm(array):
    return pltpu.with_memory_space_constraint(array, pltpu.HBM)


def device_part(q, k, v, offsets):
    params = pltpu.CompilerParams(**PARAMS)

    def call(kernel, outs, operands, places, sems=None, scratch=(), out_places=VMEM, flops=1000, aliases=None):
        return pl.pallas_call(
            kernel,
            out_shape=outs,
            in_specs=[SMEM] + places,
            out_specs=out_places,
            scratch_shapes=list(scratch) + ([] if sems is None else [pltpu.SemaphoreType.DMA((sems,))]),
            input_output_aliases=aliases or {},
            compiler_params=params,
            cost_estimate=cost(flops),
            name=kernel.__name__,
        )(hbm(offsets), *operands)

    qh, kh, vh = hbm(q), hbm(k), hbm(v)
    half_shape = shape(GROUPS, 3, HALF, GW)
    near_x, far_send, far_keep = call(
        pack_first,
        [shape(NSEL, ASK * GW), half_shape, half_shape],
        (qh, kh, vh),
        [HBM] * 3,
        sems=6 * GROUPS + 2 * ASK,
        out_places=[VMEM] * 3,
    )
    far_recv = move(far_send, CORE)
    near_r = move(near_x, PAIR)
    qm, far_recv = lax.optimization_barrier((q, far_recv))
    qo, ko, vo = hbm(move(qm, CORE)), hbm(move(k, CORE)), hbm(move(v, CORE))
    far_pack = call(pack_second, shape(HEADS, 3, HALF, HD), (far_keep, far_recv), [VMEM] * 2)
    far_mine = lax.all_to_all(far_pack, ("x", "y"), 0, 0, tiled=True)

    rows = HEADS * HD
    mine, away = call(
        local_kernel,
        [shape(NSEL, rows + HD), pltpu.HBM((NSEL, rows + HD), BF)],
        (qh, qo, kh, ko, vh, vo),
        [HBM] * 6,
        scratch=[pltpu.VMEM((n, rows), BF) for n in (NSEL, NSEL, ROWS, ROWS, ROWS, ROWS)]
        + [pltpu.VMEM((2, NSEL, HD), F32), pltpu.SemaphoreType.DMA((GROUPS, 6))],
        out_places=[VMEM] * 2,
        flops=10**10,
    )
    back = move(away, CORE)
    near_r, far_mine, mine = lax.optimization_barrier((near_r, far_mine, mine))
    far_other, near_ro = move(far_mine, CORE), move(near_r, CORE)
    near_out = call(
        near_even,
        pltpu.HBM((NSEL, ASK * GW + HD), BF),
        (hbm(near_r), kh, ko, vh, vo),
        [HBM] * 5,
        scratch=[pltpu.VMEM((ROWS, ASK * GW), BF)] * 2
        + [
            pltpu.VMEM((NSEL, ASK * GW), BF),
            pltpu.VMEM((NSEL, ASK * GW + HD), BF),
            pltpu.SemaphoreType.DMA((ASK, 9)),
            pltpu.SemaphoreType.DMA((ASK + 1,)),
        ],
        out_places=HBM,
    )
    near_back = move(near_out, TO_ODD)
    far_other, near_out = lax.optimization_barrier((far_other, near_out))
    far_out = call(far_kernel, pltpu.HBM((HEADS, HALF + 16, HD), BF), (far_mine, far_other), [VMEM] * 2)
    far_back = lax.all_to_all(far_out, ("x", "y"), 0, 0, tiled=True)
    out, near_here = call(
        settle,
        [shape(ROWS, HEADS * HD), pltpu.HBM((NSEL, GW + HD), BF)],
        (qh, near_r, near_ro, mine, back),
        [HBM] + [VMEM] * 4,
        scratch=[
            pltpu.VMEM((NSEL, GW), BF),
            pltpu.VMEM((ROWS, HEADS * HD), BF),
            pltpu.SemaphoreType.DMA((2,)),
            pltpu.SemaphoreType.DMA((GROUPS,)),
        ],
        out_places=[HBM, VMEM],
    )
    near_here = hbm(near_here)
    far_back, out = lax.optimization_barrier((far_back, out))
    far_back_other = move(far_back, CORE)
    return call(
        finish_kernel,
        shape(ROWS, HEADS * HD),
        (mine, back, far_back, far_back_other, hbm(near_back), near_here, out),
        [VMEM] * 4 + [HBM] * 3,
        scratch=[
            pltpu.VMEM((ASK, 2, BLK, GW), BF),
            pltpu.VMEM((GROUPS, BLK, GW), BF),
            pltpu.VMEM((NSEL, ASK * GW + HD), BF),
            pltpu.VMEM((NSEL, GW + HD), BF),
            pltpu.SemaphoreType.DMA((ASK, 2)),
            pltpu.SemaphoreType.DMA((GROUPS,)),
            pltpu.SemaphoreType.DMA((ASK + 1,)),
            pltpu.SemaphoreType.DMA,
        ],
        out_places=HBM,
        aliases={7: 0},
    )


def solution(mesh):
    cube = Mesh(mesh.devices.reshape(SIZES), AXES)
    rows = P(AXES, None)
    return jax.shard_map(
        device_part, mesh=cube, in_specs=(rows, rows, rows, P()), out_specs=rows, check_vma=False
    )
```

```python
import functools

import jax
import jax.numpy as jnp
import numpy as np
from jax import lax
from jax.experimental import pallas as pl
from jax.experimental.pallas import tpu as pltpu
from jax.sharding import Mesh
from jax.sharding import PartitionSpec as P

HD = 128
BLK = 128
HALF = 64
HEADS = 16
GROUPS = 4
GH = 4
GW = GH * HD
ROWS = 512
NSEL = 256
ASK = 3
AXES = ("x", "y", "z", "c")
SIZES = (4, 4, 4, 2)
SCALE = float(HD**-0.5 * np.log2(np.e))
LOW = -1e30
BF, F32 = jnp.bfloat16, jnp.float32


class Place:
    def __init__(self, offsets):
        self.x, self.y, self.z, self.core = (lax.axis_index(a) for a in AXES)
        self.offsets = offsets
        self.odd = self.z % 2 == 1

    def near(self, g):
        return self.offsets[0, g]

    def far_z(self, g):
        return self.offsets[1, g] // 8

    def far_core(self, g):
        return self.offsets[1, g] // 4 % 2

    def far_block(self, g):
        return self.offsets[1, g] % 4

    def far_here(self, g):
        return (self.far_z(g) == self.z) & (self.far_core(g) == self.core)


def route(step):
    pairs = []
    for index in np.ndindex(*SIZES):
        target = step(*index)
        if target is not None:
            pairs.append((int(np.ravel_multi_index(index, SIZES)), int(np.ravel_multi_index(target, SIZES))))
    return pairs


CORE = route(lambda x, y, z, c: (x, y, z, 1 - c))
PAIR = route(lambda x, y, z, c: (x, y, z ^ 1, c))
TO_ODD = route(lambda x, y, z, c: (x, y, z + 1, c) if z % 2 == 0 else None)


def move(array, pairs):
    return lax.ppermute(array, AXES, pairs)


def cost(flops=1000):
    return pl.CostEstimate(flops=flops, bytes_accessed=1000, transcendentals=0)


ANY = pl.BlockSpec(memory_space=pl.ANY)
SMEM = pl.BlockSpec(memory_space=pltpu.SMEM)
PARAMS = dict(vmem_limit_bytes=28 * 1024 * 1024)


def nt(a, b):
    return lax.dot_general(a, b, (((1,), (1,)), ((), ())), preferred_element_type=F32)


def nn(a, b):
    return lax.dot_general(a, b, (((1,), (0,)), ((), ())), preferred_element_type=F32)


def three(x):
    hi = x.astype(BF).astype(F32)
    rest = x - hi
    mid = rest.astype(BF).astype(F32)
    return hi, mid, rest - mid


def in_three(stats, lane, heads):
    hi, mid, low = three(stats)
    return jnp.where(lane < heads, hi, jnp.where(lane < 2 * heads, mid, low)).astype(BF)


def rows_at(first, count):
    return pl.ds(pl.multiple_of(first, count), count)


def group_cols(g):
    return pl.ds(g * GW, GW)


def run_copies(copies):
    for c in copies:
        c.start()
    for c in copies:
        c.wait()


def pack_first(offsets, q, k, v, near, send, keep, sems):
    here = Place(offsets)
    copies = []
    for g in range(GROUPS):
        for t, source in enumerate((q, k, v)):
            first = here.far_block(g) * BLK
            for half, target in ((1 - here.core, send), (here.core, keep)):
                rows = rows_at(first + half * HALF, HALF)
                copies.append(
                    pltpu.make_async_copy(source.at[rows, group_cols(g)], target.at[g, t], sems.at[len(copies)])
                )
    for odd in (False, True):

        @pl.when(here.odd == odd)
        def _():
            nears = []
            pieces = [(q, g, g) for g in range(ASK)] if odd else [(k, ASK, 0), (v, ASK, 1)]
            for source, g, place in pieces:
                for half in range(2):
                    rows = rows_at((here.near(g) + 2 * half) * BLK, BLK)
                    nears.append(
                        pltpu.make_async_copy(
                            source.at[rows, group_cols(g)],
                            near.at[pl.ds(half * BLK, BLK), group_cols(place)],
                            sems.at[len(copies) + len(nears)],
                        )
                    )
            run_copies(copies + nears)


def pack_second(offsets, kept, received, out):
    here = Place(offsets)
    for g in range(GROUPS):
        mine = here.far_core(g) == here.core
        for source, flag in ((kept, mine), (received, jnp.logical_not(mine))):

            @pl.when(flag)
            def _():
                for t in range(3):
                    for h in range(GH):
                        out[h * GROUPS + g, t] = source[g, t, :, h * HD : (h + 1) * HD]


def with_ones(val):
    return jnp.concatenate([val, jnp.ones((val.shape[0], HD), BF)], axis=1)


def with_ones(val):
    return jnp.concatenate([val, jnp.ones((val.shape[0], HD), BF)], axis=1)


def softmax_parts(parts, values):
    top = functools.reduce(jnp.maximum, [jnp.max(s, axis=1, keepdims=True) for s in parts]) * SCALE
    both = 0.0
    for s, val in zip(parts, values):
        both = both + nn(jnp.exp2(s * SCALE - top).astype(BF), with_ones(val))
    return both[:, :HD] / both[:, HD:], top + jnp.log2(both[:, HD:])


def head_cols(h):
    return slice(h * HD, (h + 1) * HD)


def near_part(heads, q_of, keys_of, vals_of, out, ready=lambda h: None, left=lambda h: None):
    lane = lax.broadcasted_iota(jnp.int32, (NSEL, HD), 1)

    def score(h):
        ready(h)
        return [nt(q_of(h), keys) for keys in keys_of(h)]

    def finish(h, weights, top, stats):
        both = sum(nn(p, with_ones(vals)) for p, vals in zip(weights, vals_of(h)))
        out[:, head_cols(h)] = (both[:, :HD] / both[:, HD:]).astype(BF)
        left(h)
        return jnp.where(lane % heads == h, top + jnp.log2(both[:, HD:]), stats)

    stats, last, scores = jnp.zeros((NSEL, HD), F32), None, score(0)
    for h in range(heads):
        ahead = score(h + 1) if h + 1 < heads else None
        top = functools.reduce(jnp.maximum, [jnp.max(s, axis=1, keepdims=True) for s in scores]) * SCALE
        weights = [jnp.exp2(s * SCALE - top).astype(BF) for s in scores]
        if last is not None:
            stats = finish(*last, stats)
        last, scores = (h, weights, top), ahead
    stats = finish(*last, stats)
    out[:, heads * HD :] = in_three(stats, lane, heads)


def near_even(offsets, qr_in, k, ko, v, vo, out, keys, vals, qr, done, sems, out_sems):
    here = Place(offsets)

    @pl.when(jnp.logical_not(here.odd))
    def _():
        copies = []
        for g in range(ASK):
            pieces = [(qr_in.at[:, group_cols(g)], qr.at[:, group_cols(g)])]
            for n, (source, half) in enumerate([(0, 0), (0, 1), (1, 0), (1, 1)]):
                rows = rows_at((here.near(g) + 2 * half) * BLK, BLK)
                for two, target in (((k, ko), keys), ((v, vo), vals)):
                    pieces.append(
                        (two[source].at[rows, group_cols(g)], target.at[pl.ds(n * BLK, BLK), group_cols(g)])
                    )
            copies.append(
                [pltpu.make_async_copy(x, y, sems.at[g, i]) for i, (x, y) in enumerate(pieces)]
            )
        for c in sum(copies, []):
            c.start()

        def ready(h):
            if h % GH == 0:
                for c in copies[h // GH]:
                    c.wait()

        def leave(g):
            cols = group_cols(g) if g < ASK else pl.ds(ASK * GW, HD)
            return pltpu.make_async_copy(done.at[:, cols], out.at[:, cols], out_sems.at[g])

        def left(h):
            if h % GH == GH - 1:
                leave(h // GH).start()

        near_part(
            ASK * GH,
            lambda h: qr[:, head_cols(h)],
            lambda h: [keys[:, head_cols(h)]],
            lambda h: [vals[:, head_cols(h)]],
            done,
            ready,
            left,
        )
        leave(ASK).start()
        for g in range(ASK + 1):
            leave(g).wait()


def far_kernel(offsets, mine, other, out):
    here = Place(offsets)

    @pl.when(here.far_z(here.y) == here.z)
    def _():
        late = here.core == 1
        for t in range(4):
            upto = 4 * t + 4
            q = mine[4 * t : upto, 0].reshape(256, HD)
            ri = lax.broadcasted_iota(jnp.int32, (256, 256), 0)
            ci = lax.broadcasted_iota(jnp.int32, (256, 256), 1)
            own_ok = (ci // HALF < ri // HALF) | ((ci // HALF == ri // HALF) & (ci <= ri))
            oth_ok = (ci // HALF < ri // HALF) | ((ci // HALF == ri // HALF) & late)
            parts, vals = [], []
            for source, ok in ((mine, own_ok), (other, oth_ok)):
                s = nt(q, source[0:upto, 1].reshape(upto * HALF, HD))
                d = jnp.where(ok, s[:, t * 256 :], LOW)
                parts.append(d if t == 0 else jnp.concatenate([s[:, : t * 256], d], axis=1))
                vals.append(source[0:upto, 2].reshape(upto * HALF, HD))
            o, m = softmax_parts(parts, vals)
            o = o.astype(BF)
            turned = jnp.transpose(m)[0:16]
            row = lax.broadcasted_iota(jnp.int32, (16, 256), 0)
            stats = jnp.zeros((16, 256), F32)
            for n, term in enumerate(three(turned)):
                stats = jnp.where(row == n, term, stats)
            stats = stats.astype(BF)
            for b in range(4):
                out[4 * t + b, 0:HALF] = o[b * HALF : (b + 1) * HALF]
                out[4 * t + b, HALF:] = stats[:, (b // 2) * 128 : (b // 2) * 128 + 128]


def spread_lanes(stats, places):
    line = lax.broadcasted_iota(jnp.int32, (HD, HD), 0)
    hit = functools.reduce(jnp.logical_or, [line == p for p in places])
    return nn(stats, jnp.where(hit, 1.0, 0.0).astype(BF))


def far_piece(here, far_own, far_oth, g, h):
    outs, masses = [], []
    picks = lax.broadcasted_iota(jnp.int32, (16, HD), 0) < 3
    picks = jnp.where(picks, 1.0, 0.0).astype(BF)
    for source in (far_own, far_oth):
        tile = source[h * GROUPS + g]
        outs.append(tile[0:HALF].astype(F32))
        turned = lax.dot_general(
            tile[HALF:], picks, (((0,), (0,)), ((), ())), preferred_element_type=F32
        )
        masses.append(jnp.where(here.y % 2 == 1, turned[HALF:], turned[:HALF]))
    first = here.core == 0

    def ordered(a, b):
        return jnp.concatenate([jnp.where(first, a, b), jnp.where(first, b, a)], axis=0)

    return ordered(*outs), ordered(*masses)


def local_parts(core):
    if core == 0:
        return [[("own", 256, True)], [("own", 512, False), ("oth", 512, True)]]
    return [[("oth", 512, False), ("own", 256, True)], [("oth", 512, True)]]


def local_weights(near, parts, scores):
    extra = [jnp.where(near == i, 1.0, 0.0).astype(F32) for i in range(2)]
    causal = lax.broadcasted_iota(jnp.int32, (BLK, BLK), 0) >= lax.broadcasted_iota(jnp.int32, (BLK, BLK), 1)
    weights, tops = [[] for _ in scores], []
    for i in range(2):
        blocks = []
        for (_, count, diagonal), sc in zip(parts, scores):
            upto = count // BLK - (1 - i if diagonal else 0)
            mine = [sc[i * BLK : (i + 1) * BLK, j * BLK : (j + 1) * BLK] for j in range(upto)]
            if diagonal:
                mine[-1] = jnp.where(causal, mine[-1], LOW)
            blocks.append(mine)
        top = functools.reduce(jnp.maximum, sum(blocks, []))
        top = jnp.max(top, axis=1, keepdims=True) * SCALE
        raised = top - extra[i]
        for n, mine in enumerate(blocks):
            pieces = [
                jnp.exp2(b * SCALE - (raised if j % 2 == i else top)).astype(BF) for j, b in enumerate(mine)
            ]
            pieces += [jnp.zeros((BLK, BLK), BF)] * (parts[n][1] // BLK - len(pieces))
            weights[n].append(jnp.concatenate(pieces, axis=1))
        tops.append(jnp.broadcast_to(top, (BLK, HD)))
    return [jnp.concatenate(w, axis=0) for w in weights], jnp.concatenate(tops, axis=0)


UNROLL = GH


def local_kernel(offsets, q_in, qo_in, k_in, ko_in, v_in, vo_in, mine, away, q, qo, k, ko, v, vo, stats, sems):
    here = Place(offsets)
    keys, vals = {"own": k, "oth": ko}, {"own": v, "oth": vo}
    lane = lax.broadcasted_iota(jnp.int32, (NSEL, HD), 1)
    stats[...] = jnp.zeros_like(stats)

    for core in range(2):
        tiles = local_parts(core)
        own = 512 if core == 0 else 256

        def stage(g, own=own):
            cols = pl.ds(pl.multiple_of(g * GW, GW), GW)
            pieces = (
                (q_in, 0, q, 256),
                (k_in, 0, k, own),
                (ko_in, 0, ko, 512),
                (qo_in, 256, qo, 256),
                (v_in, 0, v, own),
                (vo_in, 0, vo, 512),
            )
            return [
                pltpu.make_async_copy(a.at[pl.ds(first, n), cols], b.at[pl.ds(0, n), cols], sems.at[g, i])
                for i, (a, first, b, n) in enumerate(pieces)
            ]

        @pl.when(here.core == core)
        def _():
            for g in range(GROUPS):
                for c in stage(g):
                    c.start()

            @pl.loop(0, HEADS // UNROLL)
            def _(turn):
                for c in stage(turn):
                    c.wait()
                items = [(h, t) for h in range(UNROLL) for t in range(2)]

                def cols(h):
                    return pl.ds(pl.multiple_of(turn * (UNROLL * HD), HD) + h * HD, HD)

                def score(h, t):
                    queries = (qo if t else q)[:, cols(h)]
                    return [nt(queries, keys[w][0:n, cols(h)]) for w, n, _ in tiles[t]]

                def finish(h, t, weights, top):
                    target = (mine, away)[t]
                    both = 0.0
                    for (w, n, _), p in zip(tiles[t], weights):
                        both = both + nn(p, with_ones(vals[w][0:n, cols(h)]))
                    target[:, cols(h)] = (both[:, :HD] / both[:, HD:]).astype(BF)
                    here_lane = lane % HEADS == turn * UNROLL + h
                    stats[t] = jnp.where(here_lane, top + jnp.log2(both[:, HD:]), stats[t])

                scores = score(*items[0])
                last = None
                for n, (h, t) in enumerate(items):
                    ahead = score(*items[n + 1]) if n + 1 < len(items) else None
                    current = local_weights(here.near((turn * UNROLL + h) // GH), tiles[t], scores)
                    if last is not None:
                        finish(*last)
                    last = (h, t, *current)
                    scores = ahead
                finish(*last)

    for t, target in enumerate((mine, away)):
        target[:, HEADS * HD :] = in_three(stats[t], lane, HEADS)


def mix(parts):
    top = functools.reduce(jnp.maximum, [m for _, m in parts])
    up = down = 0.0
    for o, m in parts:
        e = jnp.exp2(m - top)
        up, down = up + e * o, down + e
    return (up / down).astype(BF)


def own_part(halves, half, rows, g, h):
    source = halves[half]
    return (
        source[rows, pl.ds(g * GW + h * HD, HD)].astype(F32),
        spread_lanes(source[rows, HEADS * HD :], [n * HEADS + g * GH + h for n in range(3)]),
    )


def next_part(nears, half, g, h):
    rows = slice(half * BLK, (half + 1) * BLK)
    source, place, heads = (nears[0], g * GH + h, ASK * GH) if g < ASK else (nears[1], h, GH)
    return (
        source[rows, head_cols(place)].astype(F32),
        spread_lanes(source[rows, heads * HD :], [n * heads + place for n in range(3)]),
    )


def settle(offsets, q, kv_a, kv_b, mine, back, out, near, queries, done, sems, out_sems):
    here = Place(offsets)
    halves = (mine, back)
    copies = []
    for half in range(2):
        rows = rows_at((here.near(ASK) + 2 * half) * BLK, BLK)
        copies.append(
            pltpu.make_async_copy(
                q.at[rows, group_cols(ASK)], queries.at[pl.ds(half * BLK, BLK)], sems.at[len(copies)]
            )
        )

    @pl.when(here.odd)
    def _():
        for c in copies:
            c.start()

    for half in range(2):
        done[half * NSEL : (half + 1) * NSEL, :] = halves[half][:, : HEADS * HD]

    def leave(g):
        return pltpu.make_async_copy(done.at[:, group_cols(g)], out.at[:, group_cols(g)], out_sems.at[g])

    for g in range(ASK):
        leave(g).start()

    @pl.when(here.odd)
    def _():
        for c in copies:
            c.wait()
        near_part(
            GH,
            lambda h: queries[:, head_cols(h)],
            lambda h: [r[:, head_cols(h)] for r in (kv_a, kv_b)],
            lambda h: [r[:, head_cols(GH + h)] for r in (kv_a, kv_b)],
            near,
        )
        rows = rows_at(here.near(ASK) * BLK, BLK)
        for half in range(2):
            to = rows_at(here.near(ASK) * BLK + half * NSEL, BLK)
            for h in range(GH):
                parts = [own_part(halves, half, rows, ASK, h), next_part((None, near), half, ASK, h)]
                done[to, pl.ds(ASK * GW + h * HD, HD)] = mix(parts)

    leave(ASK).start()
    for g in range(GROUPS):
        leave(g).wait()


def finish_kernel(
    offsets, mine, back, near_a, far_own, far_oth, near_in, before, out, near_o, far_o, near_b, near_sems, far_sems, sem
):
    here = Place(offsets)
    nears, halves = (near_a, near_b), (mine, back)
    want_near_b = here.odd & here.far_here(ASK)
    fetch = pltpu.make_async_copy(near_in, near_b, sem)

    @pl.when(want_near_b)
    def _():
        fetch.start()

    def near_copy(g, half):
        rows = rows_at((here.near(g) + 2 * half) * BLK, BLK)
        return pltpu.make_async_copy(near_o.at[g, half], out.at[rows, group_cols(g)], near_sems.at[g, half])

    def far_copy(g):
        rows = rows_at(here.far_block(g) * BLK, BLK)
        return pltpu.make_async_copy(far_o.at[g], out.at[rows, group_cols(g)], far_sems.at[g])

    def near_here(g, half):
        return here.odd & jnp.logical_not(here.far_here(g) & (here.far_block(g) == here.near(g) + 2 * half))

    for g in range(ASK):
        rows = rows_at(here.near(g) * BLK, BLK)
        for half in range(2):

            @pl.when(near_here(g, half))
            def _():
                for h in range(GH):
                    parts = [own_part(halves, half, rows, g, h), next_part(nears, half, g, h)]
                    near_o[g, half, :, head_cols(h)] = mix(parts)
                near_copy(g, half).start()

    @pl.when(want_near_b)
    def _():
        fetch.wait()

    for g in range(GROUPS):
        rows = rows_at(here.far_block(g) % 2 * BLK, BLK)
        near_too = here.odd & (here.far_block(g) % 2 == here.near(g))
        for half in range(2):
            for both in (False, True):

                @pl.when(here.far_here(g) & (here.far_block(g) // 2 == half) & (near_too == both))
                def _():
                    for h in range(GH):
                        parts = [own_part(halves, half, rows, g, h), far_piece(here, far_own, far_oth, g, h)]
                        if both:
                            parts.append(next_part(nears, half, g, h))
                        far_o[g, :, head_cols(h)] = mix(parts)
                    far_copy(g).start()

    for g in range(GROUPS):

        @pl.when(here.far_here(g))
        def _():
            far_copy(g).wait()

    for g in range(ASK):
        for half in range(2):

            @pl.when(near_here(g, half))
            def _():
                near_copy(g, half).wait()


VMEM = pl.BlockSpec(memory_space=pltpu.VMEM)
HBM = pl.BlockSpec(memory_space=pltpu.HBM)


def shape(*dims):
    return jax.ShapeDtypeStruct(dims, BF)


def hbm(array):
    return pltpu.with_memory_space_constraint(array, pltpu.HBM)


def device_part(q, k, v, offsets):
    params = pltpu.CompilerParams(**PARAMS)

    def call(kernel, outs, operands, places, sems=None, scratch=(), out_places=VMEM, flops=1000, aliases=None):
        return pl.pallas_call(
            kernel,
            out_shape=outs,
            in_specs=[SMEM] + places,
            out_specs=out_places,
            scratch_shapes=list(scratch) + ([] if sems is None else [pltpu.SemaphoreType.DMA((sems,))]),
            input_output_aliases=aliases or {},
            compiler_params=params,
            cost_estimate=cost(flops),
            name=kernel.__name__,
        )(hbm(offsets), *operands)

    qh, kh, vh = hbm(q), hbm(k), hbm(v)
    half_shape = shape(GROUPS, 3, HALF, GW)
    near_x, far_send, far_keep = call(
        pack_first,
        [shape(NSEL, ASK * GW), half_shape, half_shape],
        (qh, kh, vh),
        [HBM] * 3,
        sems=6 * GROUPS + 2 * ASK,
        out_places=[VMEM] * 3,
    )
    far_recv = move(far_send, CORE)
    near_r = move(near_x, PAIR)
    qm, far_recv = lax.optimization_barrier((q, far_recv))
    qo, ko, vo = hbm(move(qm, CORE)), hbm(move(k, CORE)), hbm(move(v, CORE))
    far_pack = call(pack_second, shape(HEADS, 3, HALF, HD), (far_keep, far_recv), [VMEM] * 2)
    far_mine = lax.all_to_all(far_pack, ("x", "y"), 0, 0, tiled=True)

    rows = HEADS * HD
    mine, away = call(
        local_kernel,
        [shape(NSEL, rows + HD), pltpu.HBM((NSEL, rows + HD), BF)],
        (qh, qo, kh, ko, vh, vo),
        [HBM] * 6,
        scratch=[pltpu.VMEM((n, rows), BF) for n in (NSEL, NSEL, ROWS, ROWS, ROWS, ROWS)]
        + [pltpu.VMEM((2, NSEL, HD), F32), pltpu.SemaphoreType.DMA((GROUPS, 6))],
        out_places=[VMEM] * 2,
        flops=10**10,
    )
    back = move(away, CORE)
    near_r, far_mine, mine = lax.optimization_barrier((near_r, far_mine, mine))
    far_other, near_ro = move(far_mine, CORE), move(near_r, CORE)
    near_out = call(
        near_even,
        pltpu.HBM((NSEL, ASK * GW + HD), BF),
        (hbm(near_r), kh, ko, vh, vo),
        [HBM] * 5,
        scratch=[pltpu.VMEM((ROWS, ASK * GW), BF)] * 2
        + [
            pltpu.VMEM((NSEL, ASK * GW), BF),
            pltpu.VMEM((NSEL, ASK * GW + HD), BF),
            pltpu.SemaphoreType.DMA((ASK, 9)),
            pltpu.SemaphoreType.DMA((ASK + 1,)),
        ],
        out_places=HBM,
    )
    near_back = move(near_out, TO_ODD)
    far_other, near_out = lax.optimization_barrier((far_other, near_out))
    far_out = call(far_kernel, pltpu.HBM((HEADS, HALF + 16, HD), BF), (far_mine, far_other), [VMEM] * 2)
    far_back = lax.all_to_all(far_out, ("x", "y"), 0, 0, tiled=True)
    out, near_here = call(
        settle,
        [shape(ROWS, HEADS * HD), pltpu.HBM((NSEL, GW + HD), BF)],
        (qh, near_r, near_ro, mine, back),
        [HBM] + [VMEM] * 4,
        scratch=[
            pltpu.VMEM((NSEL, GW), BF),
            pltpu.VMEM((ROWS, HEADS * HD), BF),
            pltpu.SemaphoreType.DMA((2,)),
            pltpu.SemaphoreType.DMA((GROUPS,)),
        ],
        out_places=[HBM, VMEM],
    )
    near_here = hbm(near_here)
    far_back, out = lax.optimization_barrier((far_back, out))
    far_back_other = move(far_back, CORE)
    return call(
        finish_kernel,
        shape(ROWS, HEADS * HD),
        (mine, back, near_back, far_back, far_back_other, near_here, out),
        [VMEM] * 5 + [HBM] * 2,
        scratch=[
            pltpu.VMEM((ASK, 2, BLK, GW), BF),
            pltpu.VMEM((GROUPS, BLK, GW), BF),
            pltpu.VMEM((NSEL, GW + HD), BF),
            pltpu.SemaphoreType.DMA((ASK, 2)),
            pltpu.SemaphoreType.DMA((GROUPS,)),
            pltpu.SemaphoreType.DMA,
        ],
        out_places=HBM,
        aliases={7: 0},
    )


def solution(mesh):
    cube = Mesh(mesh.devices.reshape(SIZES), AXES)
    rows = P(AXES, None)
    return jax.shard_map(
        device_part, mesh=cube, in_specs=(rows, rows, rows, P()), out_specs=rows, check_vma=False
    )
```
